512 devices in a mesh: slab: 32 (over z, y_lo), grp: 16 (over y_hi, x, core).
Axes of the slice: x: 4, y: 8 (y_hi: 2, y_lo: 4; y = y_hi * 4 + y_lo), z: 8, core: 2. Of those that a mesh axis runs over, the one named last changes fastest.
Arguments:
- particles: bfloat16 [512, 2, 256, 256], P(('slab', 'grp')), may hold values from -6 to 6
- defocus_class: int32 [512], P(('slab', 'grp')), may hold values from 0 to 15
- noise_precision: float32 [512], P(('slab', 'grp')), may hold values from 25 to 200
- live_count: int32 [16], P('grp'), may hold values from 1 to 1, as said below
- defocus: float32 [16], replicated, may hold values from 20 to 200
- reference_lines: bfloat16 [512, 2, 256], P('slab'), may hold values from -6 to 6
- line_index: int32 [16, 256, 2], replicated, may hold values from 0 to 511
- line_weight: float32 [16, 256, 2], replicated, may hold values from 0.2 to 1
- row_shifts: int32 [8], replicated, may hold values from -4 to 4
- column_shifts: int32 [8], replicated, may hold values from -4 to 4
Outputs:
- volume_sums: float32 [512, 3, 256], P(('slab', 'grp'))
- loglik: float32 [512], P(('slab', 'grp'))
The draws below stay inside these ranges and needn't reach their ends.
Inputs may be any that keep to these rules, and one draw needn't show every extreme that they name: live_count[g] live particles occupy the first slots of each device of group g; some group is full in every draw.
All inputs are finite; a program needn't handle non-finite values.
Results may differ from the reference program's by a relative error of at most 0.0042.
Values may be sent and summed in bfloat16 or wider, within the bound.
A program may use at most 128 MiB of HBM per device.

```python
import math
import jax
import jax.numpy as jnp
from jax import lax

BOX = 256
SHIFT_X = 8
SHIFT_Y = 8
POSES = 16
CLASSES = 16
PART_DEV = 1
GROUPS = 16
PARTICLES = 512
LINES = 512
N_GRP = 16


def draw_live_count(key, part):
    first_key = jax.random.fold_in(key, 11)
    second_key = jax.random.fold_in(key, 12)
    counts = jax.random.randint(first_key, (GROUPS,), 1, PART_DEV + 1)
    fullest = jax.random.randint(second_key, (), 0, GROUPS)
    return jnp.where(jnp.arange(GROUPS) == fullest, PART_DEV, counts).astype(jnp.int32)


def draw_noise_precision(key, part):
    base = jax.random.uniform(jax.random.fold_in(key, 21), (PARTICLES,), jnp.float32)
    return (25.0 * jnp.exp(base * math.log(8.0))).astype(jnp.float32)


def with_ends(values, key, smallest, high):
    extent = values.shape
    index_at = [jax.random.randint(jax.random.fold_in(key, axis), (), 0, extent[axis]) for axis in range(len(extent))]
    values = values.at[tuple(index_at)].set(smallest)
    longest = extent.index(max(extent))
    index_at[longest] = (index_at[longest] + 1) % extent[longest]
    return values.at[tuple(index_at)].set(high)


def levels(key, dims, pieces, smallest, largest):
    level = 1.0
    for axis_at, blocks in pieces:
        steps = jax.random.uniform(jax.random.fold_in(jax.random.fold_in(key, 6), axis_at), (blocks,), jnp.float32, smallest / len(pieces), largest / len(pieces))
        level = level * jnp.repeat(jnp.exp(steps), dims[axis_at] // blocks).reshape((-1,) + (1,) * (len(dims) - 1 - axis_at))
    return level


def bell_draw(stream_key, dims, scale, most, shards=(), kind=jnp.bfloat16):
    factor_of = levels(stream_key, dims, shards, -0.22, 0.18) if shards else 1.0
    entries = jax.random.normal(stream_key, dims, jnp.float32) * scale * factor_of
    return jnp.minimum(jnp.maximum(entries, -most), most).astype(kind)


def setup_inputs(seed: int = 0) -> dict:
    arg_keys = jax.random.split(jax.random.key(seed), 11)
    return {
        "particles": bell_draw(arg_keys[0], (PARTICLES, 2, BOX, BOX), 1.0, 6.0, ((0, 512),)),
        "defocus_class": with_ends(jax.random.randint(arg_keys[1], (PARTICLES,), 0, CLASSES), jax.random.fold_in(arg_keys[1], 1), 0, CLASSES - 1).astype(jnp.int32),
        "noise_precision": draw_noise_precision(jax.random.fold_in(arg_keys[10], 71), 0),
        "live_count": draw_live_count(jax.random.fold_in(arg_keys[10], 71), 0),
        "defocus": jnp.clip(jnp.exp(jax.random.uniform(arg_keys[4], (CLASSES,), jnp.float32, math.log(20.0), math.log(200.0))), 20.0, 200.0),
        "reference_lines": bell_draw(arg_keys[5], (LINES, 2, BOX), 1.0, 6.0, ((0, 32),)),
        "line_index": with_ends(jax.random.randint(arg_keys[6], (POSES, BOX, 2), 0, LINES), jax.random.fold_in(arg_keys[6], 1), 0, LINES - 1).astype(jnp.int32),
        "line_weight": jnp.clip(jax.random.uniform(arg_keys[7], (POSES, BOX, 2), jnp.float32, 0.2, 1.0), 0.2, 1.0),
        "row_shifts": with_ends(jax.random.randint(arg_keys[8], (SHIFT_X,), -4, 5), jax.random.fold_in(arg_keys[8], 1), -4, 4).astype(jnp.int32),
        "column_shifts": with_ends(jax.random.randint(arg_keys[9], (SHIFT_Y,), -4, 5), jax.random.fold_in(arg_keys[9], 1), -4, 4).astype(jnp.int32),
    }


PRECISE = lax.Precision.HIGHEST


def bfloat_rounded(values):
    return lax.optimization_barrier(values.astype(jnp.bfloat16)).astype(jnp.float32)


def phase_table(shifts):
    freq = jnp.arange(BOX, dtype=jnp.int32) - BOX // 2
    turns = jnp.mod(freq[:, None] * shifts.astype(jnp.int32)[None, :], BOX)
    angle = turns.astype(jnp.float32) * (2.0 * math.pi / BOX)
    return jnp.cos(angle), jnp.sin(angle)


def radius_squared():
    freq = (jnp.arange(BOX, dtype=jnp.int32) - BOX // 2).astype(jnp.float32) / BOX
    return freq[:, None] * freq[:, None] + freq[None, :] * freq[None, :]


def transfer_function(classes, defocus, alive_mask):
    onehot = (classes[:, None] == jnp.arange(defocus.shape[0], dtype=jnp.int32)[None, :]).astype(jnp.float32)
    chosen = jnp.sum(onehot * defocus[None, :], axis=1)
    return -jnp.sin(chosen[:, None, None] * radius_squared()[None] + 0.1) * alive_mask[:, None, None]


def project_slices(lines, line_index, line_weight):
    first_line = jnp.take(lines, line_index[:, :, 0], axis=0).astype(jnp.float32)
    second_line = jnp.take(lines, line_index[:, :, 1], axis=0).astype(jnp.float32)
    blended = first_line * line_weight[:, :, 0, None, None] + second_line * line_weight[:, :, 1, None, None]
    return blended.astype(jnp.bfloat16)


def block_terms(images, classes, precision_row, alive_mask, defocus, slices, cos_x, sin_x, cos_y, sin_y):
    ctf = transfer_function(classes, defocus, alive_mask)
    real_part = ctf * images[:, 0].astype(jnp.float32)
    imag_part = ctf * images[:, 1].astype(jnp.float32)
    cos_rows = cos_y.T[None, None]
    sin_rows = sin_y.T[None, None]
    shift_re = bfloat_rounded(real_part[:, :, None, :] * cos_rows + imag_part[:, :, None, :] * sin_rows)
    shift_im = bfloat_rounded(real_part[:, :, None, :] * sin_rows - imag_part[:, :, None, :] * cos_rows)
    slice_re = slices[:, :, 0].astype(jnp.float32)
    slice_im = slices[:, :, 1].astype(jnp.float32)
    prod_re = jnp.einsum('pky,nkty->kpnt', slice_re, shift_re, precision=PRECISE) - jnp.einsum('pky,nkty->kpnt', slice_im, shift_im, precision=PRECISE)
    prod_im = jnp.einsum('pky,nkty->kpnt', slice_re, shift_im, precision=PRECISE) + jnp.einsum('pky,nkty->kpnt', slice_im, shift_re, precision=PRECISE)
    corr = jnp.einsum('kpnt,ku->nput', prod_re, cos_x, precision=PRECISE) - jnp.einsum('kpnt,ku->nput', prod_im, sin_x, precision=PRECISE)
    score = corr * (precision_row / BOX)[:, None, None, None]
    flat_score = score.reshape(score.shape[0], -1)
    row_max = jnp.max(flat_score, axis=1, keepdims=True)
    expo_terms = jnp.exp(flat_score - row_max)
    summed = jnp.sum(expo_terms, axis=1, keepdims=True)
    posterior = (expo_terms / summed).reshape(score.shape)
    loglik = (row_max[:, 0] + jnp.log(summed[:, 0])) * alive_mask
    weight_re = bfloat_rounded(jnp.einsum('nput,ku->kpnt', posterior, cos_x, precision=PRECISE))
    weight_im = bfloat_rounded(-jnp.einsum('nput,ku->kpnt', posterior, sin_x, precision=PRECISE))
    insert_re = jnp.einsum('kpnt,nkty->pky', weight_re, shift_re, precision=PRECISE) + jnp.einsum('kpnt,nkty->pky', weight_im, shift_im, precision=PRECISE)
    insert_im = jnp.einsum('kpnt,nkty->pky', weight_im, shift_re, precision=PRECISE) - jnp.einsum('kpnt,nkty->pky', weight_re, shift_im, precision=PRECISE)
    pose_mass = jnp.sum(posterior, axis=(2, 3))
    weight_sum = jnp.einsum('np,nky->pky', pose_mass, ctf * ctf, precision=PRECISE)
    return loglik, insert_re, insert_im, weight_sum


def reference(particles, defocus_class, noise_precision, live_count, defocus, reference_lines, line_index, line_weight, row_shifts, column_shifts):
    cos_x, sin_x = phase_table(row_shifts)
    cos_y, sin_y = phase_table(column_shifts)
    slices = project_slices(reference_lines, line_index, line_weight)
    block_count = PARTICLES // PART_DEV
    images = particles.reshape(block_count, PART_DEV, 2, BOX, BOX)
    classes = defocus_class.reshape(block_count, PART_DEV)
    precisions = noise_precision.reshape(block_count, PART_DEV)
    group_of = jnp.mod(jnp.arange(block_count, dtype=jnp.int32), N_GRP)
    limits = live_count[group_of]
    alive_all = (jnp.arange(PART_DEV, dtype=jnp.int32)[None, :] < limits[:, None]).astype(jnp.float32)
    empty = jnp.zeros((POSES, BOX, BOX), jnp.float32)

    def accumulate(sums, element):
        block_images, block_classes, block_precision, block_alive = element
        loglik, insert_re, insert_im, weight_sum = block_terms(block_images, block_classes, block_precision, block_alive, defocus, slices, cos_x, sin_x, cos_y, sin_y)
        return (sums[0] + insert_re, sums[1] + insert_im, sums[2] + weight_sum), loglik

    totals, logliks = lax.scan(accumulate, (empty, empty, empty), (images, classes, precisions, alive_all))
    rows = jnp.stack([totals[0], totals[1], totals[2]], axis=2).reshape(POSES * BOX, 3, BOX)
    volume = jnp.zeros((LINES, 3, BOX), jnp.float32)
    for corner in range(2):
        scaled = rows * line_weight[:, :, corner].reshape(-1)[:, None, None]
        volume = volume + jax.ops.segment_sum(scaled, line_index[:, :, corner].reshape(-1), num_segments=LINES)
    volume = volume * (LINES / (POSES * PARTICLES))
    return volume, logliks.reshape(PARTICLES)
```

```python
import math

import jax
import jax.numpy as jnp
from jax import lax
from jax.experimental import pallas as pl
from jax.experimental.pallas import tpu as pltpu
from jax.sharding import PartitionSpec as P

MESH = pl.DeviceIdType.MESH
EXACT = lax.Precision.HIGHEST
F32 = jnp.float32
BF16 = jnp.bfloat16
I32 = jnp.int32

NX, NY, NZ, Y_LO = 4, 8, 8, 4
SLABS = NZ * Y_LO
LINES = 512
KEEP = LINES // 2
BOX = 256
POSES = 16
GROUP = 16
WIDE = GROUP * POSES
ROWS = POSES * BOX
SHIFTS = 8


def place():
    slab = lax.axis_index("slab")
    grp = lax.axis_index("grp")
    z, y_lo = slab // Y_LO, slab % Y_LO
    y_hi, x, core = grp // (2 * NX), (grp // 2) % NX, grp % 2
    return z, y_hi * Y_LO + y_lo, x, core


def device_at(z, y, x, core):
    return (z * Y_LO + y % Y_LO, (y // Y_LO) * (2 * NX) + x * 2 + core)


def gather_peer(j, sign, z, y, x, core):
    step_z = j // Y_LO
    step_y = (j % Y_LO + 1) % Y_LO - 1
    return device_at((z + NZ + sign * step_z) % NZ, (y + NY + sign * step_y) % NY, x, core)


def gather_kernel(lines_ref, out_ref, held, send_sem, recv_sem, pair_sem):
    z, y, x, core = place()
    slab = z * Y_LO + y % Y_LO
    sibling = device_at(z, y, x, 1 - core)
    barrier = pltpu.get_barrier_semaphore()

    def greet(j, carry):
        pl.semaphore_signal(
            barrier, inc=1, device_id=gather_peer(j, -1, z, y, x, core), device_id_type=MESH
        )
        return carry

    lax.fori_loop(1, SLABS, greet, 0)
    pl.semaphore_signal(barrier, inc=1, device_id=sibling, device_id_type=MESH)
    both = lines_ref[...]
    held[core, slab] = jnp.where(core == 0, both[:, 0, :], both[:, 1, :])
    pl.semaphore_wait(barrier, SLABS)

    def block_copy(j):
        return pltpu.make_async_remote_copy(
            src_ref=held.at[core, slab],
            dst_ref=held.at[core, slab],
            send_sem=send_sem.at[j],
            recv_sem=recv_sem.at[j],
            device_id=gather_peer(j, 1, z, y, x, core),
            device_id_type=MESH,
        )

    def send(j, carry):
        block_copy(j).start()
        return carry

    def settle(j, carry):
        block_copy(j).wait()
        return carry

    lax.fori_loop(1, SLABS, send, 0)
    lax.fori_loop(1, SLABS, settle, 0)
    swap = pltpu.make_async_remote_copy(
        src_ref=held.at[core],
        dst_ref=held.at[core],
        send_sem=pair_sem.at[0],
        recv_sem=pair_sem.at[1],
        device_id=sibling,
        device_id_type=MESH,
    )
    swap.start()
    swap.wait()
    out_ref[...] = held[...].reshape(out_ref.shape)


def gather_lines(lines):
    half = (2, SLABS, lines.shape[0], BOX)
    return pl.pallas_call(
        gather_kernel,
        out_shape=jax.ShapeDtypeStruct((2, LINES, BOX), BF16),
        in_specs=[pl.BlockSpec(memory_space=pltpu.VMEM)],
        out_specs=pl.BlockSpec(memory_space=pltpu.VMEM),
        scratch_shapes=[
            pltpu.VMEM(half, BF16),
            pltpu.SemaphoreType.DMA((SLABS,)),
            pltpu.SemaphoreType.DMA((SLABS,)),
            pltpu.SemaphoreType.DMA((2,)),
        ],
        compiler_params=pltpu.CompilerParams(collective_id=0, has_side_effects=True),
    )(lines)


def phase_angle(turns):
    signed = ((turns + BOX // 2) & (BOX - 1)) - BOX // 2
    return signed.astype(F32) * (2.0 * math.pi / BOX)


def shift_column(shifts_ref, shape):
    row = lax.broadcasted_iota(I32, shape, 0)
    column = jnp.zeros(shape, I32)
    for t in range(SHIFTS):
        column = jnp.where(row == t, shifts_ref[t], column)
    return column


def slot_of(line, z, y, x, core):
    line_y = ((line >> 3) & 1) * Y_LO + ((line >> 4) & (Y_LO - 1))
    return (
        ((line ^ core) & 1) * KEEP
        + ((((line >> 1) - x) & (NX - 1)) * (NY * NZ))
        + (((line_y - y) & (NY - 1)) * NZ)
        + (((line >> 6) - z) & (NZ - 1))
    )


def line_of(slot, z, y, x, core):
    line_z = (slot + z) & (NZ - 1)
    line_y = ((slot >> 3) + y) & (NY - 1)
    line_x = ((slot >> 6) + x) & (NX - 1)
    line_core = ((slot >> 8) ^ core) & 1
    return line_z * 64 + (line_y & 3) * 16 + (line_y >> 2) * 8 + line_x * 2 + line_core


def expect_kernel(
    class_ref,
    precision_ref,
    live_ref,
    defocus_ref,
    row_shift_ref,
    column_shift_ref,
    image_ref,
    index_ref,
    weight_ref,
    lines_ref,
    own_ref,
    other_ref,
    loglik_ref,
    slots,
    weights,
    lines_t,
    spread,
    shifted,
    phases,
    squares,
    rows,
):
    z, y, x, core = place()
    alive = jnp.where(0 < live_ref[0], 1.0, 0.0).astype(F32)
    chosen = defocus_ref[class_ref[0]]

    first = slot_of(index_ref[0:1, :], z, y, x, core)
    second = slot_of(index_ref[1:2, :], z, y, x, core)
    same = first == second
    first_weight = jnp.where(same, weight_ref[0:1, :] + weight_ref[1:2, :], weight_ref[0:1, :])
    second_weight = jnp.where(same, 0.0, weight_ref[1:2, :])
    slots[0:1, :] = first
    slots[1:2, :] = second
    first_high = first_weight.astype(BF16).astype(F32)
    second_high = second_weight.astype(BF16).astype(F32)
    weights[0:1, :] = first_high
    weights[1:2, :] = second_high
    weights[2:3, :] = first_weight - first_high
    weights[3:4, :] = second_weight - second_high

    slot_lines = line_of(lax.broadcasted_iota(I32, (1, LINES), 1), z, y, x, core)
    order = jnp.where(
        lax.broadcasted_iota(I32, (LINES, LINES), 0) == slot_lines, 1.0, 0.0
    ).astype(BF16)
    for c in range(2):
        lines_t[pl.ds(c * BOX, BOX), :] = lax.dot_general(
            lines_ref[c], order, (((0,), (0,)), ((), ())), preferred_element_type=F32
        ).astype(BF16)

    lane = lax.broadcasted_iota(I32, (SHIFTS, ROWS), 1)
    freq = (lane >> 4) - BOX // 2
    part = (lane >> 3) & 1
    turns = freq * shift_column(row_shift_ref, (SHIFTS, ROWS)) + part * (BOX // 4)
    row_phase = jnp.cos(phase_angle(turns))
    for t in range(SHIFTS):
        phases[pl.ds(t * SHIFTS, SHIFTS), :] = jnp.where((lane & 7) == t, row_phase, 0.0)

    lane_y = lax.broadcasted_iota(I32, (SHIFTS, BOX), 1) - BOX // 2
    angle_y = phase_angle(lane_y * shift_column(column_shift_ref, (SHIFTS, BOX)))
    cos_y = jnp.cos(angle_y)
    sin_y = jnp.sin(angle_y)
    freq_y = (lax.broadcasted_iota(I32, (GROUP, BOX), 1) - BOX // 2).astype(F32) / BOX
    row_in_group = lax.broadcasted_iota(I32, (GROUP, BOX), 0)
    one_row = (lax.broadcasted_iota(I32, (WIDE, WIDE), 0) >> 4) == (
        lax.broadcasted_iota(I32, (WIDE, WIDE), 1) >> 4
    )
    slot_row = lax.broadcasted_iota(I32, (LINES, WIDE), 0)

    def correlate(g, corr):
        at = pl.ds(pl.multiple_of(g * WIDE, WIDE), WIDE)
        kx = pl.ds(pl.multiple_of(g * GROUP, GROUP), GROUP)
        freq_x = (row_in_group + (g * GROUP - BOX // 2)).astype(F32) / BOX
        ctf = -jnp.sin(chosen * (freq_x * freq_x + freq_y * freq_y) + 0.1) * alive
        squares[kx, :] = ctf * ctf
        real = ctf * image_ref[0, 0, kx, :].astype(F32)
        imag = ctf * image_ref[0, 1, kx, :].astype(F32)
        blocks = []
        for k in range(GROUP):
            real_row = real[k : k + 1, :]
            imag_row = imag[k : k + 1, :]
            shift_re = real_row * cos_y + imag_row * sin_y
            shift_im = real_row * sin_y - imag_row * cos_y
            blocks.append(jnp.concatenate([shift_re, -shift_im], axis=1))
            blocks.append(jnp.concatenate([shift_im, shift_re], axis=1))
        shifted_rows = jnp.concatenate(blocks, axis=0).astype(BF16)
        shifted[at, :] = shifted_rows
        is_first = slot_row == slots[0:1, at]
        is_second = slot_row == slots[1:2, at]
        high = jnp.where(is_first, weights[0:1, at], jnp.where(is_second, weights[1:2, at], 0.0))
        low = jnp.where(is_first, weights[2:3, at], jnp.where(is_second, weights[3:4, at], 0.0))
        high = high.astype(BF16)
        spread[:, at] = high
        slices = jnp.dot(lines_t[...], high, preferred_element_type=F32) + jnp.dot(
            lines_t[...], low.astype(BF16), preferred_element_type=F32
        )
        products = jnp.dot(shifted_rows, slices.astype(BF16), preferred_element_type=F32)
        return corr + jnp.dot(
            phases[:, at],
            jnp.where(one_row, products, 0.0),
            precision=EXACT,
            preferred_element_type=F32,
        )

    corr = lax.fori_loop(
        0, BOX // GROUP, correlate, jnp.zeros((SHIFTS * SHIFTS, WIDE), F32)
    )
    corr = corr[:, : WIDE // 2] + corr[:, WIDE // 2 :]
    for step in (64, 32, 16):
        corr = corr + pltpu.roll(corr, step, 1)
    score = corr * (precision_ref[0] / BOX)
    top = jnp.max(score, axis=(0, 1), keepdims=True)
    terms = jnp.exp(score - top)
    total = jnp.sum(terms, axis=(0, 1), keepdims=True) * (1.0 / 8.0)
    posterior = terms / total
    loglik_ref[0] = ((top + jnp.log(total)) * alive)[0, 0]
    posterior_t = posterior.T
    mass = jnp.sum(posterior_t, axis=1, keepdims=True)[:POSES]

    def insert(g, carry):
        at = pl.ds(pl.multiple_of(g * WIDE, WIDE), WIDE)
        kx = pl.ds(pl.multiple_of(g * GROUP, GROUP), GROUP)
        weight = jnp.dot(posterior_t, phases[:, at], precision=EXACT, preferred_element_type=F32)
        weight = jnp.where(one_row, jnp.concatenate([weight, weight], axis=0), 0.0).astype(BF16)
        rows[at, : 2 * BOX] = jnp.dot(
            weight, shifted[at, :], preferred_element_type=F32
        ).astype(BF16)
        square = squares[kx, :]
        rows[at, 2 * BOX :] = jnp.concatenate(
            [square[k : k + 1, :] * mass for k in range(GROUP)], axis=0
        ).astype(BF16)
        return carry

    lax.fori_loop(0, BOX // GROUP, insert, 0)
    other_ref[...] = jnp.dot(
        spread[KEEP:, :], rows[...], preferred_element_type=F32
    ).astype(BF16)
    own_ref[...] = jnp.dot(spread[:KEEP, :], rows[...], preferred_element_type=F32)


def expect(classes, precisions, live, defocus, row_shifts, column_shifts, images, index, weight, lines):
    smem = pl.BlockSpec(memory_space=pltpu.SMEM)
    vmem = pl.BlockSpec(memory_space=pltpu.VMEM)
    return pl.pallas_call(
        expect_kernel,
        out_shape=(
            jax.ShapeDtypeStruct((KEEP, 3 * BOX), F32),
            jax.ShapeDtypeStruct((KEEP, 3 * BOX), BF16),
            jax.ShapeDtypeStruct((1,), F32),
        ),
        in_specs=[smem] * 6 + [vmem] * 4,
        out_specs=(vmem, vmem, smem),
        scratch_shapes=[
            pltpu.VMEM((2, ROWS), I32),
            pltpu.VMEM((4, ROWS), F32),
            pltpu.VMEM((2 * BOX, LINES), BF16),
            pltpu.VMEM((LINES, ROWS), BF16),
            pltpu.VMEM((ROWS, 2 * BOX), BF16),
            pltpu.VMEM((SHIFTS * SHIFTS, ROWS), F32),
            pltpu.VMEM((BOX, BOX), F32),
            pltpu.VMEM((ROWS, 3 * BOX), BF16),
        ],
        compiler_params=pltpu.CompilerParams(vmem_limit_bytes=48 * 1024 * 1024),
    )(classes, precisions, live, defocus, row_shifts, column_shifts, images, index, weight, lines)


def reduce_kernel(
    scale,
    own_ref,
    other_ref,
    out_ref,
    pair_in,
    x_out,
    x_in,
    y_out,
    y_in,
    z_out,
    z_in,
    pair_send,
    pair_recv,
    x_send,
    x_recv,
    y_send,
    y_recv,
    z_send,
    z_recv,
):
    z, y, x, core = place()
    sibling = device_at(z, y, x, 1 - core)

    def along_x(k):
        return device_at(z, y, (x + k) % NX, core)

    def along_y(k):
        return device_at(z, (y + k) % NY, x, core)

    def along_z(k):
        return device_at((z + k) % NZ, y, x, core)

    barrier = pltpu.get_barrier_semaphore()
    peers = [sibling]
    peers += [along_x(k) for k in range(1, NX)]
    peers += [along_y(k) for k in range(1, NY)]
    peers += [along_z(k) for k in range(1, NZ)]
    for peer in peers:
        pl.semaphore_signal(barrier, inc=1, device_id=peer, device_id_type=MESH)
    pl.semaphore_wait(barrier, len(peers))

    part = NY * NZ
    order = (2, 1, 3, 0)

    def remote(src, dst, send, recv, device):
        return pltpu.make_async_remote_copy(
            src_ref=src,
            dst_ref=dst,
            send_sem=send,
            recv_sem=recv,
            device_id=device,
            device_id_type=MESH,
        )

    pair = {
        k: remote(
            other_ref.at[pl.ds(k * part, part)],
            pair_in.at[k],
            pair_send.at[k],
            pair_recv.at[k],
            sibling,
        )
        for k in order
    }
    for k in order:
        pair[k].start()
    x_copies = []
    for k in order[:3]:
        pair[k].wait_recv()
        x_out[k] = (own_ref[pl.ds(k * part, part), :] + pair_in[k].astype(F32)).astype(BF16)
        copy = remote(x_out.at[k], x_in.at[k], x_send.at[k], x_recv.at[k], along_x(k))
        copy.start()
        x_copies.append(copy)
    pair[0].wait_recv()
    total = own_ref[pl.ds(0, part), :] + pair_in[0].astype(F32)
    for k, copy in zip(order[:3], x_copies):
        copy.wait_recv()
        total = total + x_in[k].astype(F32)

    y_copies = []
    tiles = 3 * BOX // 128
    for k in (4, 3, 5, 2, 6, 1, 7):
        piece = total[k * NZ : (k + 1) * NZ, :]
        y_out[k] = jnp.concatenate(
            [piece[:, t * 128 : (t + 1) * 128] for t in range(tiles)], axis=0
        ).astype(BF16)
        copy = remote(y_out.at[k], y_in.at[k], y_send.at[k], y_recv.at[k], along_y(k))
        copy.start()
        y_copies.append(copy)
    total = jnp.concatenate(
        [total[:NZ, t * 128 : (t + 1) * 128] for t in range(tiles)], axis=0
    )
    for k, copy in zip((4, 3, 5, 2, 6, 1, 7), y_copies):
        copy.wait_recv()
        total = total + y_in[k].astype(F32)
    total = jnp.concatenate([total[t * NZ : (t + 1) * NZ, :] for t in range(tiles)], axis=1)

    z_copies = []
    for k in (4, 3, 5, 2, 6, 1, 7):
        z_out[k] = total[k : k + 1, :]
        copy = remote(z_out.at[k], z_in.at[k], z_send.at[k], z_recv.at[k], along_z(k))
        copy.start()
        z_copies.append(copy)
    total = total[0:1, :]
    for k, copy in zip((4, 3, 5, 2, 6, 1, 7), z_copies):
        copy.wait_recv()
        total = total + z_in[k]
    out_ref[...] = total * scale
    for copy in list(pair.values()) + x_copies + y_copies + z_copies:
        copy.wait_send()


def reduce_volume(own, other, scale):
    vmem = pl.BlockSpec(memory_space=pltpu.VMEM)
    part = NY * NZ
    wide = 3 * BOX
    dma = pltpu.SemaphoreType.DMA
    return pl.pallas_call(
        lambda *refs: reduce_kernel(scale, *refs),
        out_shape=jax.ShapeDtypeStruct((1, wide), F32),
        in_specs=[vmem, vmem],
        out_specs=vmem,
        scratch_shapes=[
            pltpu.VMEM((NX, part, wide), BF16),
            pltpu.VMEM((NX, part, wide), BF16),
            pltpu.VMEM((NX, part, wide), BF16),
            pltpu.VMEM((NY, NZ * wide // 128, 128), BF16),
            pltpu.VMEM((NY, NZ * wide // 128, 128), BF16),
            pltpu.VMEM((NZ, 1, wide), F32),
            pltpu.VMEM((NZ, 1, wide), F32),
            dma((NX,)),
            dma((NX,)),
            dma((NX,)),
            dma((NX,)),
            dma((NY,)),
            dma((NY,)),
            dma((NZ,)),
            dma((NZ,)),
        ],
        compiler_params=pltpu.CompilerParams(collective_id=1, has_side_effects=True),
    )(own, other)


def body(
    particles,
    defocus_class,
    noise_precision,
    live_count,
    defocus,
    reference_lines,
    line_index,
    line_weight,
    row_shifts,
    column_shifts,
):
    lines = gather_lines(reference_lines)
    index = jnp.transpose(line_index, (2, 1, 0)).reshape(2, ROWS)
    weight = jnp.transpose(line_weight, (2, 1, 0)).reshape(2, ROWS)
    own, other, loglik = expect(
        defocus_class,
        noise_precision,
        live_count,
        defocus,
        row_shifts,
        column_shifts,
        particles,
        index,
        weight,
        lines,
    )
    particle_total = particles.shape[0] * lax.axis_size("slab") * lax.axis_size("grp")
    owned = reduce_volume(own, other, LINES / (POSES * particle_total))
    return owned.reshape(1, 3, BOX), loglik


def solution(mesh):
    return jax.shard_map(
        body,
        mesh=mesh,
        in_specs=(
            P(("slab", "grp"), None, None, None),
            P(("slab", "grp")),
            P(("slab", "grp")),
            P("grp"),
            P(),
            P("slab", None, None),
            P(),
            P(),
            P(),
            P(),
        ),
        out_specs=(P(("slab", "grp"), None, None), P(("slab", "grp"))),
        check_vma=False,
    )
```

```python
import functools
import math

import jax
import jax.numpy as jnp
from jax import lax
from jax.experimental import pallas as pl
from jax.experimental.pallas import tpu as pltpu
from jax.sharding import PartitionSpec as P

MESH = pl.DeviceIdType.MESH
EXACT = lax.Precision.HIGHEST
F32 = jnp.float32
BF16 = jnp.bfloat16
I32 = jnp.int32

NX, NY, NZ, Y_LO = 4, 8, 8, 4
SLABS = NZ * Y_LO
LINES = 512
KEEP = LINES // 2
BOX = 256
POSES = 16
GROUP = 16
WIDE = GROUP * POSES
ROWS = POSES * BOX
SHIFTS = 8


def place():
    slab = lax.axis_index("slab")
    grp = lax.axis_index("grp")
    z, y_lo = slab // Y_LO, slab % Y_LO
    y_hi, x, core = grp // (2 * NX), (grp // 2) % NX, grp % 2
    return z, y_hi * Y_LO + y_lo, x, core


def device_at(z, y, x, core):
    return (z * Y_LO + y % Y_LO, (y // Y_LO) * (2 * NX) + x * 2 + core)


def phase_angle(turns):
    signed = ((turns + BOX // 2) & (BOX - 1)) - BOX // 2
    return signed.astype(F32) * (2.0 * math.pi / BOX)


def shift_column(shifts_ref, shape):
    row = lax.broadcasted_iota(I32, shape, 0)
    column = jnp.zeros(shape, I32)
    for t in range(SHIFTS):
        column = jnp.where(row == t, shifts_ref[t], column)
    return column


def slot_of(line, z, y, x, core):
    line_y = ((line >> 3) & 1) * Y_LO + ((line >> 4) & (Y_LO - 1))
    return (
        ((line ^ core) & 1) * KEEP
        + ((((line >> 1) - x) & (NX - 1)) * (NY * NZ))
        + (((line_y - y) & (NY - 1)) * NZ)
        + (((line >> 6) - z) & (NZ - 1))
    )


def held_row(slot, z, y, x, core):
    line_z = (slot + z) & (NZ - 1)
    line_y = ((slot >> 3) + y) & (NY - 1)
    line_x = ((slot >> 6) + x) & (NX - 1)
    line_core = ((slot >> 8) ^ core) & 1
    return (line_y & 3) * (NZ * 16) + line_z * 16 + (line_y >> 2) * 8 + line_x * 2 + line_core


def expect_kernel(
    scale,
    class_ref,
    precision_ref,
    live_ref,
    defocus_ref,
    row_shift_ref,
    column_shift_ref,
    image_ref,
    index_ref,
    weight_ref,
    lines_ref,
    out_ref,
    loglik_ref,
    held,
    slots,
    weights,
    lines_t,
    spread,
    spread_low,
    slices,
    shifted,
    phases,
    squares,
    rows,
    sums,
    strided,
    pair_out,
    pair_in,
    ax_out,
    ax_in,
    by_out,
    by_in,
    cz_out,
    cz_in,
    ay_out,
    ay_in,
    bx_out,
    bx_in,
    cx_out,
    cx_in,
    last_out,
    last_in,
    gather_send,
    gather_recv,
    swap_send,
    swap_recv,
    pair_send,
    pair_recv,
    hop_send,
    hop_recv,
):
    z, y, x, core = place()
    y_lo = y % Y_LO
    sibling = device_at(z, y, x, 1 - core)

    def along_x(k):
        return device_at(z, y, (x + k) % NX, core)

    def along_y(k):
        return device_at(z, (y + NY + k) % NY, x, core)

    def along_z(k):
        return device_at((z + k) % NZ, y, x, core)

    def remote(src, dst, send, recv, device):
        return pltpu.make_async_remote_copy(
            src_ref=src,
            dst_ref=dst,
            send_sem=send,
            recv_sem=recv,
            device_id=device,
            device_id_type=MESH,
        )

    barrier = pltpu.get_barrier_semaphore()
    peers = [sibling]
    peers += [along_x(k) for k in range(1, NX)]
    peers += [along_y(k) for k in range(1, NY)]
    peers += [along_z(k) for k in range(1, NZ)]
    for peer in peers:
        pl.semaphore_signal(barrier, inc=1, device_id=peer, device_id_type=MESH)

    both = lines_ref[...]
    held[core, y_lo, z] = jnp.where(core == 0, both[:, 0, :], both[:, 1, :])

    alive = jnp.where(0 < live_ref[0], 1.0, 0.0).astype(F32)
    chosen = defocus_ref[class_ref[0]]

    lane_y = lax.broadcasted_iota(I32, (SHIFTS, BOX), 1) - BOX // 2
    angle_y = phase_angle(lane_y * shift_column(column_shift_ref, (SHIFTS, BOX)))
    cos_y = jnp.cos(angle_y)
    sin_y = jnp.sin(angle_y)
    freq_y = (lax.broadcasted_iota(I32, (GROUP, BOX), 1) - BOX // 2).astype(F32) / BOX
    row_in_group = lax.broadcasted_iota(I32, (GROUP, BOX), 0)

    def shift_rows(g, carry):
        at = pl.ds(pl.multiple_of(g * WIDE, WIDE), WIDE)
        kx = pl.ds(pl.multiple_of(g * GROUP, GROUP), GROUP)
        freq_x = (row_in_group + (g * GROUP - BOX // 2)).astype(F32) / BOX
        ctf = -jnp.sin(chosen * (freq_x * freq_x + freq_y * freq_y) + 0.1) * alive
        squares[kx, :] = ctf * ctf
        real = ctf * image_ref[0, 0, kx, :].astype(F32)
        imag = ctf * image_ref[0, 1, kx, :].astype(F32)
        blocks = []
        for k in range(GROUP):
            real_row = real[k : k + 1, :]
            imag_row = imag[k : k + 1, :]
            shift_re = real_row * cos_y + imag_row * sin_y
            shift_im = real_row * sin_y - imag_row * cos_y
            blocks.append(jnp.concatenate([shift_re, -shift_im], axis=1))
            blocks.append(jnp.concatenate([shift_im, shift_re], axis=1))
        shifted[at, :] = jnp.concatenate(blocks, axis=0).astype(BF16)
        return carry

    lax.fori_loop(0, BOX // GROUP, shift_rows, 0)

    pl.semaphore_wait(barrier, len(peers))
    gather_z = []
    for k in (4, 3, 5, 2, 6, 1, 7):
        copy = remote(
            held.at[core, y_lo, z],
            held.at[core, y_lo, z],
            gather_send.at[k],
            gather_recv.at[k],
            along_z(k),
        )
        copy.start()
        gather_z.append(copy)

    lane = lax.broadcasted_iota(I32, (SHIFTS, ROWS), 1)
    freq = (lane >> 4) - BOX // 2
    part = (lane >> 3) & 1
    turns = freq * shift_column(row_shift_ref, (SHIFTS, ROWS)) + part * (BOX // 4)
    row_phase = jnp.cos(phase_angle(turns))
    for t in range(SHIFTS):
        phases[pl.ds(t * SHIFTS, SHIFTS), :] = jnp.where((lane & 7) == t, row_phase, 0.0)

    first = slot_of(index_ref[0:1, :], z, y, x, core)
    second = slot_of(index_ref[1:2, :], z, y, x, core)
    same = first == second
    first_weight = jnp.where(same, weight_ref[0:1, :] + weight_ref[1:2, :], weight_ref[0:1, :])
    second_weight = jnp.where(same, 0.0, weight_ref[1:2, :])
    slots[0:1, :] = first
    slots[1:2, :] = second
    first_high = first_weight.astype(BF16).astype(F32)
    second_high = second_weight.astype(BF16).astype(F32)
    weights[0:1, :] = first_high
    weights[1:2, :] = second_high
    weights[2:3, :] = first_weight - first_high
    weights[3:4, :] = second_weight - second_high
    slot_row = lax.broadcasted_iota(I32, (LINES, WIDE), 0)

    def spread_rows(g, carry):
        at = pl.ds(pl.multiple_of(g * WIDE, WIDE), WIDE)
        is_first = slot_row == slots[0:1, at]
        is_second = slot_row == slots[1:2, at]
        high = jnp.where(is_first, weights[0:1, at], jnp.where(is_second, weights[1:2, at], 0.0))
        low = jnp.where(is_first, weights[2:3, at], jnp.where(is_second, weights[3:4, at], 0.0))
        spread[:, at] = high.astype(BF16)
        spread_low[:, at] = low.astype(BF16)
        return carry

    lax.fori_loop(0, 5, spread_rows, 0)
    for copy in gather_z:
        copy.wait_recv()
    far = 2 - 4 * core
    swaps = []

    def swap(d, residue):
        copy = remote(
            held.at[core, residue],
            held.at[core, residue],
            swap_send.at[d],
            swap_recv.at[d],
            sibling,
        )
        copy.start()
        swaps.append(copy)

    gather_y = []
    for d, step in ((2, far), (1, 1), (3, -1)):
        copy = remote(
            held.at[core, y_lo],
            held.at[core, y_lo],
            gather_send.at[NZ + d],
            gather_recv.at[NZ + d],
            along_y(step),
        )
        copy.start()
        gather_y.append(copy)
    swap(0, y_lo)
    lax.fori_loop(5, BOX // GROUP, spread_rows, 0)

    for copy, (d, residue) in zip(gather_y, ((2, y_lo + 2), (1, y_lo + 3), (3, y_lo + 1))):
        copy.wait_recv()
        swap(d, residue % Y_LO)

    slot_rows = held_row(lax.broadcasted_iota(I32, (1, LINES), 1), z, y, x, core)
    order = jnp.where(
        lax.broadcasted_iota(I32, (LINES, LINES), 0) == slot_rows, 1.0, 0.0
    ).astype(BF16)

    def transpose_half(c):
        lines_t[pl.ds(pl.multiple_of(c * BOX, BOX), BOX), :] = lax.dot_general(
            held[c].reshape(LINES, BOX),
            order,
            (((0,), (0,)), ((), ())),
            preferred_element_type=F32,
        ).astype(BF16)

    def slice_rows(c, at):
        half = pl.ds(pl.multiple_of(c * BOX, BOX), BOX)
        lines_half = lines_t[half, :]
        slices[half, at] = (
            jnp.dot(lines_half, spread[:, at], preferred_element_type=F32)
            + jnp.dot(lines_half, spread_low[:, at], preferred_element_type=F32)
        ).astype(BF16)

    def own_slices(g, carry):
        slice_rows(core, pl.ds(pl.multiple_of(g * WIDE, WIDE), WIDE))
        return carry

    transpose_half(core)
    lax.fori_loop(0, BOX // GROUP, own_slices, 0)
    for copy in swaps:
        copy.wait_recv()
    transpose_half(1 - core)

    one_row = (lax.broadcasted_iota(I32, (WIDE, WIDE), 0) >> 4) == (
        lax.broadcasted_iota(I32, (WIDE, WIDE), 1) >> 4
    )

    def correlate(g, corr):
        at = pl.ds(pl.multiple_of(g * WIDE, WIDE), WIDE)
        slice_rows(1 - core, at)
        products = jnp.dot(shifted[at, :], slices[:, at], preferred_element_type=F32)
        return corr + jnp.dot(
            phases[:, at],
            jnp.where(one_row, products, 0.0),
            precision=EXACT,
            preferred_element_type=F32,
        )

    corr = lax.fori_loop(
        0, BOX // GROUP, correlate, jnp.zeros((SHIFTS * SHIFTS, WIDE), F32)
    )
    corr = corr[:, : WIDE // 2] + corr[:, WIDE // 2 :]
    for step in (64, 32, 16):
        corr = corr + pltpu.roll(corr, step, 1)
    score = corr * (precision_ref[0] / BOX)
    top = jnp.max(score, axis=(0, 1), keepdims=True)
    terms = jnp.exp(score - top)
    total = jnp.sum(terms, axis=(0, 1), keepdims=True) * (1.0 / 8.0)
    posterior = terms / total
    loglik_ref[0] = ((top + jnp.log(total)) * alive)[0, 0]
    posterior_t = posterior.T
    mass = jnp.sum(posterior_t, axis=1, keepdims=True)[:POSES]

    pairs = []

    def spread_part(c):
        columns = rows[:, c * BOX : (c + 1) * BOX]
        pair_out[c] = jnp.dot(spread[KEEP:, :], columns, preferred_element_type=F32).astype(BF16)
        copy = remote(pair_out.at[c], pair_in.at[c], pair_send.at[c], pair_recv.at[c], sibling)
        copy.start()
        pairs.append(copy)
        sums[c] = jnp.dot(spread[:KEEP, :], columns, preferred_element_type=F32)

    def square_rows(g, carry):
        at = pl.ds(pl.multiple_of(g * WIDE, WIDE), WIDE)
        square = squares[pl.ds(pl.multiple_of(g * GROUP, GROUP), GROUP), :]
        rows[at, 2 * BOX :] = jnp.concatenate(
            [square[k : k + 1, :] * mass for k in range(GROUP)], axis=0
        ).astype(BF16)
        return carry

    def insert(g, carry):
        at = pl.ds(pl.multiple_of(g * WIDE, WIDE), WIDE)
        weight = jnp.dot(posterior_t, phases[:, at], precision=EXACT, preferred_element_type=F32)
        weight = jnp.where(one_row, jnp.concatenate([weight, weight], axis=0), 0.0).astype(BF16)
        rows[at, : 2 * BOX] = jnp.dot(
            weight, shifted[at, :], preferred_element_type=F32
        ).astype(BF16)
        return carry

    hops = []

    def hop(number, src, dst, device):
        copy = remote(src, dst, hop_send.at[number], hop_recv.at[number], device)
        copy.start()
        hops.append(copy)
        return copy

    def pack(piece):
        return jnp.concatenate([piece[:, :128], piece[:, 128:]], axis=0)

    def unpack(piece):
        return jnp.concatenate([piece[:NZ, :], piece[NZ:, :]], axis=1)

    ring8 = (4, 3, 5, 2, 6, 1, 7)
    ring4 = (2, 1, 3)

    lax.fori_loop(0, BOX // GROUP, square_rows, 0)
    spread_part(2)
    lax.fori_loop(0, BOX // GROUP, insert, 0)
    pairs[0].wait_recv()
    c_sum = sums[2] + pair_in[2].astype(F32)
    for half in range(2):
        strided[half] = c_sum[:, half * 128 : (half + 1) * 128]

    def c_rows(k):
        rows_k = pl.ds(k, NX * NY, NZ)
        return jnp.concatenate([strided[0, rows_k, :], strided[1, rows_k, :]], axis=1)

    c_hops = []
    for k in ring8:
        cz_out[k] = c_rows(k).astype(BF16)
        c_hops.append(hop(k, cz_out.at[k], cz_in.at[k], along_z(k)))
    spread_part(0)
    spread_part(1)

    pairs[1].wait_recv()
    b_sum = (sums[0] + pair_in[0].astype(F32)).reshape(NX, NY, NZ, BOX)
    b_hops = []
    for k in ring8:
        by_out[k] = b_sum[:, k].reshape(NX * NZ, BOX).astype(BF16)
        b_hops.append(hop(NZ + k, by_out.at[k], by_in.at[k], along_y(k)))
    b_sum = b_sum[:, 0].reshape(NX * NZ, BOX)
    pairs[2].wait_recv()
    a_sum = (sums[1] + pair_in[1].astype(F32)).reshape(NX, NY * NZ, BOX)
    a_hops = []
    for k in ring4:
        ax_out[k] = a_sum[k].astype(BF16)
        a_hops.append(hop(2 * NZ + k, ax_out.at[k], ax_in.at[k], along_x(k)))
    a_sum = a_sum[0]

    c_sum = c_rows(0)
    for k, copy in zip(ring8, c_hops):
        copy.wait_recv()
        c_sum = c_sum + cz_in[k].astype(F32)
    c_hops = []
    for k in ring4:
        cx_out[k] = pack(c_sum[k * NY : (k + 1) * NY, :]).astype(BF16)
        c_hops.append(hop(20 + k, cx_out.at[k], cx_in.at[k], along_x(k)))
    for k, copy in zip(ring8, b_hops):
        copy.wait_recv()
        b_sum = b_sum + by_in[k].astype(F32)
    b_hops = []
    for k in ring4:
        bx_out[k] = pack(b_sum[k * NZ : (k + 1) * NZ, :]).astype(BF16)
        b_hops.append(hop(24 + k, bx_out.at[k], bx_in.at[k], along_x(k)))
    for k, copy in zip(ring4, a_hops):
        copy.wait_recv()
        a_sum = a_sum + ax_in[k].astype(F32)
    a_hops = []
    for k in ring8:
        ay_out[k] = pack(a_sum[k * NZ : (k + 1) * NZ, :]).astype(BF16)
        a_hops.append(hop(28 + k, ay_out.at[k], ay_in.at[k], along_y(k)))

    def last(part, total, along):
        copies = []
        for k in ring8:
            last_out[part, k] = total[k : k + 1, :]
            copies.append(
                hop(36 + part * NZ + k, last_out.at[part, k], last_in.at[part, k], along(k))
            )
        return total[0:1, :], copies

    c_sum = c_sum[:NY, :]
    for k, copy in zip(ring4, c_hops):
        copy.wait_recv()
        c_sum = c_sum + unpack(cx_in[k].astype(F32))
    c_sum, c_hops = last(2, c_sum, along_y)
    b_sum = b_sum[:NZ, :]
    for k, copy in zip(ring4, b_hops):
        copy.wait_recv()
        b_sum = b_sum + unpack(bx_in[k].astype(F32))
    b_sum, b_hops = last(0, b_sum, along_z)
    a_sum = a_sum[:NZ, :]
    for k, copy in zip(ring8, a_hops):
        copy.wait_recv()
        a_sum = a_sum + unpack(ay_in[k].astype(F32))
    a_sum, a_hops = last(1, a_sum, along_z)
    for part, total, copies in ((2, c_sum, c_hops), (0, b_sum, b_hops), (1, a_sum, a_hops)):
        for k, copy in zip(ring8, copies):
            copy.wait_recv()
            total = total + last_in[part, k]
        out_ref[:, part * BOX : (part + 1) * BOX] = total * scale
    for copy in gather_z + gather_y + swaps + pairs + hops:
        copy.wait_send()


def expect(scale, *operands):
    smem = pl.BlockSpec(memory_space=pltpu.SMEM)
    vmem = pl.BlockSpec(memory_space=pltpu.VMEM)
    dma = pltpu.SemaphoreType.DMA
    hop_count = 36 + 3 * NZ

    def both_ways(shape, kind):
        return [pltpu.VMEM(shape, kind), pltpu.VMEM(shape, kind)]

    return pl.pallas_call(
        functools.partial(expect_kernel, scale),
        out_shape=(
            jax.ShapeDtypeStruct((1, 3 * BOX), F32),
            jax.ShapeDtypeStruct((1,), F32),
        ),
        in_specs=[smem] * 6 + [vmem] * 4,
        out_specs=(vmem, smem),
        scratch_shapes=[
            pltpu.VMEM((2, Y_LO, NZ, 16, BOX), BF16),
            pltpu.VMEM((2, ROWS), I32),
            pltpu.VMEM((4, ROWS), F32),
            pltpu.VMEM((2 * BOX, LINES), BF16),
            pltpu.VMEM((LINES, ROWS), BF16),
            pltpu.VMEM((LINES, ROWS), BF16),
            pltpu.VMEM((2 * BOX, ROWS), BF16),
            pltpu.VMEM((ROWS, 2 * BOX), BF16),
            pltpu.VMEM((SHIFTS * SHIFTS, ROWS), F32),
            pltpu.VMEM((BOX, BOX), F32),
            pltpu.VMEM((ROWS, 3 * BOX), BF16),
            pltpu.VMEM((3, KEEP, BOX), F32),
            pltpu.VMEM((2, KEEP, BOX // 2), F32),
        ]
        + both_ways((3, KEEP, BOX), BF16)
        + both_ways((NX, NY * NZ, BOX), BF16)
        + both_ways((NY, NX * NZ, BOX), BF16)
        + both_ways((NZ, NX * NY, BOX), BF16)
        + both_ways((NY, 2 * NZ, BOX // 2), BF16)
        + both_ways((NX, 2 * NZ, BOX // 2), BF16)
        + both_ways((NX, 2 * NY, BOX // 2), BF16)
        + both_ways((3, NZ, 1, BOX), F32)
        + [
            dma((NZ + Y_LO,)),
            dma((NZ + Y_LO,)),
            dma((Y_LO,)),
            dma((Y_LO,)),
            dma((3,)),
            dma((3,)),
            dma((hop_count,)),
            dma((hop_count,)),
        ],
        compiler_params=pltpu.CompilerParams(
            collective_id=0, has_side_effects=True, vmem_limit_bytes=48 * 1024 * 1024
        ),
    )(*operands)


def body(
    particles,
    defocus_class,
    noise_precision,
    live_count,
    defocus,
    reference_lines,
    line_index,
    line_weight,
    row_shifts,
    column_shifts,
):
    index = jnp.transpose(line_index, (2, 1, 0)).reshape(2, ROWS)
    weight = jnp.transpose(line_weight, (2, 1, 0)).reshape(2, ROWS)
    particle_total = particles.shape[0] * lax.axis_size("slab") * lax.axis_size("grp")
    owned, loglik = expect(
        LINES / (POSES * particle_total),
        defocus_class,
        noise_precision,
        live_count,
        defocus,
        row_shifts,
        column_shifts,
        particles,
        index,
        weight,
        reference_lines,
    )
    return owned.reshape(1, 3, BOX), loglik


def solution(mesh):
    return jax.shard_map(
        body,
        mesh=mesh,
        in_specs=(
            P(("slab", "grp"), None, None, None),
            P(("slab", "grp")),
            P(("slab", "grp")),
            P("grp"),
            P(),
            P("slab", None, None),
            P(),
            P(),
            P(),
            P(),
        ),
        out_specs=(P(("slab", "grp"), None, None), P(("slab", "grp"))),
        check_vma=False,
    )
```

```python
import functools
import math

import jax
import jax.numpy as jnp
from jax import lax
from jax.experimental import pallas as pl
from jax.experimental.pallas import tpu as pltpu
from jax.sharding import PartitionSpec as P

MESH = pl.DeviceIdType.MESH
EXACT = lax.Precision.HIGHEST
F32 = jnp.float32
BF16 = jnp.bfloat16
I32 = jnp.int32

NX, NY, NZ, Y_LO = 4, 8, 8, 4
SLABS = NZ * Y_LO
LINES = 512
KEEP = LINES // 2
BOX = 256
POSES = 16
GROUP = 16
WIDE = GROUP * POSES
ROWS = POSES * BOX
SHIFTS = 8


def place():
    slab = lax.axis_index("slab")
    grp = lax.axis_index("grp")
    z, y_lo = slab // Y_LO, slab % Y_LO
    y_hi, x, core = grp // (2 * NX), (grp // 2) % NX, grp % 2
    return z, y_hi * Y_LO + y_lo, x, core


def device_at(z, y, x, core):
    return (z * Y_LO + y % Y_LO, (y // Y_LO) * (2 * NX) + x * 2 + core)


def phase_angle(turns):
    signed = ((turns + BOX // 2) & (BOX - 1)) - BOX // 2
    return signed.astype(F32) * (2.0 * math.pi / BOX)


def shift_column(shifts_ref, shape):
    row = lax.broadcasted_iota(I32, shape, 0)
    column = jnp.zeros(shape, I32)
    for t in range(SHIFTS):
        column = jnp.where(row == t, shifts_ref[t], column)
    return column


def slot_of(line, z, y, x, core):
    line_y = ((line >> 3) & 1) * Y_LO + ((line >> 4) & (Y_LO - 1))
    return (
        ((line ^ core) & 1) * KEEP
        + ((((line >> 1) - x) & (NX - 1)) * (NY * NZ))
        + (((line_y - y) & (NY - 1)) * NZ)
        + (((line >> 6) - z) & (NZ - 1))
    )


def held_row(slot, z, y, x, core):
    line_z = (slot + z) & (NZ - 1)
    line_y = ((slot >> 3) + y) & (NY - 1)
    line_x = ((slot >> 6) + x) & (NX - 1)
    line_core = ((slot >> 8) ^ core) & 1
    return (line_y & 3) * (NZ * 16) + line_z * 16 + (line_y >> 2) * 8 + line_x * 2 + line_core


def expect_kernel(
    scale,
    class_ref,
    precision_ref,
    live_ref,
    defocus_ref,
    row_shift_ref,
    column_shift_ref,
    image_ref,
    index_ref,
    weight_ref,
    lines_ref,
    out_ref,
    loglik_ref,
    held,
    slots,
    weights,
    lines_t,
    spread,
    slices,
    shifted,
    phases,
    squares,
    product_high,
    product_low,
    turned,
    rows,
    sums,
    strided,
    pair_out,
    pair_in,
    ax_out,
    ax_in,
    by_out,
    by_in,
    cz_out,
    cz_in,
    ay_out,
    ay_in,
    bx_out,
    bx_in,
    cx_out,
    cx_in,
    last_out,
    last_in,
    gather_send,
    gather_recv,
    swap_send,
    swap_recv,
    pair_send,
    pair_recv,
    hop_send,
    hop_recv,
):
    z, y, x, core = place()
    y_lo = y % Y_LO
    sibling = device_at(z, y, x, 1 - core)

    def along_x(k):
        return device_at(z, y, (x + k) % NX, core)

    def along_y(k):
        return device_at(z, (y + NY + k) % NY, x, core)

    def along_z(k):
        return device_at((z + k) % NZ, y, x, core)

    def remote(src, dst, send, recv, device):
        return pltpu.make_async_remote_copy(
            src_ref=src,
            dst_ref=dst,
            send_sem=send,
            recv_sem=recv,
            device_id=device,
            device_id_type=MESH,
        )

    barrier = pltpu.get_barrier_semaphore()
    peers = [sibling]
    peers += [along_x(k) for k in range(1, NX)]
    peers += [along_y(k) for k in range(1, NY)]
    peers += [along_z(k) for k in range(1, NZ)]
    for peer in peers:
        pl.semaphore_signal(barrier, inc=1, device_id=peer, device_id_type=MESH)

    both = lines_ref[...]
    held[core, y_lo, z] = jnp.where(core == 0, both[:, 0, :], both[:, 1, :])

    alive = jnp.where(0 < live_ref[0], 1.0, 0.0).astype(F32)
    chosen = defocus_ref[class_ref[0]]

    lane_y = lax.broadcasted_iota(I32, (SHIFTS, BOX), 1) - BOX // 2
    angle_y = phase_angle(lane_y * shift_column(column_shift_ref, (SHIFTS, BOX)))
    cos_y = jnp.cos(angle_y)
    sin_y = jnp.sin(angle_y)
    freq_y = (lax.broadcasted_iota(I32, (GROUP, BOX), 1) - BOX // 2).astype(F32) / BOX
    row_in_group = lax.broadcasted_iota(I32, (GROUP, BOX), 0)

    def shift_rows(g, carry):
        at = pl.ds(pl.multiple_of(g * WIDE, WIDE), WIDE)
        kx = pl.ds(pl.multiple_of(g * GROUP, GROUP), GROUP)
        freq_x = (row_in_group + (g * GROUP - BOX // 2)).astype(F32) / BOX
        ctf = -jnp.sin(chosen * (freq_x * freq_x + freq_y * freq_y) + 0.1) * alive
        squares[kx, :] = ctf * ctf
        real = ctf * image_ref[0, 0, kx, :].astype(F32)
        imag = ctf * image_ref[0, 1, kx, :].astype(F32)
        blocks = []
        for k in range(GROUP):
            real_row = real[k : k + 1, :]
            imag_row = imag[k : k + 1, :]
            shift_re = real_row * cos_y + imag_row * sin_y
            shift_im = real_row * sin_y - imag_row * cos_y
            blocks.append(jnp.concatenate([shift_re, -shift_im], axis=1))
            blocks.append(jnp.concatenate([shift_im, shift_re], axis=1))
        shifted[at, :] = jnp.concatenate(blocks, axis=0).astype(BF16)
        return carry

    lax.fori_loop(0, BOX // GROUP, shift_rows, 0)

    pl.semaphore_wait(barrier, len(peers))
    gather_z = []
    for k in (4, 3, 5, 2, 6, 1, 7):
        copy = remote(
            held.at[core, y_lo, z],
            held.at[core, y_lo, z],
            gather_send.at[k],
            gather_recv.at[k],
            along_z(k),
        )
        copy.start()
        gather_z.append(copy)

    lane = lax.broadcasted_iota(I32, (SHIFTS, ROWS), 1)
    freq = (lane >> 4) - BOX // 2
    part = (lane >> 3) & 1
    turns = freq * shift_column(row_shift_ref, (SHIFTS, ROWS)) + part * (BOX // 4)
    row_phase = jnp.cos(phase_angle(turns))
    row_high = row_phase.astype(BF16).astype(F32)
    row_low = row_phase - row_high
    for t in range(0, SHIFTS, 2):
        for base, table in ((0, row_high), (SHIFTS * SHIFTS, row_low)):
            phases[pl.ds(base + t * SHIFTS, 2 * SHIFTS), :] = jnp.concatenate(
                [jnp.where((lane & 7) == t + u, table, 0.0) for u in range(2)], axis=0
            ).astype(BF16)

    first = slot_of(index_ref[:, 0, :], z, y, x, core)
    second = slot_of(index_ref[:, 1, :], z, y, x, core)
    first_weight = weight_ref[:, 0, :]
    second_weight = weight_ref[:, 1, :]
    same = first == second
    first_weight = jnp.where(same, first_weight + second_weight, first_weight)
    second_weight = jnp.where(same, 0.0, second_weight)
    first_high = first_weight.astype(BF16).astype(F32)
    second_high = second_weight.astype(BF16).astype(F32)
    tables = jnp.concatenate(
        [
            (first >> 4).astype(F32),
            (first & 15).astype(F32),
            (second >> 4).astype(F32),
            (second & 15).astype(F32),
            first_high,
            second_high,
            first_weight - first_high,
            second_weight - second_high,
        ],
        axis=0,
    ).astype(BF16)
    table_lane = lax.broadcasted_iota(I32, (BOX, WIDE), 1) >> 4
    table_row = lax.broadcasted_iota(I32, (BOX, WIDE), 0)
    pose_row = lax.broadcasted_iota(I32, (POSES, WIDE), 0) == (
        lax.broadcasted_iota(I32, (POSES, WIDE), 1) & (POSES - 1)
    )

    def table_rows(g, carry):
        at = pl.ds(pl.multiple_of(g * WIDE, WIDE), WIDE)
        chosen_row = jnp.where(table_row == table_lane + g * GROUP, 1.0, 0.0).astype(BF16)
        wide = jnp.dot(tables, chosen_row, preferred_element_type=F32)
        found = [
            jnp.sum(
                jnp.where(pose_row, wide[n * POSES : (n + 1) * POSES, :], 0.0),
                axis=0,
                keepdims=True,
            )
            for n in range(8)
        ]
        slots[0:1, at] = (found[0] * 16.0 + found[1]).astype(I32)
        slots[1:2, at] = (found[2] * 16.0 + found[3]).astype(I32)
        for n in range(4):
            weights[n : n + 1, at] = found[4 + n]
        return carry

    lax.fori_loop(0, BOX // GROUP, table_rows, 0, unroll=2)
    slot_row = lax.broadcasted_iota(I32, (LINES, WIDE), 0)

    def spread_rows(g, carry):
        at = pl.ds(pl.multiple_of(g * WIDE, WIDE), WIDE)
        is_first = slot_row == slots[0:1, at]
        is_second = slot_row == slots[1:2, at]
        high = jnp.where(is_first, weights[0:1, at], jnp.where(is_second, weights[1:2, at], 0.0))
        low = jnp.where(is_first, weights[2:3, at], jnp.where(is_second, weights[3:4, at], 0.0))
        spread[:LINES, at] = high.astype(BF16)
        spread[LINES:, at] = low.astype(BF16)
        return carry

    lax.fori_loop(0, 5, spread_rows, 0)
    for copy in gather_z:
        copy.wait_recv()
    far = 2 - 4 * core
    swaps = []

    def swap(d, residue):
        copy = remote(
            held.at[core, residue],
            held.at[core, residue],
            swap_send.at[d],
            swap_recv.at[d],
            sibling,
        )
        copy.start()
        swaps.append(copy)

    gather_y = []
    for d, step in ((2, far), (1, 1), (3, -1)):
        copy = remote(
            held.at[core, y_lo],
            held.at[core, y_lo],
            gather_send.at[NZ + d],
            gather_recv.at[NZ + d],
            along_y(step),
        )
        copy.start()
        gather_y.append(copy)
    swap(0, y_lo)
    lax.fori_loop(5, BOX // GROUP, spread_rows, 0)

    for copy, (d, residue) in zip(gather_y, ((2, y_lo + 2), (1, y_lo + 3), (3, y_lo + 1))):
        copy.wait_recv()
        swap(d, residue % Y_LO)

    slot_rows = held_row(lax.broadcasted_iota(I32, (1, LINES), 1), z, y, x, core)
    order = jnp.where(
        lax.broadcasted_iota(I32, (LINES, LINES), 0) == slot_rows, 1.0, 0.0
    ).astype(BF16)

    def transpose_half(c):
        half = lax.dot_general(
            held[c].reshape(LINES, BOX),
            order,
            (((0,), (0,)), ((), ())),
            preferred_element_type=F32,
        ).astype(BF16)
        lines_t[pl.ds(pl.multiple_of(c * BOX, BOX), BOX), :] = jnp.concatenate(
            [half, half], axis=1
        )

    def slice_half(c):
        half = pl.ds(pl.multiple_of(c * BOX, BOX), BOX)

        def step(n, carry):
            at = pl.ds(pl.multiple_of(n * 4 * WIDE, 4 * WIDE), 4 * WIDE)
            slices[half, at] = jnp.dot(
                lines_t[half, :], spread[:, at], preferred_element_type=F32
            ).astype(BF16)
            return carry

        lax.fori_loop(0, ROWS // (4 * WIDE), step, 0)

    transpose_half(core)
    slice_half(core)
    for copy in swaps:
        copy.wait_recv()
    transpose_half(1 - core)
    slice_half(1 - core)

    lane_row = lax.broadcasted_iota(I32, (GROUP, 128), 1) >> 4
    nothing = jnp.zeros((GROUP, 128), BF16)

    def diagonal(k, tile):
        return jnp.concatenate([tile, nothing] if k < GROUP // 2 else [nothing, tile], axis=1)

    def correlate(g, carry):
        at = pl.ds(pl.multiple_of(g * WIDE, WIDE), WIDE)
        products = jnp.dot(shifted[at, :], slices[:, at], preferred_element_type=F32)
        highs, lows = [], []
        for k in range(GROUP):
            lane_at = k // (GROUP // 2) * 128
            block = products[k * GROUP : (k + 1) * GROUP, lane_at : lane_at + 128]
            block = jnp.where(lane_row == k % (GROUP // 2), block, 0.0)
            high = block.astype(BF16)
            highs.append(diagonal(k, high))
            lows.append(diagonal(k, (block - high.astype(F32)).astype(BF16)))
        product_high[at, :] = jnp.concatenate(highs, axis=0)
        product_low[at, :] = jnp.concatenate(lows, axis=0)
        return carry

    lax.fori_loop(0, BOX // GROUP, correlate, 0, unroll=4)
    corr = jnp.dot(phases[...], product_high[...], preferred_element_type=F32)
    corr = corr[: SHIFTS * SHIFTS] + corr[SHIFTS * SHIFTS :]
    corr = corr + jnp.dot(
        phases[: SHIFTS * SHIFTS, :], product_low[...], preferred_element_type=F32
    )
    corr = corr[:, : WIDE // 2] + corr[:, WIDE // 2 :]
    for step in (64, 32, 16):
        corr = corr + pltpu.roll(corr, step, 1)
    score = corr * (precision_ref[0] / BOX)
    top = jnp.max(score, axis=(0, 1), keepdims=True)
    terms = jnp.exp(score - top)
    total = jnp.sum(terms, axis=(0, 1), keepdims=True) * (1.0 / 8.0)
    posterior = terms / total
    loglik_ref[0] = ((top + jnp.log(total)) * alive)[0, 0]
    posterior_t = posterior.T[:POSES]
    mass = jnp.sum(posterior_t, axis=1, keepdims=True)

    pairs = []

    def spread_part(c):
        columns = rows[:, c * BOX : (c + 1) * BOX]
        pair_out[c] = jnp.dot(spread[KEEP:LINES, :], columns, preferred_element_type=F32).astype(BF16)
        copy = remote(pair_out.at[c], pair_in.at[c], pair_send.at[c], pair_recv.at[c], sibling)
        copy.start()
        pairs.append(copy)
        sums[c] = jnp.dot(spread[:KEEP, :], columns, preferred_element_type=F32)

    def square_rows(g, carry):
        at = pl.ds(pl.multiple_of(g * WIDE, WIDE), WIDE)
        square = squares[pl.ds(pl.multiple_of(g * GROUP, GROUP), GROUP), :]
        rows[at, 2 * BOX :] = jnp.concatenate(
            [square[k : k + 1, :] * mass for k in range(GROUP)], axis=0
        ).astype(BF16)
        return carry

    def turn_poses():
        high = posterior_t.astype(BF16)
        low = (posterior_t - high.astype(F32)).astype(BF16)
        parts = jnp.concatenate(
            [
                jnp.concatenate([high, high], axis=1),
                jnp.concatenate([low, jnp.zeros_like(low)], axis=1),
            ],
            axis=0,
        )
        both_parts = jnp.dot(parts, phases[...], preferred_element_type=F32)
        turned[...] = (both_parts[:POSES] + both_parts[POSES:]).astype(BF16)

    def insert(g, carry):
        at = pl.ds(pl.multiple_of(g * WIDE, WIDE), WIDE)
        turns_g = turned[:, at]
        weight = jnp.concatenate(
            [
                diagonal(
                    k,
                    jnp.where(
                        lane_row == k % (GROUP // 2),
                        turns_g[:, k // (GROUP // 2) * 128 : k // (GROUP // 2) * 128 + 128],
                        nothing,
                    ),
                )
                for k in range(GROUP)
            ],
            axis=0,
        )
        rows[at, : 2 * BOX] = jnp.dot(
            weight, shifted[at, :], preferred_element_type=F32
        ).astype(BF16)
        return carry

    hops = []

    def hop(number, src, dst, device):
        copy = remote(src, dst, hop_send.at[number], hop_recv.at[number], device)
        copy.start()
        hops.append(copy)
        return copy

    def pack(piece):
        return jnp.concatenate([piece[:, :128], piece[:, 128:]], axis=0)

    def unpack(piece):
        return jnp.concatenate([piece[:NZ, :], piece[NZ:, :]], axis=1)

    ring8 = (4, 3, 5, 2, 6, 1, 7)
    ring4 = (2, 1, 3)

    lax.fori_loop(0, BOX // GROUP, square_rows, 0, unroll=2)
    spread_part(2)
    turn_poses()
    lax.fori_loop(0, BOX // GROUP, insert, 0, unroll=4)
    pairs[0].wait_recv()
    c_sum = sums[2] + pair_in[2].astype(F32)
    for half in range(2):
        strided[half] = c_sum[:, half * 128 : (half + 1) * 128]

    def c_rows(k):
        rows_k = pl.ds(k, NX * NY, NZ)
        return jnp.concatenate([strided[0, rows_k, :], strided[1, rows_k, :]], axis=1)

    c_hops = []
    for k in ring8:
        cz_out[k] = c_rows(k).astype(BF16)
        c_hops.append(hop(k, cz_out.at[k], cz_in.at[k], along_z(k)))
    spread_part(0)
    spread_part(1)

    pairs[1].wait_recv()
    b_sum = (sums[0] + pair_in[0].astype(F32)).reshape(NX, NY, NZ, BOX)
    b_hops = []
    for k in ring8:
        by_out[k] = b_sum[:, k].reshape(NX * NZ, BOX).astype(BF16)
        b_hops.append(hop(NZ + k, by_out.at[k], by_in.at[k], along_y(k)))
    b_sum = b_sum[:, 0].reshape(NX * NZ, BOX)
    pairs[2].wait_recv()
    a_sum = (sums[1] + pair_in[1].astype(F32)).reshape(NX, NY * NZ, BOX)
    a_hops = []
    for k in ring4:
        ax_out[k] = a_sum[k].astype(BF16)
        a_hops.append(hop(2 * NZ + k, ax_out.at[k], ax_in.at[k], along_x(k)))
    a_sum = a_sum[0]

    c_sum = c_rows(0)
    for k, copy in zip(ring8, c_hops):
        copy.wait_recv()
        c_sum = c_sum + cz_in[k].astype(F32)
    c_hops = []
    for k in ring4:
        cx_out[k] = pack(c_sum[k * NY : (k + 1) * NY, :]).astype(BF16)
        c_hops.append(hop(20 + k, cx_out.at[k], cx_in.at[k], along_x(k)))
    for k, copy in zip(ring8, b_hops):
        copy.wait_recv()
        b_sum = b_sum + by_in[k].astype(F32)
    b_hops = []
    for k in ring4:
        bx_out[k] = pack(b_sum[k * NZ : (k + 1) * NZ, :]).astype(BF16)
        b_hops.append(hop(24 + k, bx_out.at[k], bx_in.at[k], along_x(k)))
    for k, copy in zip(ring4, a_hops):
        copy.wait_recv()
        a_sum = a_sum + ax_in[k].astype(F32)
    a_hops = []
    for k in ring8:
        ay_out[k] = pack(a_sum[k * NZ : (k + 1) * NZ, :]).astype(BF16)
        a_hops.append(hop(28 + k, ay_out.at[k], ay_in.at[k], along_y(k)))

    def last(part, total, along):
        copies = []
        for k in ring8:
            last_out[part, k] = total[k : k + 1, :]
            copies.append(
                hop(36 + part * NZ + k, last_out.at[part, k], last_in.at[part, k], along(k))
            )
        return total[0:1, :], copies

    c_sum = c_sum[:NY, :]
    for k, copy in zip(ring4, c_hops):
        copy.wait_recv()
        c_sum = c_sum + unpack(cx_in[k].astype(F32))
    c_sum, c_hops = last(2, c_sum, along_y)
    b_sum = b_sum[:NZ, :]
    for k, copy in zip(ring4, b_hops):
        copy.wait_recv()
        b_sum = b_sum + unpack(bx_in[k].astype(F32))
    b_sum, b_hops = last(0, b_sum, along_z)
    a_sum = a_sum[:NZ, :]
    for k, copy in zip(ring8, a_hops):
        copy.wait_recv()
        a_sum = a_sum + unpack(ay_in[k].astype(F32))
    a_sum, a_hops = last(1, a_sum, along_z)
    for part, total, copies in ((2, c_sum, c_hops), (0, b_sum, b_hops), (1, a_sum, a_hops)):
        for k, copy in zip(ring8, copies):
            copy.wait_recv()
            total = total + last_in[part, k]
        out_ref[:, part * BOX : (part + 1) * BOX] = total * scale
    for copy in gather_z + gather_y + swaps + pairs + hops:
        copy.wait_send()


def expect(scale, *operands):
    smem = pl.BlockSpec(memory_space=pltpu.SMEM)
    vmem = pl.BlockSpec(memory_space=pltpu.VMEM)
    dma = pltpu.SemaphoreType.DMA
    hop_count = 36 + 3 * NZ

    def both_ways(shape, kind):
        return [pltpu.VMEM(shape, kind), pltpu.VMEM(shape, kind)]

    return pl.pallas_call(
        functools.partial(expect_kernel, scale),
        out_shape=(
            jax.ShapeDtypeStruct((1, 3 * BOX), F32),
            jax.ShapeDtypeStruct((1,), F32),
        ),
        in_specs=[smem] * 6 + [vmem] * 4,
        out_specs=(vmem, smem),
        scratch_shapes=[
            pltpu.VMEM((2, Y_LO, NZ, 16, BOX), BF16),
            pltpu.VMEM((2, ROWS), I32),
            pltpu.VMEM((4, ROWS), F32),
            pltpu.VMEM((2 * BOX, 2 * LINES), BF16),
            pltpu.VMEM((2 * LINES, ROWS), BF16),
            pltpu.VMEM((2 * BOX, ROWS), BF16),
            pltpu.VMEM((ROWS, 2 * BOX), BF16),
            pltpu.VMEM((2 * SHIFTS * SHIFTS, ROWS), BF16),
            pltpu.VMEM((BOX, BOX), F32),
            pltpu.VMEM((ROWS, WIDE), BF16),
            pltpu.VMEM((ROWS, WIDE), BF16),
            pltpu.VMEM((POSES, ROWS), BF16),
            pltpu.VMEM((ROWS, 3 * BOX), BF16),
            pltpu.VMEM((3, KEEP, BOX), F32),
            pltpu.VMEM((2, KEEP, BOX // 2), F32),
        ]
        + both_ways((3, KEEP, BOX), BF16)
        + both_ways((NX, NY * NZ, BOX), BF16)
        + both_ways((NY, NX * NZ, BOX), BF16)
        + both_ways((NZ, NX * NY, BOX), BF16)
        + both_ways((NY, 2 * NZ, BOX // 2), BF16)
        + both_ways((NX, 2 * NZ, BOX // 2), BF16)
        + both_ways((NX, 2 * NY, BOX // 2), BF16)
        + both_ways((3, NZ, 1, BOX), F32)
        + [
            dma((NZ + Y_LO,)),
            dma((NZ + Y_LO,)),
            dma((Y_LO,)),
            dma((Y_LO,)),
            dma((3,)),
            dma((3,)),
            dma((hop_count,)),
            dma((hop_count,)),
        ],
        compiler_params=pltpu.CompilerParams(
            collective_id=0, has_side_effects=True, vmem_limit_bytes=48 * 1024 * 1024
        ),
    )(*operands)


def body(
    particles,
    defocus_class,
    noise_precision,
    live_count,
    defocus,
    reference_lines,
    line_index,
    line_weight,
    row_shifts,
    column_shifts,
):
    index = jnp.transpose(line_index, (0, 2, 1))
    weight = jnp.transpose(line_weight, (0, 2, 1))
    particle_total = particles.shape[0] * lax.axis_size("slab") * lax.axis_size("grp")
    owned, loglik = expect(
        LINES / (POSES * particle_total),
        defocus_class,
        noise_precision,
        live_count,
        defocus,
        row_shifts,
        column_shifts,
        particles,
        index,
        weight,
        reference_lines,
    )
    return owned.reshape(1, 3, BOX), loglik


def solution(mesh):
    return jax.shard_map(
        body,
        mesh=mesh,
        in_specs=(
            P(("slab", "grp"), None, None, None),
            P(("slab", "grp")),
            P(("slab", "grp")),
            P("grp"),
            P(),
            P("slab", None, None),
            P(),
            P(),
            P(),
            P(),
        ),
        out_specs=(P(("slab", "grp"), None, None), P(("slab", "grp"))),
        check_vma=False,
    )
```

```python
import functools
import math

import jax
import jax.numpy as jnp
from jax import lax
from jax.experimental import pallas as pl
from jax.experimental.pallas import tpu as pltpu
from jax.sharding import PartitionSpec as P

MESH = pl.DeviceIdType.MESH
EXACT = lax.Precision.HIGHEST
F32 = jnp.float32
BF16 = jnp.bfloat16
I32 = jnp.int32

NX, NY, NZ, Y_LO = 4, 8, 8, 4
SLABS = NZ * Y_LO
LINES = 512
KEEP = LINES // 2
BOX = 256
POSES = 16
GROUP = 16
WIDE = GROUP * POSES
ROWS = POSES * BOX
SHIFTS = 8


def place():
    slab = lax.axis_index("slab")
    grp = lax.axis_index("grp")
    z, y_lo = slab // Y_LO, slab % Y_LO
    y_hi, x, core = grp // (2 * NX), (grp // 2) % NX, grp % 2
    return z, y_hi * Y_LO + y_lo, x, core


def device_at(z, y, x, core):
    return (z * Y_LO + y % Y_LO, (y // Y_LO) * (2 * NX) + x * 2 + core)


def phase_angle(turns):
    signed = ((turns + BOX // 2) & (BOX - 1)) - BOX // 2
    return signed.astype(F32) * (2.0 * math.pi / BOX)


def shift_column(shifts_ref, shape):
    row = lax.broadcasted_iota(I32, shape, 0)
    column = jnp.zeros(shape, I32)
    for t in range(SHIFTS):
        column = jnp.where(row == t, shifts_ref[t], column)
    return column


def slot_of(line, z, y, x, core):
    line_y = ((line >> 3) & 1) * Y_LO + ((line >> 4) & (Y_LO - 1))
    return (
        ((line ^ core) & 1) * KEEP
        + ((((line >> 1) - x) & (NX - 1)) * (NY * NZ))
        + (((line_y - y) & (NY - 1)) * NZ)
        + (((line >> 6) - z) & (NZ - 1))
    )


def held_row(slot, z, y, x, core):
    line_z = (slot + z) & (NZ - 1)
    line_y = ((slot >> 3) + y) & (NY - 1)
    line_x = ((slot >> 6) + x) & (NX - 1)
    line_core = ((slot >> 8) ^ core) & 1
    return (line_y & 3) * (NZ * 16) + line_z * 16 + (line_y >> 2) * 8 + line_x * 2 + line_core


def expect_kernel(
    scale,
    class_hbm,
    precision_hbm,
    live_hbm,
    defocus_hbm,
    row_shift_hbm,
    column_shift_hbm,
    image_hbm,
    index_hbm,
    weight_hbm,
    lines_hbm,
    out_ref,
    loglik_ref,
    class_ref,
    precision_ref,
    live_ref,
    defocus_ref,
    row_shift_ref,
    column_shift_ref,
    image_ref,
    index_ref,
    weight_ref,
    lines_ref,
    load_sem,
    held,
    slots,
    weights,
    lines_t,
    spread,
    slices,
    shifted,
    phases,
    squares,
    product_high,
    product_low,
    turned,
    rows,
    sums,
    strided,
    pair_out,
    pair_in,
    ax_out,
    ax_in,
    by_out,
    by_in,
    cz_out,
    cz_in,
    a_last_out,
    a_last_in,
    b_last_out,
    b_last_in,
    c_last_out,
    c_last_in,
    gather_send,
    gather_recv,
    pair_send,
    pair_recv,
    hop_send,
    hop_recv,
    ready,
):
    loads = [
        pltpu.make_async_copy(src, dst, load_sem.at[n])
        for n, (src, dst) in enumerate(
            [
                (lines_hbm, lines_ref),
                (class_hbm, class_ref),
                (live_hbm, live_ref),
                (defocus_hbm, defocus_ref),
                (column_shift_hbm, column_shift_ref),
                (row_shift_hbm, row_shift_ref),
                (image_hbm, image_ref),
                (index_hbm, index_ref),
                (weight_hbm, weight_ref),
                (precision_hbm, precision_ref),
            ]
        )
    ]
    for load in loads:
        load.start()
    z, y, x, core = place()
    y_lo = y % Y_LO
    sibling = device_at(z, y, x, 1 - core)

    def along_x(k):
        return device_at(z, y, (x + k) % NX, core)

    def along_y(k):
        return device_at(z, (y + NY + k) % NY, x, core)

    def along_z(k):
        return device_at((z + k) % NZ, y, x, core)

    def remote(src, dst, send, recv, device):
        return pltpu.make_async_remote_copy(
            src_ref=src,
            dst_ref=dst,
            send_sem=send,
            recv_sem=recv,
            device_id=device,
            device_id_type=MESH,
        )

    barrier = pltpu.get_barrier_semaphore()
    peers = [sibling]
    peers += [along_x(k) for k in range(1, NX)]
    peers += [along_y(k) for k in range(1, NY)]
    peers += [along_z(k) for k in range(1, NZ)]
    for peer in peers:
        pl.semaphore_signal(barrier, inc=1, device_id=peer, device_id_type=MESH)

    loads[0].wait()
    both = lines_ref[...]
    held[core, y_lo, z] = jnp.where(core == 0, both[:, 0, :], both[:, 1, :])

    pl.semaphore_wait(barrier, len(peers))
    for k in range(1, NX):
        pl.semaphore_signal(ready, inc=1, device_id=along_x(k), device_id_type=MESH)
    sent = []

    def send_block(src, number, device):
        copy = remote(src, src, gather_send.at[number], gather_recv.at[number], device)
        copy.start()
        sent.append(copy)
        return copy

    near_z = {
        k: send_block(held.at[core, y_lo, z], k, along_z(k)) for k in (4, 3, 5, 2, 6, 1, 7)
    }
    far = 2 - 4 * core
    steps = {1: 1, 2: far, 3: -1}
    near_y = {}
    swaps = []

    def pass_along_y(k):
        block = held.at[core, y_lo, (z + NZ - k) % NZ]
        for d in (2, 1, 3):
            near_y[d, k] = send_block(block, 8 * d + k, along_y(steps[d]))
        swaps.append(send_block(block, 32 + k, sibling))

    def pass_on(*distances):
        for k in distances:
            near_z[k].wait_recv()
            pass_along_y(k)

    def swap(*distances):
        for k in distances:
            for d, residue in ((1, y_lo + 3), (3, y_lo + 1), (2, y_lo + 2)):
                near_y[d, k].wait_recv()
                block = held.at[core, residue % Y_LO, (z + NZ - k) % NZ]
                swaps.append(send_block(block, 32 + 8 * d + k, sibling))

    pass_along_y(0)
    for load in loads[1:]:
        load.wait()

    alive = jnp.where(0 < live_ref[0], 1.0, 0.0).astype(F32)
    chosen = defocus_ref[class_ref[0]]

    lane_y = lax.broadcasted_iota(I32, (SHIFTS, BOX), 1) - BOX // 2
    angle_y = phase_angle(lane_y * shift_column(column_shift_ref, (SHIFTS, BOX)))
    cos_y = jnp.cos(angle_y)
    sin_y = jnp.sin(angle_y)
    freq_y = (lax.broadcasted_iota(I32, (GROUP, BOX), 1) - BOX // 2).astype(F32) / BOX
    row_in_group = lax.broadcasted_iota(I32, (GROUP, BOX), 0)

    def shift_rows(g, carry):
        at = pl.ds(pl.multiple_of(g * WIDE, WIDE), WIDE)
        kx = pl.ds(pl.multiple_of(g * GROUP, GROUP), GROUP)
        freq_x = (row_in_group + (g * GROUP - BOX // 2)).astype(F32) / BOX
        ctf = -jnp.sin(chosen * (freq_x * freq_x + freq_y * freq_y) + 0.1) * alive
        squares[kx, :] = ctf * ctf
        real = ctf * image_ref[0, 0, kx, :].astype(F32)
        imag = ctf * image_ref[0, 1, kx, :].astype(F32)
        blocks = []
        for k in range(GROUP):
            real_row = real[k : k + 1, :]
            imag_row = imag[k : k + 1, :]
            shift_re = real_row * cos_y + imag_row * sin_y
            shift_im = real_row * sin_y - imag_row * cos_y
            blocks.append(jnp.concatenate([shift_re, -shift_im], axis=1))
            blocks.append(jnp.concatenate([shift_im, shift_re], axis=1))
        shifted[at, :] = jnp.concatenate(blocks, axis=0).astype(BF16)
        return carry

    lax.fori_loop(0, BOX // GROUP, shift_rows, 0)

    lane = lax.broadcasted_iota(I32, (SHIFTS, ROWS), 1)
    freq = (lane >> 4) - BOX // 2
    part = (lane >> 3) & 1
    turns = freq * shift_column(row_shift_ref, (SHIFTS, ROWS)) + part * (BOX // 4)
    row_phase = jnp.cos(phase_angle(turns))
    row_high = row_phase.astype(BF16).astype(F32)
    row_low = row_phase - row_high
    for t in range(0, SHIFTS, 2):
        for base, table in ((0, row_high), (SHIFTS * SHIFTS, row_low)):
            phases[pl.ds(base + t * SHIFTS, 2 * SHIFTS), :] = jnp.concatenate(
                [jnp.where((lane & 7) == t + u, table, 0.0) for u in range(2)], axis=0
            ).astype(BF16)

    pass_on(1, 7)
    first = slot_of(index_ref[:, 0, :], z, y, x, core)
    second = slot_of(index_ref[:, 1, :], z, y, x, core)
    first_weight = weight_ref[:, 0, :]
    second_weight = weight_ref[:, 1, :]
    same = first == second
    first_weight = jnp.where(same, first_weight + second_weight, first_weight)
    second_weight = jnp.where(same, 0.0, second_weight)
    first_high = first_weight.astype(BF16).astype(F32)
    second_high = second_weight.astype(BF16).astype(F32)
    tables = jnp.concatenate(
        [
            (first >> 4).astype(F32),
            (first & 15).astype(F32),
            (second >> 4).astype(F32),
            (second & 15).astype(F32),
            first_high,
            second_high,
            first_weight - first_high,
            second_weight - second_high,
        ],
        axis=0,
    ).astype(BF16)
    table_lane = lax.broadcasted_iota(I32, (BOX, WIDE), 1) >> 4
    table_row = lax.broadcasted_iota(I32, (BOX, WIDE), 0)
    pose_row = lax.broadcasted_iota(I32, (POSES, WIDE), 0) == (
        lax.broadcasted_iota(I32, (POSES, WIDE), 1) & (POSES - 1)
    )

    def table_rows(g, carry):
        at = pl.ds(pl.multiple_of(g * WIDE, WIDE), WIDE)
        chosen_row = jnp.where(table_row == table_lane + g * GROUP, 1.0, 0.0).astype(BF16)
        wide = jnp.dot(tables, chosen_row, preferred_element_type=F32)
        found = [
            jnp.sum(
                jnp.where(pose_row, wide[n * POSES : (n + 1) * POSES, :], 0.0),
                axis=0,
                keepdims=True,
            )
            for n in range(8)
        ]
        slots[0:1, at] = (found[0] * 16.0 + found[1]).astype(I32)
        slots[1:2, at] = (found[2] * 16.0 + found[3]).astype(I32)
        for n in range(4):
            weights[n : n + 1, at] = found[4 + n]
        return carry

    lax.fori_loop(0, 8, table_rows, 0, unroll=2)
    pass_on(2, 6)
    lax.fori_loop(8, BOX // GROUP, table_rows, 0, unroll=2)
    pass_on(3, 5, 4)
    slot_row = lax.broadcasted_iota(I32, (LINES, WIDE), 0)

    def spread_rows(g, carry):
        at = pl.ds(pl.multiple_of(g * WIDE, WIDE), WIDE)
        is_first = slot_row == slots[0:1, at]
        is_second = slot_row == slots[1:2, at]
        high = jnp.where(is_first, weights[0:1, at], jnp.where(is_second, weights[1:2, at], 0.0))
        low = jnp.where(is_first, weights[2:3, at], jnp.where(is_second, weights[3:4, at], 0.0))
        spread[:LINES, at] = high.astype(BF16)
        spread[LINES:, at] = low.astype(BF16)
        return carry

    lax.fori_loop(0, 5, spread_rows, 0)
    swap(0, 1, 7)
    lax.fori_loop(5, 10, spread_rows, 0)
    swap(2, 6)
    lax.fori_loop(10, BOX // GROUP, spread_rows, 0)
    swap(3, 5, 4)

    slot_rows = held_row(lax.broadcasted_iota(I32, (1, LINES), 1), z, y, x, core)
    order = jnp.where(
        lax.broadcasted_iota(I32, (LINES, LINES), 0) == slot_rows, 1.0, 0.0
    ).astype(BF16)

    def transpose_half(c):
        half = lax.dot_general(
            held[c].reshape(LINES, BOX),
            order,
            (((0,), (0,)), ((), ())),
            preferred_element_type=F32,
        ).astype(BF16)
        lines_t[pl.ds(pl.multiple_of(c * BOX, BOX), BOX), :] = jnp.concatenate(
            [half, half], axis=1
        )

    def slice_half(c):
        half = pl.ds(pl.multiple_of(c * BOX, BOX), BOX)

        def step(n, carry):
            at = pl.ds(pl.multiple_of(n * 4 * WIDE, 4 * WIDE), 4 * WIDE)
            slices[half, at] = jnp.dot(
                lines_t[half, :], spread[:, at], preferred_element_type=F32
            ).astype(BF16)
            return carry

        lax.fori_loop(0, ROWS // (4 * WIDE), step, 0, unroll=True)

    transpose_half(core)
    slice_half(core)
    for copy in swaps:
        copy.wait_recv()
    transpose_half(1 - core)
    slice_half(1 - core)

    lane_row = lax.broadcasted_iota(I32, (GROUP, 128), 1) >> 4
    nothing = jnp.zeros((GROUP, 128), BF16)

    def diagonal(k, tile):
        return jnp.concatenate([tile, nothing] if k < GROUP // 2 else [nothing, tile], axis=1)

    def correlate(g, carry):
        at = pl.ds(pl.multiple_of(g * WIDE, WIDE), WIDE)
        products = jnp.dot(shifted[at, :], slices[:, at], preferred_element_type=F32)
        highs, lows = [], []
        for k in range(GROUP):
            lane_at = k // (GROUP // 2) * 128
            block = products[k * GROUP : (k + 1) * GROUP, lane_at : lane_at + 128]
            block = jnp.where(lane_row == k % (GROUP // 2), block, 0.0)
            high = block.astype(BF16)
            highs.append(diagonal(k, high))
            lows.append(diagonal(k, (block - high.astype(F32)).astype(BF16)))
        product_high[at, :] = jnp.concatenate(highs, axis=0)
        product_low[at, :] = jnp.concatenate(lows, axis=0)
        return carry

    lax.fori_loop(0, BOX // GROUP, correlate, 0, unroll=4)
    corr = jnp.dot(phases[...], product_high[...], preferred_element_type=F32)
    corr = corr[: SHIFTS * SHIFTS] + corr[SHIFTS * SHIFTS :]
    corr = corr + jnp.dot(
        phases[: SHIFTS * SHIFTS, :], product_low[...], preferred_element_type=F32
    )
    corr = corr[:, : WIDE // 2] + corr[:, WIDE // 2 :]
    for step in (64, 32, 16):
        corr = corr + pltpu.roll(corr, step, 1)
    score = corr * (precision_ref[0] / BOX)
    top = jnp.max(score, axis=(0, 1), keepdims=True)
    terms = jnp.exp(score - top)
    total = jnp.sum(terms, axis=(0, 1), keepdims=True) * (1.0 / 8.0)
    posterior = terms / total
    loglik_ref[0] = ((top + jnp.log(total)) * alive)[0, 0]
    posterior_t = posterior.T[:POSES]
    mass = jnp.sum(posterior_t, axis=1, keepdims=True)

    pairs = []

    def spread_part(c):
        columns = rows[:, c * BOX : (c + 1) * BOX]
        pair_out[c] = jnp.dot(spread[KEEP:LINES, :], columns, preferred_element_type=F32).astype(BF16)
        copy = remote(pair_out.at[c], pair_in.at[c], pair_send.at[c], pair_recv.at[c], sibling)
        copy.start()
        pairs.append(copy)
        sums[c] = jnp.dot(spread[:KEEP, :], columns, preferred_element_type=F32)

    def square_rows(g, carry):
        at = pl.ds(pl.multiple_of(g * WIDE, WIDE), WIDE)
        square = squares[pl.ds(pl.multiple_of(g * GROUP, GROUP), GROUP), :]
        rows[at, 2 * BOX :] = jnp.concatenate(
            [square[k : k + 1, :] * mass for k in range(GROUP)], axis=0
        ).astype(BF16)
        return carry

    def turn_poses():
        high = posterior_t.astype(BF16)
        low = (posterior_t - high.astype(F32)).astype(BF16)
        parts = jnp.concatenate(
            [
                jnp.concatenate([high, high], axis=1),
                jnp.concatenate([low, jnp.zeros_like(low)], axis=1),
            ],
            axis=0,
        )
        both_parts = jnp.dot(parts, phases[...], preferred_element_type=F32)
        turned[...] = (both_parts[:POSES] + both_parts[POSES:]).astype(BF16)

    def insert(g, carry):
        at = pl.ds(pl.multiple_of(g * WIDE, WIDE), WIDE)
        turns_g = turned[:, at]
        weight = jnp.concatenate(
            [
                diagonal(
                    k,
                    jnp.where(
                        lane_row == k % (GROUP // 2),
                        turns_g[:, k // (GROUP // 2) * 128 : k // (GROUP // 2) * 128 + 128],
                        nothing,
                    ),
                )
                for k in range(GROUP)
            ],
            axis=0,
        )
        rows[at, : 2 * BOX] = jnp.dot(
            weight, shifted[at, :], preferred_element_type=F32
        ).astype(BF16)
        return carry

    hops = []

    def hop(number, src, dst, device):
        copy = remote(src, dst, hop_send.at[number], hop_recv.at[number], device)
        copy.start()
        hops.append(copy)
        return copy

    ring8 = (4, 3, 5, 2, 6, 1, 7)
    ring4 = (2, 1, 3)

    lax.fori_loop(0, BOX // GROUP, square_rows, 0, unroll=2)
    spread_part(2)
    turn_poses()
    lax.fori_loop(0, BOX // GROUP, insert, 0, unroll=4)
    pairs[0].wait_recv()
    c_sum = sums[2] + pair_in[2].astype(F32)
    for half in range(2):
        strided[half] = c_sum[:, half * 128 : (half + 1) * 128]

    def c_rows(k):
        rows_k = pl.ds(k, NX * NY, NZ)
        return jnp.concatenate([strided[0, rows_k, :], strided[1, rows_k, :]], axis=1)

    c_hops = []
    for k in ring8:
        cz_out[k] = c_rows(k).astype(BF16)
        c_hops.append(hop(k, cz_out.at[k], cz_in.at[k], along_z(k)))
    spread_part(0)
    spread_part(1)

    pairs[1].wait_recv()
    b_sum = (sums[0] + pair_in[0].astype(F32)).reshape(NX, NY, NZ, BOX)
    b_hops = []
    for k in ring8:
        by_out[k] = b_sum[:, k].reshape(NX * NZ, BOX).astype(BF16)
        b_hops.append(hop(NZ + k, by_out.at[k], by_in.at[k], along_y(k)))
    b_sum = b_sum[:, 0].reshape(NX * NZ, BOX)
    pairs[2].wait_recv()
    a_sum = (sums[1] + pair_in[1].astype(F32)).reshape(NX, NY * NZ, BOX)
    a_hops = []
    for k in ring4:
        ax_out[k] = a_sum[k].astype(BF16)
        a_hops.append(hop(2 * NZ + k, ax_out.at[k], ax_in.at[k], along_x(k)))
    a_sum = a_sum[0]

    pl.semaphore_wait(ready, NX - 1)

    def last(rows_out, rows_in, total, number, owner):
        count = total.shape[0]
        rows_out[...] = total.reshape(count, 1, BOX)
        copies = []
        for n in range(count - 1, 0, -1):
            copies.append(
                hop(number + n, rows_out.at[n], rows_in.at[n], owner(n))
            )
        return copies

    def collect(rows_in, total, copies):
        for copy in copies:
            copy.wait_recv()
        return total[0:1, :] + jnp.sum(rows_in[1:], axis=0)

    c_sum = c_rows(0)
    for k, copy in zip(ring8, c_hops):
        copy.wait_recv()
        c_sum = c_sum + cz_in[k].astype(F32)
    c_hops = last(
        c_last_out,
        c_last_in,
        c_sum,
        20,
        lambda n: device_at(z, (y + n % NY) % NY, (x + n // NY) % NX, core),
    )
    for k, copy in zip(ring4, a_hops):
        copy.wait_recv()
        a_sum = a_sum + ax_in[k].astype(F32)
    a_hops = last(
        a_last_out,
        a_last_in,
        a_sum,
        52,
        lambda n: device_at((z + n % NZ) % NZ, (y + n // NZ) % NY, x, core),
    )
    for k, copy in zip(ring8, b_hops):
        copy.wait_recv()
        b_sum = b_sum + by_in[k].astype(F32)
    b_hops = last(
        b_last_out,
        b_last_in,
        b_sum,
        116,
        lambda n: device_at((z + n % NZ) % NZ, y, (x + n // NZ) % NX, core),
    )
    out_ref[:, 2 * BOX :] = collect(c_last_in, c_sum, c_hops) * scale
    out_ref[:, BOX : 2 * BOX] = collect(a_last_in, a_sum, a_hops) * scale
    out_ref[:, :BOX] = collect(b_last_in, b_sum, b_hops) * scale
    for copy in sent + pairs + hops:
        copy.wait_send()


def expect(scale, *operands):
    smem = pl.BlockSpec(memory_space=pltpu.SMEM)
    vmem = pl.BlockSpec(memory_space=pltpu.VMEM)
    dma = pltpu.SemaphoreType.DMA
    hop_count = 116 + NX * NZ

    def both_ways(shape, kind):
        return [pltpu.VMEM(shape, kind), pltpu.VMEM(shape, kind)]

    return pl.pallas_call(
        functools.partial(expect_kernel, scale),
        out_shape=(
            jax.ShapeDtypeStruct((1, 3 * BOX), F32),
            jax.ShapeDtypeStruct((1,), F32),
        ),
        in_specs=[pl.BlockSpec(memory_space=pltpu.HBM)] * 10,
        out_specs=(vmem, smem),
        scratch_shapes=[
            pltpu.SMEM(operand.shape, operand.dtype) for operand in operands[:6]
        ]
        + [pltpu.VMEM(operand.shape, operand.dtype) for operand in operands[6:]]
        + [dma((10,))]
        + [
            pltpu.VMEM((2, Y_LO, NZ, 16, BOX), BF16),
            pltpu.VMEM((2, ROWS), I32),
            pltpu.VMEM((4, ROWS), F32),
            pltpu.VMEM((2 * BOX, 2 * LINES), BF16),
            pltpu.VMEM((2 * LINES, ROWS), BF16),
            pltpu.VMEM((2 * BOX, ROWS), BF16),
            pltpu.VMEM((ROWS, 2 * BOX), BF16),
            pltpu.VMEM((2 * SHIFTS * SHIFTS, ROWS), BF16),
            pltpu.VMEM((BOX, BOX), F32),
            pltpu.VMEM((ROWS, WIDE), BF16),
            pltpu.VMEM((ROWS, WIDE), BF16),
            pltpu.VMEM((POSES, ROWS), BF16),
            pltpu.VMEM((ROWS, 3 * BOX), BF16),
            pltpu.VMEM((3, KEEP, BOX), F32),
            pltpu.VMEM((2, KEEP, BOX // 2), F32),
        ]
        + both_ways((3, KEEP, BOX), BF16)
        + both_ways((NX, NY * NZ, BOX), BF16)
        + both_ways((NY, NX * NZ, BOX), BF16)
        + both_ways((NZ, NX * NY, BOX), BF16)
        + both_ways((NY * NZ, 1, BOX), F32)
        + both_ways((NX * NZ, 1, BOX), F32)
        + both_ways((NX * NY, 1, BOX), F32)
        + [
            dma((2 * SLABS,)),
            dma((2 * SLABS,)),
            dma((3,)),
            dma((3,)),
            dma((hop_count,)),
            dma((hop_count,)),
            pltpu.SemaphoreType.REGULAR,
        ],
        compiler_params=pltpu.CompilerParams(
            collective_id=0, has_side_effects=True, vmem_limit_bytes=48 * 1024 * 1024
        ),
    )(*operands)


def body(
    particles,
    defocus_class,
    noise_precision,
    live_count,
    defocus,
    reference_lines,
    line_index,
    line_weight,
    row_shifts,
    column_shifts,
):
    index = jnp.transpose(line_index, (0, 2, 1))
    weight = jnp.transpose(line_weight, (0, 2, 1))
    particle_total = particles.shape[0] * lax.axis_size("slab") * lax.axis_size("grp")
    owned, loglik = expect(
        LINES / (POSES * particle_total),
        defocus_class,
        noise_precision,
        live_count,
        defocus,
        row_shifts,
        column_shifts,
        particles,
        index,
        weight,
        reference_lines,
    )
    return owned.reshape(1, 3, BOX), loglik


def solution(mesh):
    return jax.shard_map(
        body,
        mesh=mesh,
        in_specs=(
            P(("slab", "grp"), None, None, None),
            P(("slab", "grp")),
            P(("slab", "grp")),
            P("grp"),
            P(),
            P("slab", None, None),
            P(),
            P(),
            P(),
            P(),
        ),
        out_specs=(P(("slab", "grp"), None, None), P(("slab", "grp"))),
        check_vma=False,
    )
```

```python
import math

import jax
import jax.numpy as jnp
from jax import lax
from jax.experimental import pallas as pl
from jax.experimental.pallas import tpu as pltpu
from jax.sharding import PartitionSpec as P

MESH = pl.DeviceIdType.MESH
EXACT = lax.Precision.HIGHEST
F32 = jnp.float32
BF16 = jnp.bfloat16
I32 = jnp.int32

NX, NY, NZ, Y_LO = 4, 8, 8, 4
SLABS = NZ * Y_LO
LINES = 512
KEEP = LINES // 2
BOX = 256
POSES = 16
GROUP = 16
WIDE = GROUP * POSES
ROWS = POSES * BOX
SHIFTS = 8


def place():
    slab = lax.axis_index("slab")
    grp = lax.axis_index("grp")
    z, y_lo = slab // Y_LO, slab % Y_LO
    y_hi, x, core = grp // (2 * NX), (grp // 2) % NX, grp % 2
    return z, y_hi * Y_LO + y_lo, x, core


def device_at(z, y, x, core):
    return (z * Y_LO + y % Y_LO, (y // Y_LO) * (2 * NX) + x * 2 + core)


def phase_angle(turns):
    signed = ((turns + BOX // 2) & (BOX - 1)) - BOX // 2
    return signed.astype(F32) * (2.0 * math.pi / BOX)


def shift_column(shifts_ref, shape):
    row = lax.broadcasted_iota(I32, shape, 0)
    column = jnp.zeros(shape, I32)
    for t in range(SHIFTS):
        column = jnp.where(row == t, shifts_ref[t], column)
    return column


def slot_of(line, z, y, x, core):
    line_y = ((line >> 3) & 1) * Y_LO + ((line >> 4) & (Y_LO - 1))
    return (
        ((line ^ core) & 1) * KEEP
        + ((((line >> 1) - x) & (NX - 1)) * (NY * NZ))
        + (((line_y - y) & (NY - 1)) * NZ)
        + (((line >> 6) - z) & (NZ - 1))
    )


def held_row(slot, z, y, x, core):
    line_z = (slot + z) & (NZ - 1)
    line_y = ((slot >> 3) + y) & (NY - 1)
    line_x = ((slot >> 6) + x) & (NX - 1)
    line_core = ((slot >> 8) ^ core) & 1
    return (line_y & 3) * (NZ * 16) + line_z * 16 + (line_y >> 2) * 8 + line_x * 2 + line_core


def expect_kernel(
    class_hbm,
    precision_hbm,
    live_hbm,
    defocus_hbm,
    row_shift_hbm,
    column_shift_hbm,
    image_hbm,
    index_hbm,
    weight_hbm,
    lines_hbm,
    out_ref,
    loglik_ref,
    class_ref,
    precision_ref,
    live_ref,
    defocus_ref,
    row_shift_ref,
    column_shift_ref,
    image_ref,
    index_ref,
    weight_ref,
    lines_ref,
    load_sem,
    held,
    slots,
    weights,
    lines_t,
    spread,
    slices,
    shifted,
    phases,
    squares,
    products,
    turned,
    rows,
    sums,
    strided,
    pair_out,
    pair_in,
    ax_out,
    ax_in,
    by_out,
    by_in,
    cz_out,
    cz_in,
    a_last_out,
    a_last_in,
    b_last_out,
    b_last_in,
    c_last_out,
    c_last_in,
    gather_send,
    gather_recv,
    pair_send,
    pair_recv,
    hop_send,
    hop_recv,
    ready,
):
    loads = [
        pltpu.make_async_copy(src, dst, load_sem.at[n])
        for n, (src, dst) in enumerate(
            [
                (lines_hbm, lines_ref),
                (class_hbm, class_ref),
                (live_hbm, live_ref),
                (defocus_hbm, defocus_ref),
                (column_shift_hbm, column_shift_ref),
                (row_shift_hbm, row_shift_ref),
                (image_hbm, image_ref),
                (index_hbm, index_ref),
                (weight_hbm, weight_ref),
                (precision_hbm, precision_ref),
            ]
        )
    ]
    for load in loads:
        load.start()
    z, y, x, core = place()
    y_lo = y % Y_LO
    sibling = device_at(z, y, x, 1 - core)

    def along_x(k):
        return device_at(z, y, (x + k) % NX, core)

    def along_y(k):
        return device_at(z, (y + NY + k) % NY, x, core)

    def along_z(k):
        return device_at((z + k) % NZ, y, x, core)

    def remote(src, dst, send, recv, device):
        return pltpu.make_async_remote_copy(
            src_ref=src,
            dst_ref=dst,
            send_sem=send,
            recv_sem=recv,
            device_id=device,
            device_id_type=MESH,
        )

    barrier = pltpu.get_barrier_semaphore()
    peers = [sibling]
    peers += [along_x(k) for k in range(1, NX)]
    peers += [along_y(k) for k in range(1, NY)]
    peers += [along_z(k) for k in range(1, NZ)]
    for peer in peers:
        pl.semaphore_signal(barrier, inc=1, device_id=peer, device_id_type=MESH)

    loads[0].wait()
    both = lines_ref[...]
    held[core, y_lo, z] = jnp.where(core == 0, both[:, 0, :], both[:, 1, :])

    for load in loads[1:]:
        load.wait()
    alive = jnp.where(0 < live_ref[0], 1.0, 0.0).astype(F32)
    chosen = defocus_ref[class_ref[0]]

    lane_y = lax.broadcasted_iota(I32, (SHIFTS, BOX), 1) - BOX // 2
    angle_y = phase_angle(lane_y * shift_column(column_shift_ref, (SHIFTS, BOX)))
    cos_y = jnp.cos(angle_y)
    sin_y = jnp.sin(angle_y)
    freq_y = (lax.broadcasted_iota(I32, (GROUP, BOX), 1) - BOX // 2).astype(F32) / BOX
    row_in_group = lax.broadcasted_iota(I32, (GROUP, BOX), 0)

    def shift_rows(g, carry):
        at = pl.ds(pl.multiple_of(g * WIDE, WIDE), WIDE)
        kx = pl.ds(pl.multiple_of(g * GROUP, GROUP), GROUP)
        freq_x = (row_in_group + (g * GROUP - BOX // 2)).astype(F32) / BOX
        ctf = -jnp.sin(chosen * (freq_x * freq_x + freq_y * freq_y) + 0.1) * alive
        squares[kx, :] = ctf * ctf
        real = ctf * image_ref[0, 0, kx, :].astype(F32)
        imag = ctf * image_ref[0, 1, kx, :].astype(F32)
        blocks = []
        for k in range(GROUP):
            real_row = real[k : k + 1, :]
            imag_row = imag[k : k + 1, :]
            shift_re = real_row * cos_y + imag_row * sin_y
            shift_im = real_row * sin_y - imag_row * cos_y
            blocks.append(jnp.concatenate([shift_re, -shift_im], axis=1))
            blocks.append(jnp.concatenate([shift_im, shift_re], axis=1))
        shifted[at, :] = jnp.concatenate(blocks, axis=0).astype(BF16)
        return carry

    lax.fori_loop(0, BOX // GROUP, shift_rows, 0)

    pl.semaphore_wait(barrier, len(peers))
    for k in range(1, NX):
        pl.semaphore_signal(ready, inc=1, device_id=along_x(k), device_id_type=MESH)
    sent = []

    def send_block(src, number, device):
        copy = remote(src, src, gather_send.at[number], gather_recv.at[number], device)
        copy.start()
        sent.append(copy)
        return copy

    near_z = {
        k: send_block(held.at[core, y_lo, z], k, along_z(k)) for k in (4, 3, 5, 2, 6, 1, 7)
    }
    far = 2 - 4 * core
    steps = {1: 1, 2: far, 3: -1}
    near_y = {}
    swaps = []

    def pass_along_y(k):
        block = held.at[core, y_lo, (z + NZ - k) % NZ]
        for d in (2, 1, 3):
            near_y[d, k] = send_block(block, 8 * d + k, along_y(steps[d]))
        swaps.append(send_block(block, 32 + k, sibling))

    def pass_on(*distances):
        for k in distances:
            near_z[k].wait_recv()
            pass_along_y(k)

    def swap(*distances):
        for k in distances:
            for d, residue in ((1, y_lo + 3), (3, y_lo + 1), (2, y_lo + 2)):
                near_y[d, k].wait_recv()
                block = held.at[core, residue % Y_LO, (z + NZ - k) % NZ]
                swaps.append(send_block(block, 32 + 8 * d + k, sibling))

    pass_along_y(0)
    lane = lax.broadcasted_iota(I32, (SHIFTS, ROWS), 1)
    freq = (lane >> 4) - BOX // 2
    part = (lane >> 3) & 1
    turns = freq * shift_column(row_shift_ref, (SHIFTS, ROWS)) + part * (BOX // 4)
    row_phase = jnp.cos(phase_angle(turns))
    row_high = row_phase.astype(BF16).astype(F32)
    row_low = row_phase - row_high
    for t in range(0, SHIFTS, 2):
        for base, table in ((0, row_high), (SHIFTS * SHIFTS, row_low)):
            phases[pl.ds(base + t * SHIFTS, 2 * SHIFTS), :] = jnp.concatenate(
                [jnp.where((lane & 7) == t + u, table, 0.0) for u in range(2)], axis=0
            ).astype(BF16)

    pass_on(1, 7)
    first = slot_of(index_ref[:, 0, :], z, y, x, core)
    second = slot_of(index_ref[:, 1, :], z, y, x, core)
    first_weight = weight_ref[:, 0, :]
    second_weight = weight_ref[:, 1, :]
    same = first == second
    first_weight = jnp.where(same, first_weight + second_weight, first_weight)
    second_weight = jnp.where(same, 0.0, second_weight)
    first_high = first_weight.astype(BF16).astype(F32)
    second_high = second_weight.astype(BF16).astype(F32)
    tables = jnp.concatenate(
        [
            (first >> 4).astype(F32),
            (first & 15).astype(F32),
            (second >> 4).astype(F32),
            (second & 15).astype(F32),
            first_high,
            second_high,
            first_weight - first_high,
            second_weight - second_high,
        ],
        axis=0,
    ).astype(BF16)
    table_lane = lax.broadcasted_iota(I32, (BOX, WIDE), 1) >> 4
    table_row = lax.broadcasted_iota(I32, (BOX, WIDE), 0)
    pose_row = lax.broadcasted_iota(I32, (POSES, WIDE), 0) == (
        lax.broadcasted_iota(I32, (POSES, WIDE), 1) & (POSES - 1)
    )

    def table_rows(g, carry):
        at = pl.ds(pl.multiple_of(g * WIDE, WIDE), WIDE)
        chosen_row = jnp.where(table_row == table_lane + g * GROUP, 1.0, 0.0).astype(BF16)
        wide = jnp.dot(tables, chosen_row, preferred_element_type=F32)
        found = [
            jnp.sum(
                jnp.where(pose_row, wide[n * POSES : (n + 1) * POSES, :], 0.0),
                axis=0,
                keepdims=True,
            )
            for n in range(8)
        ]
        slots[0:1, at] = (found[0] * 16.0 + found[1]).astype(I32)
        slots[1:2, at] = (found[2] * 16.0 + found[3]).astype(I32)
        for n in range(4):
            weights[n : n + 1, at] = found[4 + n]
        return carry

    lax.fori_loop(0, 8, table_rows, 0, unroll=2)
    pass_on(2, 6)
    lax.fori_loop(8, BOX // GROUP, table_rows, 0, unroll=2)
    pass_on(3, 5, 4)
    slot_row = lax.broadcasted_iota(I32, (LINES, WIDE), 0)

    def spread_rows(g, carry):
        at = pl.ds(pl.multiple_of(g * WIDE, WIDE), WIDE)
        is_first = slot_row == slots[0:1, at]
        is_second = slot_row == slots[1:2, at]
        high = jnp.where(is_first, weights[0:1, at], jnp.where(is_second, weights[1:2, at], 0.0))
        low = jnp.where(is_first, weights[2:3, at], jnp.where(is_second, weights[3:4, at], 0.0))
        spread[:LINES, at] = high.astype(BF16)
        spread[LINES:, at] = low.astype(BF16)
        return carry

    lax.fori_loop(0, 5, spread_rows, 0)
    swap(0, 1, 7)
    lax.fori_loop(5, 10, spread_rows, 0)
    swap(2, 6)
    lax.fori_loop(10, BOX // GROUP, spread_rows, 0)
    swap(3, 5, 4)

    slot_rows = held_row(lax.broadcasted_iota(I32, (1, LINES), 1), z, y, x, core)
    order = jnp.where(
        lax.broadcasted_iota(I32, (LINES, LINES), 0) == slot_rows, 1.0, 0.0
    ).astype(BF16)

    def transpose_half(c):
        half = lax.dot_general(
            held[c].reshape(LINES, BOX),
            order,
            (((0,), (0,)), ((), ())),
            preferred_element_type=F32,
        ).astype(BF16)
        lines_t[pl.ds(pl.multiple_of(c * BOX, BOX), BOX), :] = jnp.concatenate(
            [half, half], axis=1
        )

    def slice_half(c):
        half = pl.ds(pl.multiple_of(c * BOX, BOX), BOX)

        def step(n, carry):
            at = pl.ds(pl.multiple_of(n * 4 * WIDE, 4 * WIDE), 4 * WIDE)
            slices[half, at] = jnp.dot(
                lines_t[half, :], spread[:, at], preferred_element_type=F32
            ).astype(BF16)
            return carry

        lax.fori_loop(0, ROWS // (4 * WIDE), step, 0, unroll=True)

    transpose_half(core)
    slice_half(core)
    for copy in swaps:
        copy.wait_recv()
    transpose_half(1 - core)
    slice_half(1 - core)

    lane_row = lax.broadcasted_iota(I32, (GROUP, 128), 1) >> 4
    nothing = jnp.zeros((GROUP, 128), BF16)

    def diagonal(k, tile):
        return jnp.concatenate([tile, nothing] if k < GROUP // 2 else [nothing, tile], axis=1)

    lane_pose = lax.broadcasted_iota(I32, (GROUP, 128), 1) < POSES

    def correlate(g, carry):
        at = pl.ds(pl.multiple_of(g * WIDE, WIDE), WIDE)
        found = jnp.dot(shifted[at, :], slices[:, at], preferred_element_type=F32)
        parts = []
        for k in range(GROUP):
            lane_at = k // (GROUP // 2) * 128
            block = found[k * GROUP : (k + 1) * GROUP, lane_at : lane_at + 128]
            if k % (GROUP // 2):
                block = pltpu.roll(block, 128 - k % (GROUP // 2) * POSES, 1)
            block = jnp.where(lane_pose, block, 0.0)
            high = block.astype(BF16)
            low = (block - high.astype(F32)).astype(BF16)
            parts.append(jnp.concatenate([high, low], axis=1))
        products[at, :] = jnp.concatenate(parts, axis=0)
        return carry

    lax.fori_loop(0, BOX // GROUP, correlate, 0, unroll=True)
    corr = jnp.dot(phases[...], products[...], preferred_element_type=F32)
    half = SHIFTS * SHIFTS
    corr = corr[:half, :POSES] + (corr[half:, :POSES] + corr[:half, 128 : 128 + POSES])
    score = corr * (precision_ref[0] / BOX)
    top = jnp.max(score, axis=(0, 1), keepdims=True)
    terms = jnp.exp(score - top)
    total = jnp.sum(terms, axis=(0, 1), keepdims=True)
    posterior = terms / total
    loglik_ref[0] = ((top + jnp.log(total)) * alive)[0, 0]
    posterior_t = posterior.T
    mass = jnp.sum(posterior_t, axis=1, keepdims=True)

    pairs = []

    def spread_half(first_slot, c):
        return jnp.dot(
            spread[first_slot : first_slot + KEEP, :],
            rows[:, c * BOX : (c + 1) * BOX],
            preferred_element_type=F32,
        )

    def spread_other(c):
        pair_out[c] = spread_half(KEEP, c).astype(BF16)
        copy = remote(pair_out.at[c], pair_in.at[c], pair_send.at[c], pair_recv.at[c], sibling)
        copy.start()
        pairs.append(copy)

    def spread_own(c):
        sums[c] = spread_half(0, c)

    def square_rows(g, carry):
        at = pl.ds(pl.multiple_of(g * WIDE, WIDE), WIDE)
        square = squares[pl.ds(pl.multiple_of(g * GROUP, GROUP), GROUP), :]
        rows[at, 2 * BOX :] = jnp.concatenate(
            [square[k : k + 1, :] * mass for k in range(GROUP)], axis=0
        ).astype(BF16)
        return carry

    def turn_poses():
        high = posterior_t.astype(BF16)
        low = (posterior_t - high.astype(F32)).astype(BF16)
        parts = jnp.concatenate(
            [
                jnp.concatenate([high, high], axis=1),
                jnp.concatenate([low, jnp.zeros_like(low)], axis=1),
            ],
            axis=0,
        )
        both_parts = jnp.dot(parts, phases[...], preferred_element_type=F32)
        turned[...] = (both_parts[:POSES] + both_parts[POSES:]).astype(BF16)

    def insert(g, carry):
        at = pl.ds(pl.multiple_of(g * WIDE, WIDE), WIDE)
        turns_g = turned[:, at]
        weight = jnp.concatenate(
            [
                diagonal(
                    k,
                    jnp.where(
                        lane_row == k % (GROUP // 2),
                        turns_g[:, k // (GROUP // 2) * 128 : k // (GROUP // 2) * 128 + 128],
                        nothing,
                    ),
                )
                for k in range(GROUP)
            ],
            axis=0,
        )
        rows[at, : 2 * BOX] = jnp.dot(
            weight, shifted[at, :], preferred_element_type=F32
        ).astype(BF16)
        return carry

    hops = []

    def hop(number, src, dst, device):
        copy = remote(src, dst, hop_send.at[number], hop_recv.at[number], device)
        copy.start()
        hops.append(copy)
        return copy

    ring8 = (4, 3, 5, 2, 6, 1, 7)
    ring4 = (2, 1, 3)

    lax.fori_loop(0, BOX // GROUP, square_rows, 0, unroll=4)
    spread_other(2)
    spread_own(2)
    turn_poses()
    lax.fori_loop(0, BOX // GROUP, insert, 0, unroll=True)
    pairs[0].wait_recv()
    c_sum = sums[2] + pair_in[2].astype(F32)
    for half in range(2):
        strided[half] = c_sum[:, half * 128 : (half + 1) * 128]

    def c_rows(k):
        rows_k = pl.ds(k, NX * NY, NZ)
        return jnp.concatenate([strided[0, rows_k, :], strided[1, rows_k, :]], axis=1)

    c_hops = []
    for k in ring8:
        cz_out[k] = c_rows(k).astype(BF16)
        c_hops.append(hop(k, cz_out.at[k], cz_in.at[k], along_z(k)))
    spread_other(0)
    spread_other(1)
    spread_own(0)
    spread_own(1)

    pairs[1].wait_recv()
    b_sum = (sums[0] + pair_in[0].astype(F32)).reshape(NX, NY, NZ, BOX)
    b_hops = []
    for k in ring8:
        by_out[k] = b_sum[:, k].reshape(NX * NZ, BOX).astype(BF16)
        b_hops.append(hop(NZ + k, by_out.at[k], by_in.at[k], along_y(k)))
    b_sum = b_sum[:, 0].reshape(NX * NZ, BOX)
    pairs[2].wait_recv()
    a_sum = (sums[1] + pair_in[1].astype(F32)).reshape(NX, NY * NZ, BOX)
    a_hops = []
    for k in ring4:
        ax_out[k] = a_sum[k].astype(BF16)
        a_hops.append(hop(2 * NZ + k, ax_out.at[k], ax_in.at[k], along_x(k)))
    a_sum = a_sum[0]

    pl.semaphore_wait(ready, NX - 1)

    def last(rows_out, rows_in, total, number, size, owner):
        count = total.shape[0]
        rows_out[...] = total.reshape(count, 1, BOX)
        copies = []
        def hops_to(n):
            far_step, near_step = divmod(n, 8)
            return min(far_step, size - far_step) + min(near_step, 8 - near_step)

        for n in sorted(range(1, count), key=hops_to, reverse=True):
            copies.append(
                hop(number + n, rows_out.at[n], rows_in.at[n], owner(n))
            )
        return copies

    def collect(rows_in, total, copies):
        for copy in copies:
            copy.wait_recv()
        return total[0:1, :] + jnp.sum(rows_in[1:], axis=0)

    c_sum = c_rows(0)
    for k, copy in zip(ring8, c_hops):
        copy.wait_recv()
        c_sum = c_sum + cz_in[k].astype(F32)
    c_hops = last(
        c_last_out,
        c_last_in,
        c_sum,
        20,
        NX,
        lambda n: device_at(z, (y + n % NY) % NY, (x + n // NY) % NX, core),
    )
    for k, copy in zip(ring4, a_hops):
        copy.wait_recv()
        a_sum = a_sum + ax_in[k].astype(F32)
    a_hops = last(
        a_last_out,
        a_last_in,
        a_sum,
        52,
        NY,
        lambda n: device_at((z + n % NZ) % NZ, (y + n // NZ) % NY, x, core),
    )
    for k, copy in zip(ring8, b_hops):
        copy.wait_recv()
        b_sum = b_sum + by_in[k].astype(F32)
    b_hops = last(
        b_last_out,
        b_last_in,
        b_sum,
        116,
        NX,
        lambda n: device_at((z + n % NZ) % NZ, y, (x + n // NZ) % NX, core),
    )
    out_ref[:, 2 * BOX :] = collect(c_last_in, c_sum, c_hops)
    out_ref[:, BOX : 2 * BOX] = collect(a_last_in, a_sum, a_hops)
    out_ref[:, :BOX] = collect(b_last_in, b_sum, b_hops)
    for copy in sent + pairs + hops:
        copy.wait_send()


def expect(*operands):
    smem = pl.BlockSpec(memory_space=pltpu.SMEM)
    vmem = pl.BlockSpec(memory_space=pltpu.VMEM)
    dma = pltpu.SemaphoreType.DMA
    hop_count = 116 + NX * NZ

    def both_ways(shape, kind):
        return [pltpu.VMEM(shape, kind), pltpu.VMEM(shape, kind)]

    return pl.pallas_call(
        expect_kernel,
        out_shape=(
            jax.ShapeDtypeStruct((1, 3 * BOX), F32),
            jax.ShapeDtypeStruct((1,), F32),
        ),
        in_specs=[pl.BlockSpec(memory_space=pltpu.HBM)] * 10,
        out_specs=(vmem, smem),
        scratch_shapes=[
            pltpu.SMEM(operand.shape, operand.dtype) for operand in operands[:6]
        ]
        + [pltpu.VMEM(operand.shape, operand.dtype) for operand in operands[6:]]
        + [dma((10,))]
        + [
            pltpu.VMEM((2, Y_LO, NZ, 16, BOX), BF16),
            pltpu.VMEM((2, ROWS), I32),
            pltpu.VMEM((4, ROWS), F32),
            pltpu.VMEM((2 * BOX, 2 * LINES), BF16),
            pltpu.VMEM((2 * LINES, ROWS), BF16),
            pltpu.VMEM((2 * BOX, ROWS), BF16),
            pltpu.VMEM((ROWS, 2 * BOX), BF16),
            pltpu.VMEM((2 * SHIFTS * SHIFTS, ROWS), BF16),
            pltpu.VMEM((BOX, BOX), F32),
            pltpu.VMEM((ROWS, WIDE), BF16),
            pltpu.VMEM((POSES, ROWS), BF16),
            pltpu.VMEM((ROWS, 3 * BOX), BF16),
            pltpu.VMEM((3, KEEP, BOX), F32),
            pltpu.VMEM((2, KEEP, BOX // 2), F32),
        ]
        + both_ways((3, KEEP, BOX), BF16)
        + both_ways((NX, NY * NZ, BOX), BF16)
        + both_ways((NY, NX * NZ, BOX), BF16)
        + both_ways((NZ, NX * NY, BOX), BF16)
        + both_ways((NY * NZ, 1, BOX), F32)
        + both_ways((NX * NZ, 1, BOX), F32)
        + both_ways((NX * NY, 1, BOX), F32)
        + [
            dma((2 * SLABS,)),
            dma((2 * SLABS,)),
            dma((3,)),
            dma((3,)),
            dma((hop_count,)),
            dma((hop_count,)),
            pltpu.SemaphoreType.REGULAR,
        ],
        compiler_params=pltpu.CompilerParams(
            collective_id=0, has_side_effects=True, vmem_limit_bytes=60 * 1024 * 1024
        ),
    )(*operands)


def body(
    particles,
    defocus_class,
    noise_precision,
    live_count,
    defocus,
    reference_lines,
    line_index,
    line_weight,
    row_shifts,
    column_shifts,
):
    index = jnp.transpose(line_index, (0, 2, 1))
    weight = jnp.transpose(line_weight, (0, 2, 1))
    particle_total = particles.shape[0] * lax.axis_size("slab") * lax.axis_size("grp")
    owned, loglik = expect(
        defocus_class,
        noise_precision,
        live_count,
        defocus,
        row_shifts,
        column_shifts,
        particles,
        index,
        weight,
        reference_lines,
    )
    return owned.reshape(1, 3, BOX) * (LINES / (POSES * particle_total)), loglik


def solution(mesh):
    return jax.shard_map(
        body,
        mesh=mesh,
        in_specs=(
            P(("slab", "grp"), None, None, None),
            P(("slab", "grp")),
            P(("slab", "grp")),
            P("grp"),
            P(),
            P("slab", None, None),
            P(),
            P(),
            P(),
            P(),
        ),
        out_specs=(P(("slab", "grp"), None, None), P(("slab", "grp"))),
        check_vma=False,
    )
```

```python
import math

import jax
import jax.numpy as jnp
from jax import lax
from jax.experimental import pallas as pl
from jax.experimental.pallas import tpu as pltpu
from jax.sharding import PartitionSpec as P

MESH = pl.DeviceIdType.MESH
EXACT = lax.Precision.HIGHEST
F32 = jnp.float32
BF16 = jnp.bfloat16
I32 = jnp.int32
I16 = jnp.int16

NX, NY, NZ, Y_LO = 4, 8, 8, 4
SLABS = NZ * Y_LO
LINES = 512
KEEP = LINES // 2
BOX = 256
POSES = 16
GROUP = 16
WIDE = GROUP * POSES
ROWS = POSES * BOX
SHIFTS = 8


def place():
    slab = lax.axis_index("slab")
    grp = lax.axis_index("grp")
    z, y_lo = slab // Y_LO, slab % Y_LO
    y_hi, x, core = grp // (2 * NX), (grp // 2) % NX, grp % 2
    return z, y_hi * Y_LO + y_lo, x, core


def device_at(z, y, x, core):
    return (z * Y_LO + y % Y_LO, (y // Y_LO) * (2 * NX) + x * 2 + core)


def phase_angle(turns):
    signed = ((turns + BOX // 2) & (BOX - 1)) - BOX // 2
    return signed.astype(F32) * (2.0 * math.pi / BOX)


def shift_column(shifts_ref, shape):
    row = lax.broadcasted_iota(I32, shape, 0)
    column = jnp.zeros(shape, I32)
    for t in range(SHIFTS):
        column = jnp.where(row == t, shifts_ref[t], column)
    return column


def slot_of(line, z, y, x, core):
    line_y = ((line >> 3) & 1) * Y_LO + ((line >> 4) & (Y_LO - 1))
    return (
        ((line ^ core) & 1) * KEEP
        + ((((line >> 1) - x) & (NX - 1)) * (NY * NZ))
        + (((line_y - y) & (NY - 1)) * NZ)
        + (((line >> 6) - z) & (NZ - 1))
    )


def held_row(slot, z, y, x, core):
    line_z = (slot + z) & (NZ - 1)
    line_y = ((slot >> 3) + y) & (NY - 1)
    line_x = ((slot >> 6) + x) & (NX - 1)
    line_core = ((slot >> 8) ^ core) & 1
    return (line_y & 3) * (NZ * 16) + line_z * 16 + (line_y >> 2) * 8 + line_x * 2 + line_core


def expect_kernel(
    class_hbm,
    precision_hbm,
    live_hbm,
    defocus_hbm,
    row_shift_hbm,
    column_shift_hbm,
    image_hbm,
    index_hbm,
    weight_hbm,
    lines_hbm,
    out_ref,
    loglik_ref,
    class_ref,
    precision_ref,
    live_ref,
    defocus_ref,
    row_shift_ref,
    column_shift_ref,
    image_ref,
    index_ref,
    weight_ref,
    lines_ref,
    load_sem,
    held,
    slots,
    weights,
    lines_t,
    spread,
    slices,
    shifted,
    phases,
    squares,
    products,
    turned,
    rows,
    sums,
    strided,
    pair_out,
    pair_in,
    ax_out,
    ax_in,
    by_out,
    by_in,
    cz_out,
    cz_in,
    a_last_out,
    a_last_in,
    b_last_out,
    b_last_in,
    c_last_out,
    c_last_in,
    gather_send,
    gather_recv,
    pair_send,
    pair_recv,
    hop_send,
    hop_recv,
    last_send,
    last_recv,
    ready,
):
    loads = [
        pltpu.make_async_copy(src, dst, load_sem.at[n])
        for n, (src, dst) in enumerate(
            [
                (lines_hbm, lines_ref),
                (class_hbm, class_ref),
                (live_hbm, live_ref),
                (defocus_hbm, defocus_ref),
                (column_shift_hbm, column_shift_ref),
                (row_shift_hbm, row_shift_ref),
                (image_hbm, image_ref),
                (index_hbm, index_ref),
                (weight_hbm, weight_ref),
                (precision_hbm, precision_ref),
            ]
        )
    ]
    for load in loads:
        load.start()
    z, y, x, core = place()
    y_lo = y % Y_LO
    sibling = device_at(z, y, x, 1 - core)

    def along_x(k):
        return device_at(z, y, (x + k) % NX, core)

    def along_y(k):
        return device_at(z, (y + NY + k) % NY, x, core)

    def along_z(k):
        return device_at((z + k) % NZ, y, x, core)

    def remote(src, dst, send, recv, device):
        return pltpu.make_async_remote_copy(
            src_ref=src,
            dst_ref=dst,
            send_sem=send,
            recv_sem=recv,
            device_id=device,
            device_id_type=MESH,
        )

    barrier = pltpu.get_barrier_semaphore()
    peers = [sibling]
    peers += [along_x(k) for k in range(1, NX)]
    peers += [along_y(k) for k in range(1, NY)]
    peers += [along_z(k) for k in range(1, NZ)]
    for peer in peers:
        pl.semaphore_signal(barrier, inc=1, device_id=peer, device_id_type=MESH)

    loads[0].wait()
    both = lines_ref[...]
    held[core, y_lo, z] = jnp.where(core == 0, both[:, 0, :], both[:, 1, :])

    for load in loads[1:]:
        load.wait()
    alive = jnp.where(0 < live_ref[0], 1.0, 0.0).astype(F32)
    chosen = defocus_ref[class_ref[0]]

    lane_y = lax.broadcasted_iota(I32, (SHIFTS, BOX), 1) - BOX // 2
    angle_y = phase_angle(lane_y * shift_column(column_shift_ref, (SHIFTS, BOX)))
    cos_y = jnp.cos(angle_y)
    sin_y = jnp.sin(angle_y)
    freq_y = (lax.broadcasted_iota(I32, (GROUP, BOX), 1) - BOX // 2).astype(F32) / BOX
    row_in_group = lax.broadcasted_iota(I32, (GROUP, BOX), 0)

    def shift_rows(g, carry):
        at = pl.ds(pl.multiple_of(g * WIDE, WIDE), WIDE)
        kx = pl.ds(pl.multiple_of(g * GROUP, GROUP), GROUP)
        freq_x = (row_in_group + (g * GROUP - BOX // 2)).astype(F32) / BOX
        ctf = -jnp.sin(chosen * (freq_x * freq_x + freq_y * freq_y) + 0.1) * alive
        squares[kx, :] = ctf * ctf
        real = ctf * image_ref[0, 0, kx, :].astype(F32)
        imag = ctf * image_ref[0, 1, kx, :].astype(F32)
        blocks = []
        for k in range(GROUP):
            real_row = real[k : k + 1, :]
            imag_row = imag[k : k + 1, :]
            shift_re = real_row * cos_y + imag_row * sin_y
            shift_im = real_row * sin_y - imag_row * cos_y
            blocks.append(jnp.concatenate([shift_re, -shift_im], axis=1))
            blocks.append(jnp.concatenate([shift_im, shift_re], axis=1))
        shifted[at, :] = jnp.concatenate(blocks, axis=0).astype(BF16)
        return carry

    lax.fori_loop(0, BOX // GROUP, shift_rows, 0)

    pl.semaphore_wait(barrier, len(peers))
    for k in range(1, NX):
        pl.semaphore_signal(ready, inc=1, device_id=along_x(k), device_id_type=MESH)

    def send_block(src, send, recv, device):
        copy = remote(src, src, gather_send.at[send], gather_recv.at[recv], device)
        copy.start()
        return copy

    def landed(blocks, number):
        pltpu.make_async_copy(blocks, blocks, gather_recv.at[number]).wait()

    def left(blocks, number):
        pltpu.make_async_copy(blocks, blocks, gather_send.at[number]).wait()

    groups = ((0, 1, 7), (2, 6), (3, 5, 4))
    near_z = {
        k: send_block(held.at[core, y_lo, z], 0, k, along_z(k)) for k in (4, 3, 5, 2, 6, 1, 7)
    }
    far = 2 - 4 * core
    steps = {1: 1, 2: far, 3: -1}

    def pass_along_y(k):
        block = held.at[core, y_lo, (z + NZ - k) % NZ]
        group = [k in members for members in groups].index(True)
        for d in (2, 1, 3):
            send_block(block, 1, NZ + group, along_y(steps[d]))
        send_block(block, 2, 11, sibling)

    def pass_on(*distances):
        for k in distances:
            near_z[k].wait_recv()
            pass_along_y(k)

    def swap(group):
        landed(held.at[core, pl.ds(0, 3), pl.ds(0, len(groups[group]))], NZ + group)
        for k in groups[group]:
            for residue in (y_lo + 3, y_lo + 1, y_lo + 2):
                send_block(held.at[core, residue % Y_LO, (z + NZ - k) % NZ], 2, 11, sibling)

    pass_along_y(0)
    lane = lax.broadcasted_iota(I32, (SHIFTS, ROWS), 1)
    freq = (lane >> 4) - BOX // 2
    part = (lane >> 3) & 1
    turns = freq * shift_column(row_shift_ref, (SHIFTS, ROWS)) + part * (BOX // 4)
    row_phase = jnp.cos(phase_angle(turns))
    row_high = row_phase.astype(BF16).astype(F32)
    row_low = row_phase - row_high
    for t in range(0, SHIFTS, 2):
        for base, table in ((0, row_high), (SHIFTS * SHIFTS, row_low)):
            phases[pl.ds(base + t * SHIFTS, 2 * SHIFTS), :] = jnp.concatenate(
                [jnp.where((lane & 7) == t + u, table, 0.0) for u in range(2)], axis=0
            ).astype(BF16)

    pass_on(1, 7)
    first = slot_of(index_ref[:, 0, :], z, y, x, core)
    second = slot_of(index_ref[:, 1, :], z, y, x, core)
    first_weight = weight_ref[:, 0, :]
    second_weight = weight_ref[:, 1, :]
    same = first == second
    first_weight = jnp.where(same, first_weight + second_weight, first_weight)
    second_weight = jnp.where(same, 0.0, second_weight)
    first_high = first_weight.astype(BF16).astype(F32)
    second_high = second_weight.astype(BF16).astype(F32)
    tables = jnp.concatenate(
        [
            (first >> 4).astype(F32),
            (first & 15).astype(F32),
            (second >> 4).astype(F32),
            (second & 15).astype(F32),
            first_high,
            second_high,
            first_weight - first_high,
            second_weight - second_high,
        ],
        axis=0,
    ).astype(BF16)
    table_lane = lax.broadcasted_iota(I32, (BOX, WIDE), 1) >> 4
    table_row = lax.broadcasted_iota(I32, (BOX, WIDE), 0)
    pose_row = lax.broadcasted_iota(I32, (POSES, WIDE), 0) == (
        lax.broadcasted_iota(I32, (POSES, WIDE), 1) & (POSES - 1)
    )

    def table_rows(g, carry):
        at = pl.ds(pl.multiple_of(g * WIDE, WIDE), WIDE)
        chosen_row = jnp.where(table_row == table_lane + g * GROUP, 1.0, 0.0).astype(BF16)
        wide = jnp.dot(tables, chosen_row, preferred_element_type=F32)
        found = [
            jnp.sum(
                jnp.where(pose_row, wide[n * POSES : (n + 1) * POSES, :], 0.0),
                axis=0,
                keepdims=True,
            )
            for n in range(8)
        ]
        for n in range(2):
            slot = (found[2 * n] * 16.0 + found[2 * n + 1]).astype(I32)
            slots[n, :, at] = jnp.broadcast_to(slot, (GROUP, WIDE)).astype(I16)
        for n in range(4):
            weights[n, :, at] = jnp.broadcast_to(found[4 + n], (GROUP, WIDE)).astype(BF16)
        return carry

    lax.fori_loop(0, 8, table_rows, 0, unroll=2)
    pass_on(2, 6)
    lax.fori_loop(8, BOX // GROUP, table_rows, 0, unroll=2)
    pass_on(3, 5, 4)
    slot_row = lax.broadcasted_iota(I32, (GROUP, WIDE), 0).astype(I16)

    def spread_rows(g, carry):
        at = pl.ds(pl.multiple_of(g * WIDE, WIDE), WIDE)
        first_slot, second_slot = slots[0, :, at], slots[1, :, at]
        parts = [weights[n, :, at] for n in range(4)]
        for block in range(LINES // GROUP):
            row = slot_row + jnp.int16(block * GROUP)
            is_first = first_slot == row
            is_second = second_slot == row
            for n, base in ((0, 0), (2, LINES)):
                rest = jnp.where(is_second, parts[n + 1], jnp.zeros_like(parts[n]))
                spread[base + block * GROUP : base + (block + 1) * GROUP, at] = jnp.where(
                    is_first, parts[n], rest
                )
        return carry

    lax.fori_loop(0, 5, spread_rows, 0)
    swap(0)
    lax.fori_loop(5, 10, spread_rows, 0)
    swap(1)
    lax.fori_loop(10, BOX // GROUP, spread_rows, 0)
    swap(2)

    slot_rows = held_row(lax.broadcasted_iota(I32, (1, LINES), 1), z, y, x, core)
    order = jnp.where(
        lax.broadcasted_iota(I32, (LINES, LINES), 0) == slot_rows, 1.0, 0.0
    ).astype(BF16)

    def transpose_half(c):
        half = lax.dot_general(
            held[c].reshape(LINES, BOX),
            order,
            (((0,), (0,)), ((), ())),
            preferred_element_type=F32,
        ).astype(BF16)
        lines_t[pl.ds(pl.multiple_of(c * BOX, BOX), BOX), :] = jnp.concatenate(
            [half, half], axis=1
        )

    def slice_half(c):
        half = pl.ds(pl.multiple_of(c * BOX, BOX), BOX)

        def step(n, carry):
            at = pl.ds(pl.multiple_of(n * 4 * WIDE, 4 * WIDE), 4 * WIDE)
            slices[half, at] = jnp.dot(
                lines_t[half, :], spread[:, at], preferred_element_type=F32
            ).astype(BF16)
            return carry

        lax.fori_loop(0, ROWS // (4 * WIDE), step, 0, unroll=True)

    transpose_half(core)
    slice_half(core)
    landed(held.at[1 - core], 11)
    transpose_half(1 - core)
    slice_half(1 - core)

    lane_row = lax.broadcasted_iota(I32, (GROUP, 128), 1) >> 4
    nothing = jnp.zeros((GROUP, 128), BF16)

    def diagonal(k, tile):
        return jnp.concatenate([tile, nothing] if k < GROUP // 2 else [nothing, tile], axis=1)

    lane_pose = lax.broadcasted_iota(I32, (GROUP, 128), 1) < POSES

    def correlate(g, carry):
        at = pl.ds(pl.multiple_of(g * WIDE, WIDE), WIDE)
        found = jnp.dot(shifted[at, :], slices[:, at], preferred_element_type=F32)
        parts = []
        for k in range(GROUP):
            lane_at = k // (GROUP // 2) * 128
            block = found[k * GROUP : (k + 1) * GROUP, lane_at : lane_at + 128]
            if k % (GROUP // 2):
                block = pltpu.roll(block, 128 - k % (GROUP // 2) * POSES, 1)
            block = jnp.where(lane_pose, block, 0.0)
            high = block.astype(BF16)
            low = (block - high.astype(F32)).astype(BF16)
            parts.append(jnp.concatenate([high, low], axis=1))
        products[at, :] = jnp.concatenate(parts, axis=0)
        return carry

    lax.fori_loop(0, BOX // GROUP, correlate, 0, unroll=True)
    corr = jnp.dot(phases[...], products[...], preferred_element_type=F32)
    half = SHIFTS * SHIFTS
    corr = corr[:half, :POSES] + (corr[half:, :POSES] + corr[:half, 128 : 128 + POSES])
    score = corr * (precision_ref[0] / BOX)
    top = jnp.max(score, axis=(0, 1), keepdims=True)
    terms = jnp.exp(score - top)
    total = jnp.sum(terms, axis=(0, 1), keepdims=True)
    posterior = terms / total
    loglik_ref[0] = ((top + jnp.log(total)) * alive)[0, 0]
    posterior_t = posterior.T
    mass = jnp.sum(posterior_t, axis=1, keepdims=True)

    pairs = []

    def spread_half(first_slot, c):
        return jnp.dot(
            spread[first_slot : first_slot + KEEP, :],
            rows[:, c * BOX : (c + 1) * BOX],
            preferred_element_type=F32,
        )

    def spread_other(c):
        pair_out[c] = spread_half(KEEP, c).astype(BF16)
        copy = remote(pair_out.at[c], pair_in.at[c], pair_send.at[c], pair_recv.at[c], sibling)
        copy.start()
        pairs.append(copy)

    def spread_own(c):
        sums[c] = spread_half(0, c)

    def square_rows(g, carry):
        at = pl.ds(pl.multiple_of(g * WIDE, WIDE), WIDE)
        square = squares[pl.ds(pl.multiple_of(g * GROUP, GROUP), GROUP), :]
        rows[at, 2 * BOX :] = jnp.concatenate(
            [square[k : k + 1, :] * mass for k in range(GROUP)], axis=0
        ).astype(BF16)
        return carry

    def turn_poses():
        high = posterior_t.astype(BF16)
        low = (posterior_t - high.astype(F32)).astype(BF16)
        parts = jnp.concatenate(
            [
                jnp.concatenate([high, high], axis=1),
                jnp.concatenate([low, jnp.zeros_like(low)], axis=1),
            ],
            axis=0,
        )
        both_parts = jnp.dot(parts, phases[...], preferred_element_type=F32)
        turned[...] = (both_parts[:POSES] + both_parts[POSES:]).astype(BF16)

    def insert(g, carry):
        at = pl.ds(pl.multiple_of(g * WIDE, WIDE), WIDE)
        turns_g = turned[:, at]
        weight = jnp.concatenate(
            [
                diagonal(
                    k,
                    jnp.where(
                        lane_row == k % (GROUP // 2),
                        turns_g[:, k // (GROUP // 2) * 128 : k // (GROUP // 2) * 128 + 128],
                        nothing,
                    ),
                )
                for k in range(GROUP)
            ],
            axis=0,
        )
        rows[at, : 2 * BOX] = jnp.dot(
            weight, shifted[at, :], preferred_element_type=F32
        ).astype(BF16)
        return carry

    hops = []

    def hop(number, src, dst, device):
        copy = remote(src, dst, hop_send.at[number], hop_recv.at[number], device)
        copy.start()
        hops.append(copy)
        return copy

    ring8 = (4, 3, 5, 2, 6, 1, 7)
    ring4 = (2, 1, 3)

    lax.fori_loop(0, BOX // GROUP, square_rows, 0, unroll=4)
    spread_other(2)
    spread_own(2)
    turn_poses()
    lax.fori_loop(0, BOX // GROUP, insert, 0, unroll=True)
    pairs[0].wait_recv()
    c_sum = sums[2] + pair_in[2].astype(F32)
    for half in range(2):
        strided[half] = c_sum[:, half * 128 : (half + 1) * 128]

    def c_rows(k):
        rows_k = pl.ds(k, NX * NY, NZ)
        return jnp.concatenate([strided[0, rows_k, :], strided[1, rows_k, :]], axis=1)

    c_hops = []
    for k in ring8:
        cz_out[k] = c_rows(k).astype(BF16)
        c_hops.append(hop(k, cz_out.at[k], cz_in.at[k], along_z(k)))
    spread_other(0)
    spread_other(1)
    spread_own(0)
    spread_own(1)

    pairs[1].wait_recv()
    b_sum = (sums[0] + pair_in[0].astype(F32)).reshape(NX, NY, NZ, BOX)
    b_hops = []
    for k in ring8:
        by_out[k] = b_sum[:, k].reshape(NX * NZ, BOX).astype(BF16)
        b_hops.append(hop(NZ + k, by_out.at[k], by_in.at[k], along_y(k)))
    b_sum = b_sum[:, 0].reshape(NX * NZ, BOX)
    pairs[2].wait_recv()
    a_sum = (sums[1] + pair_in[1].astype(F32)).reshape(NX, NY * NZ, BOX)
    a_hops = []
    for k in ring4:
        ax_out[k] = a_sum[k].astype(BF16)
        a_hops.append(hop(2 * NZ + k, ax_out.at[k], ax_in.at[k], along_x(k)))
    a_sum = a_sum[0]

    pl.semaphore_wait(ready, NX - 1)
    left(held.at[core, y_lo, pl.ds(0, NZ - 1)], 0)
    left(held.at[core, pl.ds(0, 3)], 1)
    left(held.at[core], 2)
    for copy in pairs + hops:
        copy.wait_send()

    def last(rows_out, rows_in, total, number, size, owner):
        count = total.shape[0]
        rows_out[...] = total.reshape(count, 1, BOX)

        def hops_to(n):
            far_step, near_step = divmod(n, 8)
            return min(far_step, size - far_step) + min(near_step, 8 - near_step)

        for n in sorted(range(1, count), key=hops_to, reverse=True):
            remote(
                rows_out.at[n], rows_in.at[n], last_send.at[number], last_recv.at[number], owner(n)
            ).start()

    def collect(rows_in, total, number):
        arrived = rows_in.at[pl.ds(1, total.shape[0] - 1)]
        pltpu.make_async_copy(arrived, arrived, last_recv.at[number]).wait()
        return total[0:1, :] + jnp.sum(rows_in[1:], axis=0)

    def drain(rows_out, number):
        gone = rows_out.at[pl.ds(1, rows_out.shape[0] - 1)]
        pltpu.make_async_copy(gone, gone, last_send.at[number]).wait()

    c_sum = c_rows(0)
    for k, copy in zip(ring8, c_hops):
        copy.wait_recv()
        c_sum = c_sum + cz_in[k].astype(F32)
    last(
        c_last_out,
        c_last_in,
        c_sum,
        2,
        NX,
        lambda n: device_at(z, (y + n % NY) % NY, (x + n // NY) % NX, core),
    )
    for k, copy in zip(ring4, a_hops):
        copy.wait_recv()
        a_sum = a_sum + ax_in[k].astype(F32)
    last(
        a_last_out,
        a_last_in,
        a_sum,
        1,
        NY,
        lambda n: device_at((z + n % NZ) % NZ, (y + n // NZ) % NY, x, core),
    )
    for k, copy in zip(ring8, b_hops):
        copy.wait_recv()
        b_sum = b_sum + by_in[k].astype(F32)
    last(
        b_last_out,
        b_last_in,
        b_sum,
        0,
        NX,
        lambda n: device_at((z + n % NZ) % NZ, y, (x + n // NZ) % NX, core),
    )
    out_ref[:, 2 * BOX :] = collect(c_last_in, c_sum, 2)
    out_ref[:, BOX : 2 * BOX] = collect(a_last_in, a_sum, 1)
    out_ref[:, :BOX] = collect(b_last_in, b_sum, 0)
    drain(c_last_out, 2)
    drain(a_last_out, 1)
    drain(b_last_out, 0)


def expect(*operands):
    smem = pl.BlockSpec(memory_space=pltpu.SMEM)
    vmem = pl.BlockSpec(memory_space=pltpu.VMEM)
    dma = pltpu.SemaphoreType.DMA
    hop_count = 2 * NZ + NX

    def both_ways(shape, kind):
        return [pltpu.VMEM(shape, kind), pltpu.VMEM(shape, kind)]

    return pl.pallas_call(
        expect_kernel,
        out_shape=(
            jax.ShapeDtypeStruct((1, 3 * BOX), F32),
            jax.ShapeDtypeStruct((1,), F32),
        ),
        in_specs=[pl.BlockSpec(memory_space=pltpu.HBM)] * 10,
        out_specs=(vmem, smem),
        scratch_shapes=[
            pltpu.SMEM(operand.shape, operand.dtype) for operand in operands[:6]
        ]
        + [pltpu.VMEM(operand.shape, operand.dtype) for operand in operands[6:]]
        + [dma((10,))]
        + [
            pltpu.VMEM((2, Y_LO, NZ, 16, BOX), BF16),
            pltpu.VMEM((2, GROUP, ROWS), I16),
            pltpu.VMEM((4, GROUP, ROWS), BF16),
            pltpu.VMEM((2 * BOX, 2 * LINES), BF16),
            pltpu.VMEM((2 * LINES, ROWS), BF16),
            pltpu.VMEM((2 * BOX, ROWS), BF16),
            pltpu.VMEM((ROWS, 2 * BOX), BF16),
            pltpu.VMEM((2 * SHIFTS * SHIFTS, ROWS), BF16),
            pltpu.VMEM((BOX, BOX), F32),
            pltpu.VMEM((ROWS, WIDE), BF16),
            pltpu.VMEM((POSES, ROWS), BF16),
            pltpu.VMEM((ROWS, 3 * BOX), BF16),
            pltpu.VMEM((3, KEEP, BOX), F32),
            pltpu.VMEM((2, KEEP, BOX // 2), F32),
        ]
        + both_ways((3, KEEP, BOX), BF16)
        + both_ways((NX, NY * NZ, BOX), BF16)
        + both_ways((NY, NX * NZ, BOX), BF16)
        + both_ways((NZ, NX * NY, BOX), BF16)
        + both_ways((NY * NZ, 1, BOX), F32)
        + both_ways((NX * NZ, 1, BOX), F32)
        + both_ways((NX * NY, 1, BOX), F32)
        + [
            dma((3,)),
            dma((12,)),
            dma((3,)),
            dma((3,)),
            dma((hop_count,)),
            dma((hop_count,)),
            dma((3,)),
            dma((3,)),
            pltpu.SemaphoreType.REGULAR,
        ],
        compiler_params=pltpu.CompilerParams(
            collective_id=0, has_side_effects=True, vmem_limit_bytes=60 * 1024 * 1024
        ),
    )(*operands)


def body(
    particles,
    defocus_class,
    noise_precision,
    live_count,
    defocus,
    reference_lines,
    line_index,
    line_weight,
    row_shifts,
    column_shifts,
):
    index = jnp.transpose(line_index, (0, 2, 1))
    weight = jnp.transpose(line_weight, (0, 2, 1))
    particle_total = particles.shape[0] * lax.axis_size("slab") * lax.axis_size("grp")
    owned, loglik = expect(
        defocus_class,
        noise_precision,
        live_count,
        defocus,
        row_shifts,
        column_shifts,
        particles,
        index,
        weight,
        reference_lines,
    )
    return owned.reshape(1, 3, BOX) * (LINES / (POSES * particle_total)), loglik


def solution(mesh):
    return jax.shard_map(
        body,
        mesh=mesh,
        in_specs=(
            P(("slab", "grp"), None, None, None),
            P(("slab", "grp")),
            P(("slab", "grp")),
            P("grp"),
            P(),
            P("slab", None, None),
            P(),
            P(),
            P(),
            P(),
        ),
        out_specs=(P(("slab", "grp"), None, None), P(("slab", "grp"))),
        check_vma=False,
    )
```

```python
import math

import jax
import jax.numpy as jnp
from jax import lax
from jax.experimental import pallas as pl
from jax.experimental.pallas import tpu as pltpu
from jax.sharding import PartitionSpec as P

MESH = pl.DeviceIdType.MESH
EXACT = lax.Precision.HIGHEST
F32 = jnp.float32
BF16 = jnp.bfloat16
I32 = jnp.int32
I16 = jnp.int16

NX, NY, NZ, Y_LO = 4, 8, 8, 4
SLABS = NZ * Y_LO
LINES = 512
KEEP = LINES // 2
BOX = 256
POSES = 16
GROUP = 16
WIDE = GROUP * POSES
ROWS = POSES * BOX
SHIFTS = 8


def place():
    slab = lax.axis_index("slab")
    grp = lax.axis_index("grp")
    z, y_lo = slab // Y_LO, slab % Y_LO
    y_hi, x, core = grp // (2 * NX), (grp // 2) % NX, grp % 2
    return z, y_hi * Y_LO + y_lo, x, core


def device_at(z, y, x, core):
    return (z * Y_LO + y % Y_LO, (y // Y_LO) * (2 * NX) + x * 2 + core)


def phase_angle(turns):
    signed = ((turns + BOX // 2) & (BOX - 1)) - BOX // 2
    return signed.astype(F32) * (2.0 * math.pi / BOX)


def shift_column(shifts_ref, shape):
    row = lax.broadcasted_iota(I32, shape, 0)
    column = jnp.zeros(shape, I32)
    for t in range(SHIFTS):
        column = jnp.where(row == t, shifts_ref[t], column)
    return column


def slot_of(line, z, y, x, core):
    line_y = ((line >> 3) & 1) * Y_LO + ((line >> 4) & (Y_LO - 1))
    return (
        ((line ^ core) & 1) * KEEP
        + ((((line >> 1) - x) & (NX - 1)) * (NY * NZ))
        + (((line_y - y) & (NY - 1)) * NZ)
        + (((line >> 6) - z) & (NZ - 1))
    )


def held_row(slot, z, y, x, core):
    line_z = (slot + z) & (NZ - 1)
    line_y = ((slot >> 3) + y) & (NY - 1)
    line_x = ((slot >> 6) + x) & (NX - 1)
    line_core = ((slot >> 8) ^ core) & 1
    return (line_y & 3) * (NZ * 16) + line_z * 16 + (line_y >> 2) * 8 + line_x * 2 + line_core


def expect_kernel(
    class_hbm,
    precision_hbm,
    live_hbm,
    defocus_hbm,
    row_shift_hbm,
    column_shift_hbm,
    image_hbm,
    index_hbm,
    weight_hbm,
    lines_hbm,
    out_ref,
    loglik_ref,
    class_ref,
    precision_ref,
    live_ref,
    defocus_ref,
    row_shift_ref,
    column_shift_ref,
    image_ref,
    index_ref,
    weight_ref,
    lines_ref,
    load_sem,
    held,
    slots,
    weights,
    lines_t,
    spread,
    slices,
    shifted,
    phases,
    squares,
    products,
    turned,
    rows,
    pose_slots,
    pose_weights,
    spread_square,
    sums,
    strided,
    pair_out,
    pair_in,
    ax_out,
    ax_in,
    by_out,
    by_in,
    cz_out,
    cz_in,
    a_last_out,
    a_last_in,
    b_last_out,
    b_last_in,
    c_last_out,
    c_last_in,
    gather_send,
    gather_recv,
    pair_send,
    pair_recv,
    hop_send,
    hop_recv,
    last_send,
    last_recv,
    ready,
):
    z, y, x, core = place()
    y_lo = y % Y_LO
    sibling = device_at(z, y, x, 1 - core)

    def along_x(k):
        return device_at(z, y, (x + k) % NX, core)

    def along_y(k):
        return device_at(z, (y + NY + k) % NY, x, core)

    def along_z(k):
        return device_at((z + k) % NZ, y, x, core)

    def remote(src, dst, send, recv, device):
        return pltpu.make_async_remote_copy(
            src_ref=src,
            dst_ref=dst,
            send_sem=send,
            recv_sem=recv,
            device_id=device,
            device_id_type=MESH,
        )

    barrier = pltpu.get_barrier_semaphore()
    peers = [sibling]
    peers += [along_x(k) for k in range(1, NX)]
    peers += [along_y(k) for k in range(1, NY)]
    peers += [along_z(k) for k in range(1, NZ)]
    for peer in peers:
        pl.semaphore_signal(barrier, inc=1, device_id=peer, device_id_type=MESH)

    loads = [
        pltpu.make_async_copy(src, dst, load_sem.at[n])
        for n, (src, dst) in enumerate(
            [
                (lines_hbm, lines_ref),
                (class_hbm, class_ref),
                (live_hbm, live_ref),
                (defocus_hbm, defocus_ref),
                (column_shift_hbm, column_shift_ref),
                (row_shift_hbm, row_shift_ref),
                (image_hbm, image_ref),
                (index_hbm, index_ref),
                (weight_hbm, weight_ref),
                (precision_hbm, precision_ref),
            ]
        )
    ]
    for load in loads:
        load.start()

    loads[0].wait()
    both = lines_ref[...]
    held[core, y_lo, z] = jnp.where(core == 0, both[:, 0, :], both[:, 1, :])

    for load in loads[1:]:
        load.wait()
    alive = jnp.where(0 < live_ref[0], 1.0, 0.0).astype(F32)
    chosen = defocus_ref[class_ref[0]]

    lane_y = lax.broadcasted_iota(I32, (SHIFTS, BOX), 1) - BOX // 2
    angle_y = phase_angle(lane_y * shift_column(column_shift_ref, (SHIFTS, BOX)))
    cos_y = jnp.cos(angle_y)
    sin_y = jnp.sin(angle_y)
    freq_y = (lax.broadcasted_iota(I32, (GROUP, BOX), 1) - BOX // 2).astype(F32) / BOX
    row_in_group = lax.broadcasted_iota(I32, (GROUP, BOX), 0)

    def shift_rows(g, carry):
        at = pl.ds(pl.multiple_of(g * WIDE, WIDE), WIDE)
        kx = pl.ds(pl.multiple_of(g * GROUP, GROUP), GROUP)
        freq_x = (row_in_group + (g * GROUP - BOX // 2)).astype(F32) / BOX
        ctf = -jnp.sin(chosen * (freq_x * freq_x + freq_y * freq_y) + 0.1) * alive
        squares[kx, :] = ctf * ctf
        real = ctf * image_ref[0, 0, kx, :].astype(F32)
        imag = ctf * image_ref[0, 1, kx, :].astype(F32)
        blocks = []
        for k in range(GROUP):
            real_row = real[k : k + 1, :]
            imag_row = imag[k : k + 1, :]
            shift_re = real_row * cos_y + imag_row * sin_y
            shift_im = real_row * sin_y - imag_row * cos_y
            blocks.append(jnp.concatenate([shift_re, -shift_im], axis=1))
            blocks.append(jnp.concatenate([shift_im, shift_re], axis=1))
        shifted[at, :] = jnp.concatenate(blocks, axis=0).astype(BF16)
        return carry

    lax.fori_loop(0, BOX // GROUP, shift_rows, 0)

    pl.semaphore_wait(barrier, len(peers))
    for k in range(1, NX):
        pl.semaphore_signal(ready, inc=1, device_id=along_x(k), device_id_type=MESH)

    def send_block(src, send, recv, device):
        copy = remote(src, src, gather_send.at[send], gather_recv.at[recv], device)
        copy.start()
        return copy

    def landed(blocks, number):
        pltpu.make_async_copy(blocks, blocks, gather_recv.at[number]).wait()

    def left(blocks, number):
        pltpu.make_async_copy(blocks, blocks, gather_send.at[number]).wait()

    groups = ((0, 1, 7), (2, 6), (3, 5, 4))
    near_z = {
        k: send_block(held.at[core, y_lo, z], 0, k, along_z(k)) for k in (4, 3, 5, 2, 6, 1, 7)
    }
    far = 2 - 4 * core
    steps = {1: 1, 2: far, 3: -1}

    def pass_along_y(k):
        block = held.at[core, y_lo, (z + NZ - k) % NZ]
        group = [k in members for members in groups].index(True)
        for d in (2, 1, 3):
            send_block(block, 1, NZ + group, along_y(steps[d]))
        send_block(block, 2, 11, sibling)

    def pass_on(*distances):
        for k in distances:
            near_z[k].wait_recv()
            pass_along_y(k)

    def swap(group):
        landed(held.at[core, pl.ds(0, 3), pl.ds(0, len(groups[group]))], NZ + group)
        for k in groups[group]:
            for residue in (y_lo + 3, y_lo + 1, y_lo + 2):
                send_block(held.at[core, residue % Y_LO, (z + NZ - k) % NZ], 2, 11, sibling)

    pass_along_y(0)
    lane = lax.broadcasted_iota(I32, (SHIFTS, ROWS), 1)
    freq = (lane >> 4) - BOX // 2
    part = (lane >> 3) & 1
    turns = freq * shift_column(row_shift_ref, (SHIFTS, ROWS)) + part * (BOX // 4)
    row_phase = jnp.cos(phase_angle(turns))
    row_high = row_phase.astype(BF16).astype(F32)
    row_low = row_phase - row_high
    for t in range(0, SHIFTS, 2):
        for base, table in ((0, row_high), (SHIFTS * SHIFTS, row_low)):
            phases[pl.ds(base + t * SHIFTS, 2 * SHIFTS), :] = jnp.concatenate(
                [jnp.where((lane & 7) == t + u, table, 0.0) for u in range(2)], axis=0
            ).astype(BF16)

    pass_on(1, 7)
    first = slot_of(index_ref[:, 0, :], z, y, x, core)
    second = slot_of(index_ref[:, 1, :], z, y, x, core)
    first_weight = weight_ref[:, 0, :]
    second_weight = weight_ref[:, 1, :]
    same = first == second
    first_weight = jnp.where(same, first_weight + second_weight, first_weight)
    second_weight = jnp.where(same, 0.0, second_weight)
    first_high = first_weight.astype(BF16).astype(F32)
    second_high = second_weight.astype(BF16).astype(F32)
    tables = jnp.concatenate(
        [
            (first >> 4).astype(F32),
            (first & 15).astype(F32),
            (second >> 4).astype(F32),
            (second & 15).astype(F32),
            first_high,
            second_high,
            first_weight - first_high,
            second_weight - second_high,
        ],
        axis=0,
    ).astype(BF16)
    table_lane = lax.broadcasted_iota(I32, (BOX, WIDE), 1) >> 4
    table_row = lax.broadcasted_iota(I32, (BOX, WIDE), 0)
    pose_row = lax.broadcasted_iota(I32, (POSES, WIDE), 0) == (
        lax.broadcasted_iota(I32, (POSES, WIDE), 1) & (POSES - 1)
    )

    def table_rows(g, carry):
        at = pl.ds(pl.multiple_of(g * WIDE, WIDE), WIDE)
        chosen_row = jnp.where(table_row == table_lane + g * GROUP, 1.0, 0.0).astype(BF16)
        wide = jnp.dot(tables, chosen_row, preferred_element_type=F32)
        found = [
            jnp.sum(
                jnp.where(pose_row, wide[n * POSES : (n + 1) * POSES, :], 0.0),
                axis=0,
                keepdims=True,
            )
            for n in range(8)
        ]
        for n in range(2):
            slot = (found[2 * n] * 16.0 + found[2 * n + 1]).astype(I32)
            slots[n, :, at] = jnp.broadcast_to(slot, (GROUP, WIDE)).astype(I16)
        for n in range(4):
            weights[n, :, at] = jnp.broadcast_to(found[4 + n], (GROUP, WIDE)).astype(BF16)
        return carry

    lax.fori_loop(0, 8, table_rows, 0, unroll=2)
    pass_on(2, 6)
    lax.fori_loop(8, BOX // GROUP, table_rows, 0, unroll=2)
    pass_on(3, 5, 4)
    slot_row = lax.broadcasted_iota(I32, (GROUP, WIDE), 0).astype(I16)

    def spread_rows(g, carry):
        at = pl.ds(pl.multiple_of(g * WIDE, WIDE), WIDE)
        first_slot, second_slot = slots[0, :, at], slots[1, :, at]
        parts = [weights[n, :, at] for n in range(4)]
        for block in range(LINES // GROUP):
            row = slot_row + jnp.int16(block * GROUP)
            is_first = first_slot == row
            is_second = second_slot == row
            for n, base in ((0, 0), (2, LINES)):
                rest = jnp.where(is_second, parts[n + 1], jnp.zeros_like(parts[n]))
                spread[base + block * GROUP : base + (block + 1) * GROUP, at] = jnp.where(
                    is_first, parts[n], rest
                )
        return carry

    lax.fori_loop(0, 5, spread_rows, 0)
    swap(0)
    lax.fori_loop(5, 10, spread_rows, 0)
    swap(1)
    lax.fori_loop(10, BOX // GROUP, spread_rows, 0)

    square = squares[...].astype(BF16)
    slot_rows = lax.broadcasted_iota(I32, (GROUP, BOX), 0).astype(I16)
    for n, table, target, kind in (
        (0, first, pose_slots, I16),
        (1, second, pose_slots, I16),
        (0, first_high, pose_weights, BF16),
        (1, second_high, pose_weights, BF16),
    ):
        for p in range(POSES):
            target[n, p * GROUP : (p + 1) * GROUP, :] = jnp.broadcast_to(
                table[p : p + 1, :], (GROUP, BOX)
            ).astype(kind)

    def spread_squares(p, carry):
        rows_p = pl.ds(pl.multiple_of(p * GROUP, GROUP), GROUP)
        first_slot, second_slot = pose_slots[0, rows_p, :], pose_slots[1, rows_p, :]
        first_part, second_part = pose_weights[0, rows_p, :], pose_weights[1, rows_p, :]
        blocks = []
        for block in range(LINES // GROUP):
            row = slot_rows + jnp.int16(block * GROUP)
            rest = jnp.where(second_slot == row, second_part, jnp.zeros_like(second_part))
            blocks.append(jnp.where(first_slot == row, first_part, rest))
        spread_square[p] = jnp.dot(
            jnp.concatenate(blocks, axis=0), square, preferred_element_type=F32
        )
        return carry

    lax.fori_loop(0, POSES, spread_squares, 0, unroll=4)
    swap(2)

    slot_lines = held_row(lax.broadcasted_iota(I32, (1, LINES), 1), z, y, x, core)
    order = jnp.where(
        lax.broadcasted_iota(I32, (LINES, LINES), 0) == slot_lines, 1.0, 0.0
    ).astype(BF16)

    def transpose_half(c):
        half = lax.dot_general(
            held[c].reshape(LINES, BOX),
            order,
            (((0,), (0,)), ((), ())),
            preferred_element_type=F32,
        ).astype(BF16)
        lines_t[pl.ds(pl.multiple_of(c * BOX, BOX), BOX), :] = jnp.concatenate(
            [half, half], axis=1
        )

    def slice_half(c):
        half = pl.ds(pl.multiple_of(c * BOX, BOX), BOX)

        def step(n, carry):
            at = pl.ds(pl.multiple_of(n * 4 * WIDE, 4 * WIDE), 4 * WIDE)
            slices[half, at] = jnp.dot(
                lines_t[half, :], spread[:, at], preferred_element_type=F32
            ).astype(BF16)
            return carry

        lax.fori_loop(0, ROWS // (4 * WIDE), step, 0, unroll=True)

    transpose_half(core)
    slice_half(core)
    landed(held.at[1 - core], 11)
    transpose_half(1 - core)
    slice_half(1 - core)

    lane_row = lax.broadcasted_iota(I32, (GROUP, 128), 1) >> 4
    nothing = jnp.zeros((GROUP, 128), BF16)

    def diagonal(k, tile):
        return jnp.concatenate([tile, nothing] if k < GROUP // 2 else [nothing, tile], axis=1)

    lane_pose = lax.broadcasted_iota(I32, (GROUP, 128), 1) < POSES

    def correlate(g, carry):
        at = pl.ds(pl.multiple_of(g * WIDE, WIDE), WIDE)
        found = jnp.dot(shifted[at, :], slices[:, at], preferred_element_type=F32)
        parts = []
        for k in range(GROUP):
            lane_at = k // (GROUP // 2) * 128
            block = found[k * GROUP : (k + 1) * GROUP, lane_at : lane_at + 128]
            if k % (GROUP // 2):
                block = pltpu.roll(block, 128 - k % (GROUP // 2) * POSES, 1)
            block = jnp.where(lane_pose, block, 0.0)
            high = block.astype(BF16)
            low = (block - high.astype(F32)).astype(BF16)
            parts.append(jnp.concatenate([high, low], axis=1))
        products[at, :] = jnp.concatenate(parts, axis=0)
        return carry

    lax.fori_loop(0, BOX // GROUP, correlate, 0, unroll=True)
    corr = jnp.dot(phases[...], products[...], preferred_element_type=F32)
    half = SHIFTS * SHIFTS
    corr = corr[:half, :POSES] + (corr[half:, :POSES] + corr[:half, 128 : 128 + POSES])
    score = corr * (precision_ref[0] / BOX)
    top = jnp.max(score, axis=(0, 1), keepdims=True)
    terms = jnp.exp(score - top)
    total = jnp.sum(terms, axis=(0, 1), keepdims=True)
    posterior = terms / total
    loglik_ref[0] = ((top + jnp.log(total)) * alive)[0, 0]
    posterior_t = posterior.T
    mass = jnp.sum(posterior_t, axis=1, keepdims=True)

    ring8 = (4, 3, 5, 2, 6, 1, 7)
    ring4 = (2, 1, 3)
    pairs = []

    def spread_half(first_slot, c):
        return jnp.dot(
            spread[first_slot : first_slot + KEEP, :],
            rows[:, c * BOX : (c + 1) * BOX],
            preferred_element_type=F32,
        )

    def send_pair(c, total):
        pair_out[c] = total.astype(BF16)
        copy = remote(pair_out.at[c], pair_in.at[c], pair_send.at[c], pair_recv.at[c], sibling)
        copy.start()
        pairs.append(copy)

    part = NY * NZ
    a_pairs = {}

    def send_pair_blocks(c, total):
        pair_out[c] = total.astype(BF16)
        for n, k in enumerate(ring4 + (0,)):
            block = pl.ds(k * part, part)
            copy = remote(
                pair_out.at[c, block],
                pair_in.at[c, block],
                pair_send.at[3 + n],
                pair_recv.at[3 + n],
                sibling,
            )
            copy.start()
            pairs.append(copy)
            a_pairs[k] = copy

    def spread_own(c):
        sums[c] = spread_half(0, c)

    def spread_mass(first_slot):
        total = spread_square[0, first_slot : first_slot + KEEP, :] * mass[0:1, :]
        for p in range(1, POSES):
            total = total + spread_square[p, first_slot : first_slot + KEEP, :] * mass[p : p + 1, :]
        return total

    def turn_poses():
        high = posterior_t.astype(BF16)
        low = (posterior_t - high.astype(F32)).astype(BF16)
        parts = jnp.concatenate(
            [
                jnp.concatenate([high, high], axis=1),
                jnp.concatenate([low, jnp.zeros_like(low)], axis=1),
            ],
            axis=0,
        )
        both_parts = jnp.dot(parts, phases[...], preferred_element_type=F32)
        turned[...] = (both_parts[:POSES] + both_parts[POSES:]).astype(BF16)

    def insert(g, carry):
        at = pl.ds(pl.multiple_of(g * WIDE, WIDE), WIDE)
        turns_g = turned[:, at]
        weight = jnp.concatenate(
            [
                diagonal(
                    k,
                    jnp.where(
                        lane_row == k % (GROUP // 2),
                        turns_g[:, k // (GROUP // 2) * 128 : k // (GROUP // 2) * 128 + 128],
                        nothing,
                    ),
                )
                for k in range(GROUP)
            ],
            axis=0,
        )
        rows[at, :] = jnp.dot(
            weight, shifted[at, :], preferred_element_type=F32
        ).astype(BF16)
        return carry

    hops = []

    def hop(number, src, dst, device):
        copy = remote(src, dst, hop_send.at[number], hop_recv.at[number], device)
        copy.start()
        hops.append(copy)
        return copy


    send_pair(2, spread_mass(KEEP))
    sums[2] = spread_mass(0)
    turn_poses()
    lax.fori_loop(0, BOX // GROUP, insert, 0, unroll=True)
    pairs[0].wait_recv()
    c_sum = sums[2] + pair_in[2].astype(F32)
    for half in range(2):
        strided[half] = c_sum[:, half * 128 : (half + 1) * 128]

    def c_rows(k):
        rows_k = pl.ds(k, NX * NY, NZ)
        return jnp.concatenate([strided[0, rows_k, :], strided[1, rows_k, :]], axis=1)

    c_hops = []
    for k in ring8:
        cz_out[k] = c_rows(k).astype(BF16)
        c_hops.append(hop(k, cz_out.at[k], cz_in.at[k], along_z(k)))
    send_pair(0, spread_half(KEEP, 0))
    send_pair_blocks(1, spread_half(KEEP, 1))
    spread_own(0)
    spread_own(1)

    pairs[1].wait_recv()
    b_sum = (sums[0] + pair_in[0].astype(F32)).reshape(NX, NY, NZ, BOX)
    b_hops = []
    for k in ring8:
        by_out[k] = b_sum[:, k].reshape(NX * NZ, BOX).astype(BF16)
        b_hops.append(hop(NZ + k, by_out.at[k], by_in.at[k], along_y(k)))
    b_sum = b_sum[:, 0].reshape(NX * NZ, BOX)
    def a_block(k):
        a_pairs[k].wait_recv()
        block = pl.ds(k * part, part)
        return sums[1, block, :] + pair_in[1, block, :].astype(F32)

    a_hops = []
    for k in ring4:
        ax_out[k] = a_block(k).astype(BF16)
        a_hops.append(hop(2 * NZ + k, ax_out.at[k], ax_in.at[k], along_x(k)))
    a_sum = a_block(0)

    pl.semaphore_wait(ready, NX - 1)
    left(held.at[core, y_lo, pl.ds(0, NZ - 1)], 0)
    left(held.at[core, pl.ds(0, 3)], 1)
    left(held.at[core], 2)
    for copy in pairs + hops:
        copy.wait_send()

    def last(rows_out, rows_in, total, number, size, owner):
        count = total.shape[0]
        rows_out[...] = total.reshape(count, 1, BOX)

        def hops_to(n):
            far_step, near_step = divmod(n, 8)
            return min(far_step, size - far_step) + min(near_step, 8 - near_step)

        for n in sorted(range(1, count), key=hops_to, reverse=True):
            remote(
                rows_out.at[n], rows_in.at[n], last_send.at[number], last_recv.at[number], owner(n)
            ).start()

    def collect(rows_in, total, number):
        arrived = rows_in.at[pl.ds(1, total.shape[0] - 1)]
        pltpu.make_async_copy(arrived, arrived, last_recv.at[number]).wait()
        return total[0:1, :] + jnp.sum(rows_in[1:], axis=0)

    def drain(rows_out, number):
        gone = rows_out.at[pl.ds(1, rows_out.shape[0] - 1)]
        pltpu.make_async_copy(gone, gone, last_send.at[number]).wait()

    c_sum = c_rows(0)
    for k, copy in zip(ring8, c_hops):
        copy.wait_recv()
        c_sum = c_sum + cz_in[k].astype(F32)
    last(
        c_last_out,
        c_last_in,
        c_sum,
        2,
        NX,
        lambda n: device_at(z, (y + n % NY) % NY, (x + n // NY) % NX, core),
    )
    for k, copy in zip(ring4, a_hops):
        copy.wait_recv()
        a_sum = a_sum + ax_in[k].astype(F32)
    last(
        a_last_out,
        a_last_in,
        a_sum,
        1,
        NY,
        lambda n: device_at((z + n % NZ) % NZ, (y + n // NZ) % NY, x, core),
    )
    for k, copy in zip(ring8, b_hops):
        copy.wait_recv()
        b_sum = b_sum + by_in[k].astype(F32)
    last(
        b_last_out,
        b_last_in,
        b_sum,
        0,
        NX,
        lambda n: device_at((z + n % NZ) % NZ, y, (x + n // NZ) % NX, core),
    )
    out_ref[:, 2 * BOX :] = collect(c_last_in, c_sum, 2)
    out_ref[:, BOX : 2 * BOX] = collect(a_last_in, a_sum, 1)
    out_ref[:, :BOX] = collect(b_last_in, b_sum, 0)
    drain(c_last_out, 2)
    drain(a_last_out, 1)
    drain(b_last_out, 0)


def expect(*operands):
    smem = pl.BlockSpec(memory_space=pltpu.SMEM)
    vmem = pl.BlockSpec(memory_space=pltpu.VMEM)
    dma = pltpu.SemaphoreType.DMA
    hop_count = 2 * NZ + NX

    def both_ways(shape, kind):
        return [pltpu.VMEM(shape, kind), pltpu.VMEM(shape, kind)]

    return pl.pallas_call(
        expect_kernel,
        out_shape=(
            jax.ShapeDtypeStruct((1, 3 * BOX), F32),
            jax.ShapeDtypeStruct((1,), F32),
        ),
        in_specs=[pl.BlockSpec(memory_space=pltpu.HBM)] * 10,
        out_specs=(vmem, smem),
        scratch_shapes=[
            pltpu.SMEM(operand.shape, operand.dtype) for operand in operands[:6]
        ]
        + [pltpu.VMEM(operand.shape, operand.dtype) for operand in operands[6:]]
        + [dma((10,))]
        + [
            pltpu.VMEM((2, Y_LO, NZ, 16, BOX), BF16),
            pltpu.VMEM((2, GROUP, ROWS), I16),
            pltpu.VMEM((4, GROUP, ROWS), BF16),
            pltpu.VMEM((2 * BOX, 2 * LINES), BF16),
            pltpu.VMEM((2 * LINES, ROWS), BF16),
            pltpu.VMEM((2 * BOX, ROWS), BF16),
            pltpu.VMEM((ROWS, 2 * BOX), BF16),
            pltpu.VMEM((2 * SHIFTS * SHIFTS, ROWS), BF16),
            pltpu.VMEM((BOX, BOX), F32),
            pltpu.VMEM((ROWS, WIDE), BF16),
            pltpu.VMEM((POSES, ROWS), BF16),
            pltpu.VMEM((ROWS, 2 * BOX), BF16),
            pltpu.VMEM((2, POSES * GROUP, BOX), I16),
            pltpu.VMEM((2, POSES * GROUP, BOX), BF16),
            pltpu.VMEM((POSES, LINES, BOX), F32),
            pltpu.VMEM((3, KEEP, BOX), F32),
            pltpu.VMEM((2, KEEP, BOX // 2), F32),
        ]
        + both_ways((3, KEEP, BOX), BF16)
        + both_ways((NX, NY * NZ, BOX), BF16)
        + both_ways((NY, NX * NZ, BOX), BF16)
        + both_ways((NZ, NX * NY, BOX), BF16)
        + both_ways((NY * NZ, 1, BOX), F32)
        + both_ways((NX * NZ, 1, BOX), F32)
        + both_ways((NX * NY, 1, BOX), F32)
        + [
            dma((3,)),
            dma((12,)),
            dma((7,)),
            dma((7,)),
            dma((hop_count,)),
            dma((hop_count,)),
            dma((3,)),
            dma((3,)),
            pltpu.SemaphoreType.REGULAR,
        ],
        compiler_params=pltpu.CompilerParams(
            collective_id=0, has_side_effects=True, vmem_limit_bytes=60 * 1024 * 1024
        ),
    )(*operands)


def body(
    particles,
    defocus_class,
    noise_precision,
    live_count,
    defocus,
    reference_lines,
    line_index,
    line_weight,
    row_shifts,
    column_shifts,
):
    index = jnp.transpose(line_index, (0, 2, 1))
    weight = jnp.transpose(line_weight, (0, 2, 1))
    particle_total = particles.shape[0] * lax.axis_size("slab") * lax.axis_size("grp")
    owned, loglik = expect(
        defocus_class,
        noise_precision,
        live_count,
        defocus,
        row_shifts,
        column_shifts,
        particles,
        index,
        weight,
        reference_lines,
    )
    return owned.reshape(1, 3, BOX) * (LINES / (POSES * particle_total)), loglik


def solution(mesh):
    return jax.shard_map(
        body,
        mesh=mesh,
        in_specs=(
            P(("slab", "grp"), None, None, None),
            P(("slab", "grp")),
            P(("slab", "grp")),
            P("grp"),
            P(),
            P("slab", None, None),
            P(),
            P(),
            P(),
            P(),
        ),
        out_specs=(P(("slab", "grp"), None, None), P(("slab", "grp"))),
        check_vma=False,
    )
```

```python
import math

import jax
import jax.numpy as jnp
from jax import lax
from jax.experimental import pallas as pl
from jax.experimental.pallas import tpu as pltpu
from jax.sharding import PartitionSpec as P

MESH = pl.DeviceIdType.MESH
EXACT = lax.Precision.HIGHEST
F32 = jnp.float32
BF16 = jnp.bfloat16
I32 = jnp.int32
I16 = jnp.int16

NX, NY, NZ, Y_LO = 4, 8, 8, 4
SLABS = NZ * Y_LO
LINES = 512
KEEP = LINES // 2
BOX = 256
POSES = 16
GROUP = 16
WIDE = GROUP * POSES
ROWS = POSES * BOX
SHIFTS = 8


def place():
    slab = lax.axis_index("slab")
    grp = lax.axis_index("grp")
    z, y_lo = slab // Y_LO, slab % Y_LO
    y_hi, x, core = grp // (2 * NX), (grp // 2) % NX, grp % 2
    return z, y_hi * Y_LO + y_lo, x, core


def device_at(z, y, x, core):
    return (z * Y_LO + y % Y_LO, (y // Y_LO) * (2 * NX) + x * 2 + core)


def phase_angle(turns):
    signed = ((turns + BOX // 2) & (BOX - 1)) - BOX // 2
    return signed.astype(F32) * (2.0 * math.pi / BOX)


def shift_column(shifts_ref, shape):
    row = lax.broadcasted_iota(I32, shape, 0)
    column = jnp.zeros(shape, I32)
    for t in range(SHIFTS):
        column = jnp.where(row == t, shifts_ref[t], column)
    return column


def slot_of(line, z, y, x, core):
    line_y = ((line >> 3) & 1) * Y_LO + ((line >> 4) & (Y_LO - 1))
    return (
        ((line ^ core) & 1) * KEEP
        + ((((line >> 1) - x) & (NX - 1)) * (NY * NZ))
        + (((line_y - y) & (NY - 1)) * NZ)
        + (((line >> 6) - z) & (NZ - 1))
    )


def held_row(slot, z, y, x, core):
    line_z = (slot + z) & (NZ - 1)
    line_y = ((slot >> 3) + y) & (NY - 1)
    line_x = ((slot >> 6) + x) & (NX - 1)
    line_core = ((slot >> 8) ^ core) & 1
    return (line_y & 3) * (NZ * 16) + line_z * 16 + (line_y >> 2) * 8 + line_x * 2 + line_core


def expect_kernel(
    class_hbm,
    precision_hbm,
    live_hbm,
    defocus_hbm,
    row_shift_hbm,
    column_shift_hbm,
    image_hbm,
    index_hbm,
    weight_hbm,
    lines_hbm,
    out_ref,
    loglik_ref,
    class_ref,
    precision_ref,
    live_ref,
    defocus_ref,
    row_shift_ref,
    column_shift_ref,
    image_ref,
    index_ref,
    weight_ref,
    lines_ref,
    load_sem,
    held,
    slots,
    weights,
    lines_t,
    spread,
    slices,
    shifted,
    phases,
    squares,
    products,
    turned,
    rows,
    pose_slots,
    pose_weights,
    spread_square,
    sums,
    strided,
    pair_out,
    pair_in,
    ax_out,
    ax_in,
    by_out,
    by_in,
    cz_out,
    cz_in,
    a_last_out,
    a_last_in,
    b_last_out,
    b_last_in,
    c_last_out,
    c_last_in,
    gather_send,
    gather_recv,
    pair_send,
    pair_recv,
    hop_send,
    hop_recv,
    last_send,
    last_recv,
    ready,
):
    z, y, x, core = place()
    y_lo = y % Y_LO
    sibling = device_at(z, y, x, 1 - core)

    def along_x(k):
        return device_at(z, y, (x + k) % NX, core)

    def along_y(k):
        return device_at(z, (y + NY + k) % NY, x, core)

    def along_z(k):
        return device_at((z + k) % NZ, y, x, core)

    def remote(src, dst, send, recv, device):
        return pltpu.make_async_remote_copy(
            src_ref=src,
            dst_ref=dst,
            send_sem=send,
            recv_sem=recv,
            device_id=device,
            device_id_type=MESH,
        )

    barrier = pltpu.get_barrier_semaphore()
    peers = [sibling]
    peers += [along_x(k) for k in range(1, NX)]
    peers += [along_y(k) for k in range(1, NY)]
    peers += [along_z(k) for k in range(1, NZ)]
    for peer in peers:
        pl.semaphore_signal(barrier, inc=1, device_id=peer, device_id_type=MESH)

    loads = [
        pltpu.make_async_copy(src, dst, load_sem.at[n])
        for n, (src, dst) in enumerate(
            [
                (lines_hbm, lines_ref),
                (class_hbm, class_ref),
                (live_hbm, live_ref),
                (defocus_hbm, defocus_ref),
                (column_shift_hbm, column_shift_ref),
                (row_shift_hbm, row_shift_ref),
                (image_hbm, image_ref),
                (index_hbm, index_ref),
                (weight_hbm, weight_ref),
                (precision_hbm, precision_ref),
            ]
        )
    ]
    for load in loads:
        load.start()

    loads[0].wait()
    both = lines_ref[...]
    held[core, y_lo, z] = jnp.where(core == 0, both[:, 0, :], both[:, 1, :])

    pl.semaphore_wait(barrier, len(peers))
    for k in range(1, NX):
        pl.semaphore_signal(ready, inc=1, device_id=along_x(k), device_id_type=MESH)

    def send_block(src, send, recv, device):
        copy = remote(src, src, gather_send.at[send], gather_recv.at[recv], device)
        copy.start()
        return copy

    def landed(blocks, number):
        pltpu.make_async_copy(blocks, blocks, gather_recv.at[number]).wait()

    def left(blocks, number):
        pltpu.make_async_copy(blocks, blocks, gather_send.at[number]).wait()

    groups = ((0, 1, 7), (2, 6), (3, 5, 4))
    near_z = {
        k: send_block(held.at[core, y_lo, z], 0, k, along_z(k)) for k in (4, 3, 5, 2, 6, 1, 7)
    }
    far = 2 - 4 * core
    steps = {1: 1, 2: far, 3: -1}

    def pass_along_y(k):
        block = held.at[core, y_lo, (z + NZ - k) % NZ]
        group = [k in members for members in groups].index(True)
        for d in (2, 1, 3):
            send_block(block, 1, NZ + group, along_y(steps[d]))
        send_block(block, 2, 11, sibling)

    def pass_on(*distances):
        for k in distances:
            near_z[k].wait_recv()
            pass_along_y(k)

    def swap(group):
        landed(held.at[core, pl.ds(0, 3), pl.ds(0, len(groups[group]))], NZ + group)
        for k in groups[group]:
            for residue in (y_lo + 3, y_lo + 1, y_lo + 2):
                send_block(held.at[core, residue % Y_LO, (z + NZ - k) % NZ], 2, 11, sibling)

    pass_along_y(0)
    for load in loads[1:]:
        load.wait()
    alive = jnp.where(0 < live_ref[0], 1.0, 0.0).astype(F32)
    chosen = defocus_ref[class_ref[0]]

    lane_y = lax.broadcasted_iota(I32, (SHIFTS, BOX), 1) - BOX // 2
    angle_y = phase_angle(lane_y * shift_column(column_shift_ref, (SHIFTS, BOX)))
    cos_y = jnp.cos(angle_y)
    sin_y = jnp.sin(angle_y)
    freq_y = (lax.broadcasted_iota(I32, (GROUP, BOX), 1) - BOX // 2).astype(F32) / BOX
    row_in_group = lax.broadcasted_iota(I32, (GROUP, BOX), 0)

    def shift_rows(g, carry):
        at = pl.ds(pl.multiple_of(g * WIDE, WIDE), WIDE)
        kx = pl.ds(pl.multiple_of(g * GROUP, GROUP), GROUP)
        freq_x = (row_in_group + (g * GROUP - BOX // 2)).astype(F32) / BOX
        ctf = -jnp.sin(chosen * (freq_x * freq_x + freq_y * freq_y) + 0.1) * alive
        squares[kx, :] = (ctf * ctf).astype(BF16)
        real = ctf * image_ref[0, 0, kx, :].astype(F32)
        imag = ctf * image_ref[0, 1, kx, :].astype(F32)
        blocks = []
        for k in range(GROUP):
            real_row = real[k : k + 1, :]
            imag_row = imag[k : k + 1, :]
            shift_re = real_row * cos_y + imag_row * sin_y
            shift_im = real_row * sin_y - imag_row * cos_y
            blocks.append(jnp.concatenate([shift_re, -shift_im], axis=1))
            blocks.append(jnp.concatenate([shift_im, shift_re], axis=1))
        shifted[at, :] = jnp.concatenate(blocks, axis=0).astype(BF16)
        return carry


    lane = lax.broadcasted_iota(I32, (SHIFTS, ROWS), 1)
    freq = (lane >> 4) - BOX // 2
    part = (lane >> 3) & 1
    turns = freq * shift_column(row_shift_ref, (SHIFTS, ROWS)) + part * (BOX // 4)
    row_phase = jnp.cos(phase_angle(turns))
    row_high = row_phase.astype(BF16).astype(F32)
    row_low = row_phase - row_high
    for t in range(0, SHIFTS, 2):
        for base, table in ((0, row_high), (SHIFTS * SHIFTS, row_low)):
            phases[pl.ds(base + t * SHIFTS, 2 * SHIFTS), :] = jnp.concatenate(
                [jnp.where((lane & 7) == t + u, table, 0.0) for u in range(2)], axis=0
            ).astype(BF16)

    first = slot_of(index_ref[:, 0, :], z, y, x, core)
    second = slot_of(index_ref[:, 1, :], z, y, x, core)
    first_weight = weight_ref[:, 0, :]
    second_weight = weight_ref[:, 1, :]
    same = first == second
    first_weight = jnp.where(same, first_weight + second_weight, first_weight)
    second_weight = jnp.where(same, 0.0, second_weight)
    first_high = first_weight.astype(BF16).astype(F32)
    second_high = second_weight.astype(BF16).astype(F32)
    tables = jnp.concatenate(
        [
            (first >> 4).astype(F32),
            (first & 15).astype(F32),
            (second >> 4).astype(F32),
            (second & 15).astype(F32),
            first_high,
            second_high,
            first_weight - first_high,
            second_weight - second_high,
        ],
        axis=0,
    ).astype(BF16)
    table_step = (
        lax.broadcasted_iota(I32, (BOX, WIDE), 0)
        - (lax.broadcasted_iota(I32, (BOX, WIDE), 1) >> 4)
    ).astype(I16)
    one = jnp.ones((BOX, WIDE), BF16)
    pose_row = lax.broadcasted_iota(I32, (POSES, WIDE), 0) == (
        lax.broadcasted_iota(I32, (POSES, WIDE), 1) & (POSES - 1)
    )

    def table_rows(g, carry):
        at = pl.ds(pl.multiple_of(g * WIDE, WIDE), WIDE)
        first_row = jnp.full((BOX, WIDE), g * GROUP, I32).astype(I16)
        chosen_row = jnp.where(table_step == first_row, one, jnp.zeros_like(one))
        wide = jnp.dot(tables, chosen_row, preferred_element_type=F32)
        found = [
            jnp.sum(
                jnp.where(pose_row, wide[n * POSES : (n + 1) * POSES, :], 0.0),
                axis=0,
                keepdims=True,
            )
            for n in range(8)
        ]
        for n in range(2):
            slot = (found[2 * n] * 16.0 + found[2 * n + 1]).astype(I32)
            slots[n, :, at] = jnp.broadcast_to(slot, (GROUP, WIDE)).astype(I16)
        for n in range(4):
            weights[n, :, at] = jnp.broadcast_to(found[4 + n], (GROUP, WIDE)).astype(BF16)
        return carry

    lax.fori_loop(0, BOX // GROUP, table_rows, 0, unroll=8)
    pass_on(1, 7)
    slot_row = lax.broadcasted_iota(I32, (GROUP, WIDE), 0).astype(I16)

    def spread_rows(g, carry):
        at = pl.ds(pl.multiple_of(g * WIDE, WIDE), WIDE)
        first_slot, second_slot = slots[0, :, at], slots[1, :, at]
        parts = [weights[n, :, at] for n in range(4)]
        for block in range(LINES // GROUP):
            row = slot_row + jnp.int16(block * GROUP)
            is_first = first_slot == row
            is_second = second_slot == row
            for n, base in ((0, 0), (2, LINES)):
                rest = jnp.where(is_second, parts[n + 1], jnp.zeros_like(parts[n]))
                spread[base + block * GROUP : base + (block + 1) * GROUP, at] = jnp.where(
                    is_first, parts[n], rest
                )
        return carry

    lax.fori_loop(0, BOX // GROUP, spread_rows, 0)
    pass_on(2, 6)

    slot_rows = lax.broadcasted_iota(I32, (GROUP, BOX), 0).astype(I16)
    for n, table, target, kind in (
        (0, first, pose_slots, I16),
        (1, second, pose_slots, I16),
        (0, first_high, pose_weights, BF16),
        (1, second_high, pose_weights, BF16),
    ):
        for p in range(POSES):
            target[n, p * GROUP : (p + 1) * GROUP, :] = jnp.broadcast_to(
                table[p : p + 1, :], (GROUP, BOX)
            ).astype(kind)

    def spread_squares(p, carry):
        rows_p = pl.ds(pl.multiple_of(p * GROUP, GROUP), GROUP)
        first_slot, second_slot = pose_slots[0, rows_p, :], pose_slots[1, rows_p, :]
        first_part, second_part = pose_weights[0, rows_p, :], pose_weights[1, rows_p, :]
        blocks = []
        for block in range(LINES // GROUP):
            row = slot_rows + jnp.int16(block * GROUP)
            rest = jnp.where(second_slot == row, second_part, jnp.zeros_like(second_part))
            blocks.append(jnp.where(first_slot == row, first_part, rest))
        spread_square[p] = jnp.dot(
            jnp.concatenate(blocks, axis=0), squares[...], preferred_element_type=F32
        )
        return carry

    pass_on(3, 5, 4)
    lax.fori_loop(0, 8, shift_rows, 0)
    swap(0)
    lax.fori_loop(8, BOX // GROUP, shift_rows, 0)
    swap(1)
    lax.fori_loop(0, POSES, spread_squares, 0, unroll=8)
    swap(2)

    slot_lines = held_row(lax.broadcasted_iota(I32, (1, LINES), 1), z, y, x, core)
    order = jnp.where(
        lax.broadcasted_iota(I32, (LINES, LINES), 0) == slot_lines, 1.0, 0.0
    ).astype(BF16)

    def transpose_half(c):
        half = lax.dot_general(
            held[c].reshape(LINES, BOX),
            order,
            (((0,), (0,)), ((), ())),
            preferred_element_type=F32,
        ).astype(BF16)
        lines_t[pl.ds(pl.multiple_of(c * BOX, BOX), BOX), :] = jnp.concatenate(
            [half, half], axis=1
        )

    def slice_half(c):
        half = pl.ds(pl.multiple_of(c * BOX, BOX), BOX)

        def step(n, carry):
            at = pl.ds(pl.multiple_of(n * 4 * WIDE, 4 * WIDE), 4 * WIDE)
            slices[half, at] = jnp.dot(
                lines_t[half, :], spread[:, at], preferred_element_type=F32
            ).astype(BF16)
            return carry

        lax.fori_loop(0, ROWS // (4 * WIDE), step, 0, unroll=True)

    transpose_half(core)
    slice_half(core)
    landed(held.at[1 - core], 11)
    transpose_half(1 - core)
    slice_half(1 - core)

    lane_row = lax.broadcasted_iota(I32, (GROUP, 128), 1) >> 4
    nothing = jnp.zeros((GROUP, 128), BF16)

    def diagonal(k, tile):
        return jnp.concatenate([tile, nothing] if k < GROUP // 2 else [nothing, tile], axis=1)

    lane_pose = lax.broadcasted_iota(I32, (GROUP, 128), 1) < POSES

    def correlate(g, carry):
        at = pl.ds(pl.multiple_of(g * WIDE, WIDE), WIDE)
        found = jnp.dot(shifted[at, :], slices[:, at], preferred_element_type=F32)
        parts = []
        for k in range(GROUP):
            lane_at = k // (GROUP // 2) * 128
            block = found[k * GROUP : (k + 1) * GROUP, lane_at : lane_at + 128]
            if k % (GROUP // 2):
                block = pltpu.roll(block, 128 - k % (GROUP // 2) * POSES, 1)
            block = jnp.where(lane_pose, block, 0.0)
            high = block.astype(BF16)
            low = (block - high.astype(F32)).astype(BF16)
            parts.append(jnp.concatenate([high, low], axis=1))
        products[at, :] = jnp.concatenate(parts, axis=0)
        return carry

    lax.fori_loop(0, BOX // GROUP, correlate, 0, unroll=True)
    corr = jnp.dot(phases[...], products[...], preferred_element_type=F32)
    half = SHIFTS * SHIFTS
    corr = corr[:half, :POSES] + (corr[half:, :POSES] + corr[:half, 128 : 128 + POSES])
    score = corr * (precision_ref[0] / BOX)
    top = jnp.max(score, axis=(0, 1), keepdims=True)
    terms = jnp.exp(score - top)
    total = jnp.sum(terms, axis=(0, 1), keepdims=True)
    posterior = terms / total
    loglik_ref[0] = ((top + jnp.log(total)) * alive)[0, 0]
    posterior_t = posterior.T
    mass = jnp.sum(posterior_t, axis=1, keepdims=True)

    ring8 = (4, 3, 5, 2, 6, 1, 7)
    ring4 = (2, 1, 3)
    pairs = []

    def spread_half(first_slot, c):
        return jnp.dot(
            spread[first_slot : first_slot + KEEP, :],
            rows[:, c * BOX : (c + 1) * BOX],
            preferred_element_type=F32,
        )

    def send_pair(c, total):
        pair_out[c] = total.astype(BF16)
        copy = remote(pair_out.at[c], pair_in.at[c], pair_send.at[c], pair_recv.at[c], sibling)
        copy.start()
        pairs.append(copy)

    part = NY * NZ
    a_pairs = {}

    def send_pair_blocks(c, total):
        pair_out[c] = total.astype(BF16)
        for n, k in enumerate(ring4 + (0,)):
            block = pl.ds(k * part, part)
            copy = remote(
                pair_out.at[c, block],
                pair_in.at[c, block],
                pair_send.at[3 + n],
                pair_recv.at[3 + n],
                sibling,
            )
            copy.start()
            pairs.append(copy)
            a_pairs[k] = copy

    def spread_own(c):
        sums[c] = spread_half(0, c)

    def spread_mass(first_slot):
        total = spread_square[0, first_slot : first_slot + KEEP, :] * mass[0:1, :]
        for p in range(1, POSES):
            total = total + spread_square[p, first_slot : first_slot + KEEP, :] * mass[p : p + 1, :]
        return total

    def turn_poses():
        high = posterior_t.astype(BF16)
        low = (posterior_t - high.astype(F32)).astype(BF16)
        parts = jnp.concatenate(
            [
                jnp.concatenate([high, high], axis=1),
                jnp.concatenate([low, jnp.zeros_like(low)], axis=1),
            ],
            axis=0,
        )
        both_parts = jnp.dot(parts, phases[...], preferred_element_type=F32)
        turned[...] = (both_parts[:POSES] + both_parts[POSES:]).astype(BF16)

    def insert(g, carry):
        at = pl.ds(pl.multiple_of(g * WIDE, WIDE), WIDE)
        turns_g = turned[:, at]
        weight = jnp.concatenate(
            [
                diagonal(
                    k,
                    jnp.where(
                        lane_row == k % (GROUP // 2),
                        turns_g[:, k // (GROUP // 2) * 128 : k // (GROUP // 2) * 128 + 128],
                        nothing,
                    ),
                )
                for k in range(GROUP)
            ],
            axis=0,
        )
        rows[at, :] = jnp.dot(
            weight, shifted[at, :], preferred_element_type=F32
        ).astype(BF16)
        return carry

    hops = []

    def hop(number, src, dst, device):
        copy = remote(src, dst, hop_send.at[number], hop_recv.at[number], device)
        copy.start()
        hops.append(copy)
        return copy


    send_pair(2, spread_mass(KEEP))
    sums[2] = spread_mass(0)
    turn_poses()
    lax.fori_loop(0, BOX // GROUP, insert, 0, unroll=True)
    pairs[0].wait_recv()
    c_sum = sums[2] + pair_in[2].astype(F32)
    for half in range(2):
        strided[half] = c_sum[:, half * 128 : (half + 1) * 128]

    def c_rows(k):
        rows_k = pl.ds(k, NX * NY, NZ)
        return jnp.concatenate([strided[0, rows_k, :], strided[1, rows_k, :]], axis=1)

    c_hops = []
    for k in ring8:
        cz_out[k] = c_rows(k).astype(BF16)
        c_hops.append(hop(k, cz_out.at[k], cz_in.at[k], along_z(k)))
    send_pair(0, spread_half(KEEP, 0))
    send_pair_blocks(1, spread_half(KEEP, 1))
    spread_own(0)
    spread_own(1)

    pairs[1].wait_recv()
    b_sum = (sums[0] + pair_in[0].astype(F32)).reshape(NX, NY, NZ, BOX)
    b_hops = []
    for k in ring8:
        by_out[k] = b_sum[:, k].reshape(NX * NZ, BOX).astype(BF16)
        b_hops.append(hop(NZ + k, by_out.at[k], by_in.at[k], along_y(k)))
    b_sum = b_sum[:, 0].reshape(NX * NZ, BOX)
    def a_block(k):
        a_pairs[k].wait_recv()
        block = pl.ds(k * part, part)
        return sums[1, block, :] + pair_in[1, block, :].astype(F32)

    a_hops = []
    for k in ring4:
        ax_out[k] = a_block(k).astype(BF16)
        a_hops.append(hop(2 * NZ + k, ax_out.at[k], ax_in.at[k], along_x(k)))
    a_sum = a_block(0)

    pl.semaphore_wait(ready, NX - 1)
    left(held.at[core, y_lo, pl.ds(0, NZ - 1)], 0)
    left(held.at[core, pl.ds(0, 3)], 1)
    left(held.at[core], 2)
    for copy in pairs + hops:
        copy.wait_send()

    def last(rows_out, rows_in, total, number, size, owner):
        count = total.shape[0]
        rows_out[...] = total.reshape(count, 1, BOX)

        def hops_to(n):
            far_step, near_step = divmod(n, 8)
            return min(far_step, size - far_step) + min(near_step, 8 - near_step)

        for n in sorted(range(1, count), key=hops_to, reverse=True):
            remote(
                rows_out.at[n], rows_in.at[n], last_send.at[number], last_recv.at[number], owner(n)
            ).start()

    def collect(rows_in, total, number):
        arrived = rows_in.at[pl.ds(1, total.shape[0] - 1)]
        pltpu.make_async_copy(arrived, arrived, last_recv.at[number]).wait()
        return total[0:1, :] + jnp.sum(rows_in[1:], axis=0)

    def drain(rows_out, number):
        gone = rows_out.at[pl.ds(1, rows_out.shape[0] - 1)]
        pltpu.make_async_copy(gone, gone, last_send.at[number]).wait()

    c_sum = c_rows(0)
    for k, copy in zip(ring8, c_hops):
        copy.wait_recv()
        c_sum = c_sum + cz_in[k].astype(F32)
    last(
        c_last_out,
        c_last_in,
        c_sum,
        2,
        NX,
        lambda n: device_at(z, (y + n % NY) % NY, (x + n // NY) % NX, core),
    )
    for k, copy in zip(ring4, a_hops):
        copy.wait_recv()
        a_sum = a_sum + ax_in[k].astype(F32)
    last(
        a_last_out,
        a_last_in,
        a_sum,
        1,
        NY,
        lambda n: device_at((z + n % NZ) % NZ, (y + n // NZ) % NY, x, core),
    )
    for k, copy in zip(ring8, b_hops):
        copy.wait_recv()
        b_sum = b_sum + by_in[k].astype(F32)
    last(
        b_last_out,
        b_last_in,
        b_sum,
        0,
        NX,
        lambda n: device_at((z + n % NZ) % NZ, y, (x + n // NZ) % NX, core),
    )
    out_ref[:, 2 * BOX :] = collect(c_last_in, c_sum, 2)
    out_ref[:, BOX : 2 * BOX] = collect(a_last_in, a_sum, 1)
    out_ref[:, :BOX] = collect(b_last_in, b_sum, 0)
    drain(c_last_out, 2)
    drain(a_last_out, 1)
    drain(b_last_out, 0)


def expect(*operands):
    smem = pl.BlockSpec(memory_space=pltpu.SMEM)
    vmem = pl.BlockSpec(memory_space=pltpu.VMEM)
    dma = pltpu.SemaphoreType.DMA
    hop_count = 2 * NZ + NX

    def both_ways(shape, kind):
        return [pltpu.VMEM(shape, kind), pltpu.VMEM(shape, kind)]

    return pl.pallas_call(
        expect_kernel,
        out_shape=(
            jax.ShapeDtypeStruct((1, 3 * BOX), F32),
            jax.ShapeDtypeStruct((1,), F32),
        ),
        in_specs=[pl.BlockSpec(memory_space=pltpu.HBM)] * 10,
        out_specs=(vmem, smem),
        scratch_shapes=[
            pltpu.SMEM(operand.shape, operand.dtype) for operand in operands[:6]
        ]
        + [pltpu.VMEM(operand.shape, operand.dtype) for operand in operands[6:]]
        + [dma((10,))]
        + [
            pltpu.VMEM((2, Y_LO, NZ, 16, BOX), BF16),
            pltpu.VMEM((2, GROUP, ROWS), I16),
            pltpu.VMEM((4, GROUP, ROWS), BF16),
            pltpu.VMEM((2 * BOX, 2 * LINES), BF16),
            pltpu.VMEM((2 * LINES, ROWS), BF16),
            pltpu.VMEM((2 * BOX, ROWS), BF16),
            pltpu.VMEM((ROWS, 2 * BOX), BF16),
            pltpu.VMEM((2 * SHIFTS * SHIFTS, ROWS), BF16),
            pltpu.VMEM((BOX, BOX), BF16),
            pltpu.VMEM((ROWS, WIDE), BF16),
            pltpu.VMEM((POSES, ROWS), BF16),
            pltpu.VMEM((ROWS, 2 * BOX), BF16),
            pltpu.VMEM((2, POSES * GROUP, BOX), I16),
            pltpu.VMEM((2, POSES * GROUP, BOX), BF16),
            pltpu.VMEM((POSES, LINES, BOX), F32),
            pltpu.VMEM((3, KEEP, BOX), F32),
            pltpu.VMEM((2, KEEP, BOX // 2), F32),
        ]
        + both_ways((3, KEEP, BOX), BF16)
        + both_ways((NX, NY * NZ, BOX), BF16)
        + both_ways((NY, NX * NZ, BOX), BF16)
        + both_ways((NZ, NX * NY, BOX), BF16)
        + both_ways((NY * NZ, 1, BOX), F32)
        + both_ways((NX * NZ, 1, BOX), F32)
        + both_ways((NX * NY, 1, BOX), F32)
        + [
            dma((3,)),
            dma((12,)),
            dma((7,)),
            dma((7,)),
            dma((hop_count,)),
            dma((hop_count,)),
            dma((3,)),
            dma((3,)),
            pltpu.SemaphoreType.REGULAR,
        ],
        compiler_params=pltpu.CompilerParams(
            collective_id=0, has_side_effects=True, vmem_limit_bytes=60 * 1024 * 1024
        ),
    )(*operands)


def body(
    particles,
    defocus_class,
    noise_precision,
    live_count,
    defocus,
    reference_lines,
    line_index,
    line_weight,
    row_shifts,
    column_shifts,
):
    index = jnp.transpose(line_index, (0, 2, 1))
    weight = jnp.transpose(line_weight, (0, 2, 1))
    particle_total = particles.shape[0] * lax.axis_size("slab") * lax.axis_size("grp")
    owned, loglik = expect(
        defocus_class,
        noise_precision,
        live_count,
        defocus,
        row_shifts,
        column_shifts,
        particles,
        index,
        weight,
        reference_lines,
    )
    return owned.reshape(1, 3, BOX) * (LINES / (POSES * particle_total)), loglik


def solution(mesh):
    return jax.shard_map(
        body,
        mesh=mesh,
        in_specs=(
            P(("slab", "grp"), None, None, None),
            P(("slab", "grp")),
            P(("slab", "grp")),
            P("grp"),
            P(),
            P("slab", None, None),
            P(),
            P(),
            P(),
            P(),
        ),
        out_specs=(P(("slab", "grp"), None, None), P(("slab", "grp"))),
        check_vma=False,
    )
```

```python
import math

import jax
import jax.numpy as jnp
from jax import lax
from jax.experimental import pallas as pl
from jax.experimental.pallas import tpu as pltpu
from jax.sharding import PartitionSpec as P

MESH = pl.DeviceIdType.MESH
EXACT = lax.Precision.HIGHEST
F32 = jnp.float32
BF16 = jnp.bfloat16
I32 = jnp.int32
I16 = jnp.int16

NX, NY, NZ, Y_LO = 4, 8, 8, 4
SLABS = NZ * Y_LO
LINES = 512
KEEP = LINES // 2
BOX = 256
POSES = 16
GROUP = 16
WIDE = GROUP * POSES
ROWS = POSES * BOX
SHIFTS = 8


def place():
    slab = lax.axis_index("slab")
    grp = lax.axis_index("grp")
    z, y_lo = slab // Y_LO, slab % Y_LO
    y_hi, x, core = grp // (2 * NX), (grp // 2) % NX, grp % 2
    return z, y_hi * Y_LO + y_lo, x, core


def device_at(z, y, x, core):
    return (z * Y_LO + y % Y_LO, (y // Y_LO) * (2 * NX) + x * 2 + core)


def phase_angle(turns):
    signed = ((turns + BOX // 2) & (BOX - 1)) - BOX // 2
    return signed.astype(F32) * (2.0 * math.pi / BOX)


def shift_column(shifts_ref, shape):
    row = lax.broadcasted_iota(I32, shape, 0)
    column = jnp.zeros(shape, I32)
    for t in range(SHIFTS):
        column = jnp.where(row == t, shifts_ref[t], column)
    return column


def slot_of(line, z, y, x, core):
    line_y = ((line >> 3) & 1) * Y_LO + ((line >> 4) & (Y_LO - 1))
    return (
        ((line ^ core) & 1) * KEEP
        + ((((line >> 1) - x) & (NX - 1)) * (NY * NZ))
        + (((line_y - y) & (NY - 1)) * NZ)
        + (((line >> 6) - z) & (NZ - 1))
    )


def held_row(slot, z, y, x, core):
    line_z = (slot + z) & (NZ - 1)
    line_y = ((slot >> 3) + y) & (NY - 1)
    line_x = ((slot >> 6) + x) & (NX - 1)
    line_core = ((slot >> 8) ^ core) & 1
    return (line_y & 3) * (NZ * 16) + line_z * 16 + (line_y >> 2) * 8 + line_x * 2 + line_core


def expect_kernel(
    class_hbm,
    precision_hbm,
    live_hbm,
    defocus_hbm,
    row_shift_hbm,
    column_shift_hbm,
    image_hbm,
    index_hbm,
    weight_hbm,
    lines_hbm,
    out_ref,
    loglik_ref,
    class_ref,
    precision_ref,
    live_ref,
    defocus_ref,
    row_shift_ref,
    column_shift_ref,
    image_ref,
    index_ref,
    weight_ref,
    lines_ref,
    load_sem,
    held,
    slots,
    weights,
    lines_t,
    spread,
    slices,
    shifted,
    phases,
    squares,
    products,
    turned,
    rows,
    pose_slots,
    pose_weights,
    spread_square,
    sums,
    strided,
    pair_out,
    pair_in,
    ax_out,
    ax_in,
    by_out,
    by_in,
    cz_out,
    cz_in,
    a_last_out,
    a_last_in,
    b_last_out,
    b_last_in,
    c_last_out,
    c_last_in,
    gather_send,
    gather_recv,
    pair_send,
    pair_recv,
    hop_send,
    hop_recv,
    last_send,
    last_recv,
    ready,
):
    z, y, x, core = place()
    y_lo = y % Y_LO
    sibling = device_at(z, y, x, 1 - core)

    def along_x(k):
        return device_at(z, y, (x + k) % NX, core)

    def along_y(k):
        return device_at(z, (y + NY + k) % NY, x, core)

    def along_z(k):
        return device_at((z + k) % NZ, y, x, core)

    def remote(src, dst, send, recv, device):
        return pltpu.make_async_remote_copy(
            src_ref=src,
            dst_ref=dst,
            send_sem=send,
            recv_sem=recv,
            device_id=device,
            device_id_type=MESH,
        )

    barrier = pltpu.get_barrier_semaphore()
    peers = [sibling]
    peers += [along_x(k) for k in range(1, NX)]
    peers += [along_y(k) for k in range(1, NY)]
    peers += [along_z(k) for k in range(1, NZ)]
    for peer in peers:
        pl.semaphore_signal(barrier, inc=1, device_id=peer, device_id_type=MESH)

    loads = [
        pltpu.make_async_copy(src, dst, load_sem.at[n])
        for n, (src, dst) in enumerate(
            [
                (lines_hbm, lines_ref),
                (class_hbm, class_ref),
                (live_hbm, live_ref),
                (defocus_hbm, defocus_ref),
                (column_shift_hbm, column_shift_ref),
                (row_shift_hbm, row_shift_ref),
                (image_hbm, image_ref),
                (index_hbm, index_ref),
                (weight_hbm, weight_ref),
                (precision_hbm, precision_ref),
            ]
        )
    ]
    for load in loads:
        load.start()

    loads[0].wait()
    both = lines_ref[...]
    held[core, y_lo, z] = jnp.where(core == 0, both[:, 0, :], both[:, 1, :])

    pl.semaphore_wait(barrier, len(peers))
    for k in range(1, NX):
        pl.semaphore_signal(ready, inc=1, device_id=along_x(k), device_id_type=MESH)

    def send_block(src, send, recv, device):
        copy = remote(src, src, gather_send.at[send], gather_recv.at[recv], device)
        copy.start()
        return copy

    def landed(blocks, number):
        pltpu.make_async_copy(blocks, blocks, gather_recv.at[number]).wait()

    def left(blocks, number):
        pltpu.make_async_copy(blocks, blocks, gather_send.at[number]).wait()

    groups = ((0, 1, 7), (2, 6), (3, 5, 4))
    near_z = {
        k: send_block(held.at[core, y_lo, z], 0, k, along_z(k)) for k in (4, 3, 5, 2, 6, 1, 7)
    }
    far = 2 - 4 * core
    steps = {1: 1, 2: far, 3: -1}

    def pass_along_y(k):
        block = held.at[core, y_lo, (z + NZ - k) % NZ]
        group = [k in members for members in groups].index(True)
        for d in (2, 1, 3):
            send_block(block, 1, NZ + group, along_y(steps[d]))
        send_block(block, 2, 11, sibling)

    def pass_on(*distances):
        for k in distances:
            near_z[k].wait_recv()
            pass_along_y(k)

    def swap(group):
        landed(held.at[core, pl.ds(0, 3), pl.ds(0, len(groups[group]))], NZ + group)
        for k in groups[group]:
            for residue in (y_lo + 3, y_lo + 1, y_lo + 2):
                send_block(held.at[core, residue % Y_LO, (z + NZ - k) % NZ], 2, 11, sibling)

    pass_along_y(0)
    for load in loads[1:]:
        load.wait()
    alive = jnp.where(0 < live_ref[0], 1.0, 0.0).astype(F32)
    chosen = defocus_ref[class_ref[0]]

    lane_y = lax.broadcasted_iota(I32, (SHIFTS, BOX), 1) - BOX // 2
    angle_y = phase_angle(lane_y * shift_column(column_shift_ref, (SHIFTS, BOX)))
    cos_y = jnp.cos(angle_y)
    sin_y = jnp.sin(angle_y)
    freq_y = (lax.broadcasted_iota(I32, (GROUP, BOX), 1) - BOX // 2).astype(F32) / BOX
    row_in_group = lax.broadcasted_iota(I32, (GROUP, BOX), 0)

    def shift_rows(g, carry):
        at = pl.ds(pl.multiple_of(g * WIDE, WIDE), WIDE)
        kx = pl.ds(pl.multiple_of(g * GROUP, GROUP), GROUP)
        freq_x = (row_in_group + (g * GROUP - BOX // 2)).astype(F32) / BOX
        ctf = -jnp.sin(chosen * (freq_x * freq_x + freq_y * freq_y) + 0.1) * alive
        squares[kx, :] = (ctf * ctf).astype(BF16)
        real = ctf * image_ref[0, 0, kx, :].astype(F32)
        imag = ctf * image_ref[0, 1, kx, :].astype(F32)
        blocks = []
        for k in range(GROUP):
            real_row = real[k : k + 1, :]
            imag_row = imag[k : k + 1, :]
            shift_re = real_row * cos_y + imag_row * sin_y
            shift_im = real_row * sin_y - imag_row * cos_y
            blocks.append(jnp.concatenate([shift_re, -shift_im], axis=1))
            blocks.append(jnp.concatenate([shift_im, shift_re], axis=1))
        shifted[at, :] = jnp.concatenate(blocks, axis=0).astype(BF16)
        return carry

    lane = lax.broadcasted_iota(I32, (SHIFTS, ROWS), 1)
    freq = (lane >> 4) - BOX // 2
    part = (lane >> 3) & 1
    turns = freq * shift_column(row_shift_ref, (SHIFTS, ROWS)) + part * (BOX // 4)
    row_phase = jnp.cos(phase_angle(turns))
    row_high = row_phase.astype(BF16).astype(F32)
    row_low = row_phase - row_high
    for t in range(0, SHIFTS, 2):
        for base, table in ((0, row_high), (SHIFTS * SHIFTS, row_low)):
            phases[pl.ds(base + t * SHIFTS, 2 * SHIFTS), :] = jnp.concatenate(
                [jnp.where((lane & 7) == t + u, table, 0.0) for u in range(2)], axis=0
            ).astype(BF16)

    first = slot_of(index_ref[:, 0, :], z, y, x, core)
    second = slot_of(index_ref[:, 1, :], z, y, x, core)
    first_weight = weight_ref[:, 0, :]
    second_weight = weight_ref[:, 1, :]
    same = first == second
    first_weight = jnp.where(same, first_weight + second_weight, first_weight)
    second_weight = jnp.where(same, 0.0, second_weight)
    first_high = first_weight.astype(BF16).astype(F32)
    second_high = second_weight.astype(BF16).astype(F32)
    tables = jnp.concatenate(
        [
            (first >> 4).astype(F32),
            (first & 15).astype(F32),
            (second >> 4).astype(F32),
            (second & 15).astype(F32),
            first_high,
            second_high,
            first_weight - first_high,
            second_weight - second_high,
        ],
        axis=0,
    ).astype(BF16)
    table_step = (
        lax.broadcasted_iota(I32, (BOX, WIDE), 0)
        - (lax.broadcasted_iota(I32, (BOX, WIDE), 1) >> 4)
    ).astype(I16)
    one = jnp.ones((BOX, WIDE), BF16)
    pose_row = lax.broadcasted_iota(I32, (POSES, WIDE), 0) == (
        lax.broadcasted_iota(I32, (POSES, WIDE), 1) & (POSES - 1)
    )

    def table_rows(g, carry):
        at = pl.ds(pl.multiple_of(g * WIDE, WIDE), WIDE)
        first_row = jnp.full((BOX, WIDE), g * GROUP, I32).astype(I16)
        chosen_row = jnp.where(table_step == first_row, one, jnp.zeros_like(one))
        wide = jnp.dot(tables, chosen_row, preferred_element_type=F32)
        found = [
            jnp.sum(
                jnp.where(pose_row, wide[n * POSES : (n + 1) * POSES, :], 0.0),
                axis=0,
                keepdims=True,
            )
            for n in range(8)
        ]
        for n in range(2):
            slot = (found[2 * n] * 16.0 + found[2 * n + 1]).astype(I32)
            slots[n, :, at] = jnp.broadcast_to(slot, (GROUP, WIDE)).astype(I16)
        for n in range(4):
            weights[n, :, at] = jnp.broadcast_to(found[4 + n], (GROUP, WIDE)).astype(BF16)
        return carry

    lax.fori_loop(0, BOX // GROUP, table_rows, 0, unroll=8)
    pass_on(1, 7)
    slot_row = lax.broadcasted_iota(I32, (GROUP, WIDE), 0).astype(I16)

    def spread_rows(g, carry):
        at = pl.ds(pl.multiple_of(g * WIDE, WIDE), WIDE)
        first_slot, second_slot = slots[0, :, at], slots[1, :, at]
        parts = [weights[n, :, at] for n in range(4)]
        for block in range(LINES // GROUP):
            row = slot_row + jnp.int16(block * GROUP)
            is_first = first_slot == row
            is_second = second_slot == row
            for n, base in ((0, 0), (2, LINES)):
                rest = jnp.where(is_second, parts[n + 1], jnp.zeros_like(parts[n]))
                spread[base + block * GROUP : base + (block + 1) * GROUP, at] = jnp.where(
                    is_first, parts[n], rest
                )
        return carry

    lax.fori_loop(0, BOX // GROUP, spread_rows, 0)
    pass_on(2, 6)

    slot_rows = lax.broadcasted_iota(I32, (GROUP, BOX), 0).astype(I16)
    for n, table, target, kind in (
        (0, first, pose_slots, I16),
        (1, second, pose_slots, I16),
        (0, first_high, pose_weights, BF16),
        (1, second_high, pose_weights, BF16),
    ):
        for p in range(POSES):
            target[n, p * GROUP : (p + 1) * GROUP, :] = jnp.broadcast_to(
                table[p : p + 1, :], (GROUP, BOX)
            ).astype(kind)

    def spread_squares(p, carry):
        rows_p = pl.ds(pl.multiple_of(p * GROUP, GROUP), GROUP)
        first_slot, second_slot = pose_slots[0, rows_p, :], pose_slots[1, rows_p, :]
        first_part, second_part = pose_weights[0, rows_p, :], pose_weights[1, rows_p, :]
        blocks = []
        for block in range(LINES // GROUP):
            row = slot_rows + jnp.int16(block * GROUP)
            rest = jnp.where(second_slot == row, second_part, jnp.zeros_like(second_part))
            blocks.append(jnp.where(first_slot == row, first_part, rest))
        spread_square[p] = jnp.dot(
            jnp.concatenate(blocks, axis=0), squares[...], preferred_element_type=F32
        )
        return carry

    pass_on(3, 5, 4)
    lax.fori_loop(0, 8, shift_rows, 0)
    swap(0)
    lax.fori_loop(8, BOX // GROUP, shift_rows, 0)
    swap(1)
    lax.fori_loop(0, POSES, spread_squares, 0, unroll=8)
    swap(2)

    slot_lines = held_row(lax.broadcasted_iota(I32, (1, LINES), 1), z, y, x, core)
    order = jnp.where(
        lax.broadcasted_iota(I32, (LINES, LINES), 0) == slot_lines, 1.0, 0.0
    ).astype(BF16)

    def transpose_half(c):
        half = lax.dot_general(
            held[c].reshape(LINES, BOX),
            order,
            (((0,), (0,)), ((), ())),
            preferred_element_type=F32,
        ).astype(BF16)
        lines_t[pl.ds(pl.multiple_of(c * BOX, BOX), BOX), :] = jnp.concatenate(
            [half, half], axis=1
        )

    def slice_half(c):
        half = pl.ds(pl.multiple_of(c * BOX, BOX), BOX)

        def step(n, carry):
            at = pl.ds(pl.multiple_of(n * 4 * WIDE, 4 * WIDE), 4 * WIDE)
            slices[half, at] = jnp.dot(
                lines_t[half, :], spread[:, at], preferred_element_type=F32
            ).astype(BF16)
            return carry

        lax.fori_loop(0, ROWS // (4 * WIDE), step, 0, unroll=True)

    transpose_half(core)
    slice_half(core)
    landed(held.at[1 - core], 11)
    transpose_half(1 - core)
    slice_half(1 - core)

    lane_row = lax.broadcasted_iota(I32, (GROUP, 128), 1) >> 4
    nothing = jnp.zeros((GROUP, 128), BF16)

    def diagonal(k, tile):
        return jnp.concatenate([tile, nothing] if k < GROUP // 2 else [nothing, tile], axis=1)

    lane_pose = lax.broadcasted_iota(I32, (GROUP, 128), 1) < POSES

    def correlate(g, carry):
        at = pl.ds(pl.multiple_of(g * WIDE, WIDE), WIDE)
        found = jnp.dot(shifted[at, :], slices[:, at], preferred_element_type=F32)
        parts = []
        for k in range(GROUP):
            lane_at = k // (GROUP // 2) * 128
            block = found[k * GROUP : (k + 1) * GROUP, lane_at : lane_at + 128]
            if k % (GROUP // 2):
                block = pltpu.roll(block, 128 - k % (GROUP // 2) * POSES, 1)
            block = jnp.where(lane_pose, block, 0.0)
            high = block.astype(BF16)
            low = (block - high.astype(F32)).astype(BF16)
            parts.append(jnp.concatenate([high, low], axis=1))
        products[at, :] = jnp.concatenate(parts, axis=0)
        return carry

    lax.fori_loop(0, BOX // GROUP, correlate, 0, unroll=True)
    corr = jnp.dot(phases[...], products[...], preferred_element_type=F32)
    half = SHIFTS * SHIFTS
    corr = corr[:half, :POSES] + (corr[half:, :POSES] + corr[:half, 128 : 128 + POSES])
    score = corr * (precision_ref[0] / BOX)
    top = jnp.max(score, axis=(0, 1), keepdims=True)
    terms = jnp.exp(score - top)
    total = jnp.sum(terms, axis=(0, 1), keepdims=True)
    posterior = terms / total
    loglik_ref[0] = ((top + jnp.log(total)) * alive)[0, 0]
    posterior_t = posterior.T
    mass = jnp.sum(posterior_t, axis=1, keepdims=True)

    ring8 = (4, 3, 5, 2, 6, 1, 7)
    ring4 = (2, 1, 3)
    pairs = []

    def spread_half(first_slot, c):
        return jnp.dot(
            spread[first_slot : first_slot + KEEP, :],
            rows[:, c * BOX : (c + 1) * BOX],
            preferred_element_type=F32,
        )

    def send_pair(c, total):
        pair_out[c] = total.astype(BF16)
        copy = remote(pair_out.at[c], pair_in.at[c], pair_send.at[c], pair_recv.at[c], sibling)
        copy.start()
        pairs.append(copy)

    part = NY * NZ
    a_pairs = {}

    def send_pair_blocks(c, total):
        pair_out[c] = total.astype(BF16)
        for n, k in enumerate(ring4 + (0,)):
            block = pl.ds(k * part, part)
            copy = remote(
                pair_out.at[c, block],
                pair_in.at[c, block],
                pair_send.at[3 + n],
                pair_recv.at[3 + n],
                sibling,
            )
            copy.start()
            pairs.append(copy)
            a_pairs[k] = copy

    def spread_own(c):
        sums[c] = spread_half(0, c)

    def spread_mass(first_slot):
        total = spread_square[0, first_slot : first_slot + KEEP, :] * mass[0:1, :]
        for p in range(1, POSES):
            total = total + spread_square[p, first_slot : first_slot + KEEP, :] * mass[p : p + 1, :]
        return total

    def turn_poses():
        high = posterior_t.astype(BF16)
        low = (posterior_t - high.astype(F32)).astype(BF16)
        parts = jnp.concatenate(
            [
                jnp.concatenate([high, high], axis=1),
                jnp.concatenate([low, jnp.zeros_like(low)], axis=1),
            ],
            axis=0,
        )
        both_parts = jnp.dot(parts, phases[...], preferred_element_type=F32)
        turned[...] = (both_parts[:POSES] + both_parts[POSES:]).astype(BF16)

    def insert(c):
        columns = slice(c * BOX, (c + 1) * BOX)

        def step(g, carry):
            at = pl.ds(pl.multiple_of(g * WIDE, WIDE), WIDE)
            turns_g = turned[:, at]
            weight = jnp.concatenate(
                [
                    diagonal(
                        k,
                        jnp.where(
                            lane_row == k % (GROUP // 2),
                            turns_g[:, k // (GROUP // 2) * 128 : k // (GROUP // 2) * 128 + 128],
                            nothing,
                        ),
                    )
                    for k in range(GROUP)
                ],
                axis=0,
            )
            rows[at, columns] = jnp.dot(
                weight, shifted[at, columns], preferred_element_type=F32
            ).astype(BF16)
            return carry

        lax.fori_loop(0, BOX // GROUP, step, 0, unroll=True)

    hops = []

    def hop(number, src, dst, device):
        copy = remote(src, dst, hop_send.at[number], hop_recv.at[number], device)
        copy.start()
        hops.append(copy)
        return copy


    send_pair(2, spread_mass(KEEP))
    turn_poses()
    insert(0)
    send_pair(0, spread_half(KEEP, 0))
    sums[2] = spread_mass(0)
    insert(1)
    pairs[0].wait_recv()
    c_sum = sums[2] + pair_in[2].astype(F32)
    for half in range(2):
        strided[half] = c_sum[:, half * 128 : (half + 1) * 128]

    def c_rows(k):
        rows_k = pl.ds(k, NX * NY, NZ)
        return jnp.concatenate([strided[0, rows_k, :], strided[1, rows_k, :]], axis=1)

    c_hops = []
    for k in ring8:
        cz_out[k] = c_rows(k).astype(BF16)
        c_hops.append(hop(k, cz_out.at[k], cz_in.at[k], along_z(k)))
    send_pair_blocks(1, spread_half(KEEP, 1))
    spread_own(0)

    pairs[1].wait_recv()
    b_sum = (sums[0] + pair_in[0].astype(F32)).reshape(NX, NY, NZ, BOX)
    b_hops = []
    for k in ring8:
        by_out[k] = b_sum[:, k].reshape(NX * NZ, BOX).astype(BF16)
        b_hops.append(hop(NZ + k, by_out.at[k], by_in.at[k], along_y(k)))
    b_sum = b_sum[:, 0].reshape(NX * NZ, BOX)

    spread_own(1)

    def a_block(k):
        a_pairs[k].wait_recv()
        block = pl.ds(k * part, part)
        return sums[1, block, :] + pair_in[1, block, :].astype(F32)

    a_hops = []
    for k in ring4:
        ax_out[k] = a_block(k).astype(BF16)
        a_hops.append(hop(2 * NZ + k, ax_out.at[k], ax_in.at[k], along_x(k)))
    a_sum = a_block(0)

    pl.semaphore_wait(ready, NX - 1)
    left(held.at[core, y_lo, pl.ds(0, NZ - 1)], 0)
    left(held.at[core, pl.ds(0, 3)], 1)
    left(held.at[core], 2)
    for copy in pairs + hops:
        copy.wait_send()

    def last(rows_out, rows_in, total, number, size, owner):
        count = total.shape[0]
        rows_out[...] = total.reshape(count, 1, BOX)

        def hops_to(n):
            far_step, near_step = divmod(n, 8)
            return min(far_step, size - far_step) + min(near_step, 8 - near_step)

        for n in sorted(range(1, count), key=hops_to, reverse=True):
            remote(
                rows_out.at[n], rows_in.at[n], last_send.at[number], last_recv.at[number], owner(n)
            ).start()

    def collect(rows_in, total, number):
        arrived = rows_in.at[pl.ds(1, total.shape[0] - 1)]
        pltpu.make_async_copy(arrived, arrived, last_recv.at[number]).wait()
        return total[0:1, :] + jnp.sum(rows_in[1:], axis=0)

    def drain(rows_out, number):
        gone = rows_out.at[pl.ds(1, rows_out.shape[0] - 1)]
        pltpu.make_async_copy(gone, gone, last_send.at[number]).wait()

    c_sum = c_rows(0)
    for k, copy in zip(ring8, c_hops):
        copy.wait_recv()
        c_sum = c_sum + cz_in[k].astype(F32)
    last(
        c_last_out,
        c_last_in,
        c_sum,
        2,
        NX,
        lambda n: device_at(z, (y + n % NY) % NY, (x + n // NY) % NX, core),
    )
    for k, copy in zip(ring4, a_hops):
        copy.wait_recv()
        a_sum = a_sum + ax_in[k].astype(F32)
    last(
        a_last_out,
        a_last_in,
        a_sum,
        1,
        NY,
        lambda n: device_at((z + n % NZ) % NZ, (y + n // NZ) % NY, x, core),
    )
    for k, copy in zip(ring8, b_hops):
        copy.wait_recv()
        b_sum = b_sum + by_in[k].astype(F32)
    last(
        b_last_out,
        b_last_in,
        b_sum,
        0,
        NX,
        lambda n: device_at((z + n % NZ) % NZ, y, (x + n // NZ) % NX, core),
    )
    out_ref[:, 2 * BOX :] = collect(c_last_in, c_sum, 2)
    out_ref[:, BOX : 2 * BOX] = collect(a_last_in, a_sum, 1)
    out_ref[:, :BOX] = collect(b_last_in, b_sum, 0)
    drain(c_last_out, 2)
    drain(a_last_out, 1)
    drain(b_last_out, 0)


def expect(*operands):
    smem = pl.BlockSpec(memory_space=pltpu.SMEM)
    vmem = pl.BlockSpec(memory_space=pltpu.VMEM)
    dma = pltpu.SemaphoreType.DMA
    hop_count = 2 * NZ + NX

    def both_ways(shape, kind):
        return [pltpu.VMEM(shape, kind), pltpu.VMEM(shape, kind)]

    return pl.pallas_call(
        expect_kernel,
        out_shape=(
            jax.ShapeDtypeStruct((1, 3 * BOX), F32),
            jax.ShapeDtypeStruct((1,), F32),
        ),
        in_specs=[pl.BlockSpec(memory_space=pltpu.HBM)] * 10,
        out_specs=(vmem, smem),
        scratch_shapes=[
            pltpu.SMEM(operand.shape, operand.dtype) for operand in operands[:6]
        ]
        + [pltpu.VMEM(operand.shape, operand.dtype) for operand in operands[6:]]
        + [dma((10,))]
        + [
            pltpu.VMEM((2, Y_LO, NZ, 16, BOX), BF16),
            pltpu.VMEM((2, GROUP, ROWS), I16),
            pltpu.VMEM((4, GROUP, ROWS), BF16),
            pltpu.VMEM((2 * BOX, 2 * LINES), BF16),
            pltpu.VMEM((2 * LINES, ROWS), BF16),
            pltpu.VMEM((2 * BOX, ROWS), BF16),
            pltpu.VMEM((ROWS, 2 * BOX), BF16),
            pltpu.VMEM((2 * SHIFTS * SHIFTS, ROWS), BF16),
            pltpu.VMEM((BOX, BOX), BF16),
            pltpu.VMEM((ROWS, WIDE), BF16),
            pltpu.VMEM((POSES, ROWS), BF16),
            pltpu.VMEM((ROWS, 2 * BOX), BF16),
            pltpu.VMEM((2, POSES * GROUP, BOX), I16),
            pltpu.VMEM((2, POSES * GROUP, BOX), BF16),
            pltpu.VMEM((POSES, LINES, BOX), F32),
            pltpu.VMEM((3, KEEP, BOX), F32),
            pltpu.VMEM((2, KEEP, BOX // 2), F32),
        ]
        + both_ways((3, KEEP, BOX), BF16)
        + both_ways((NX, NY * NZ, BOX), BF16)
        + both_ways((NY, NX * NZ, BOX), BF16)
        + both_ways((NZ, NX * NY, BOX), BF16)
        + both_ways((NY * NZ, 1, BOX), F32)
        + both_ways((NX * NZ, 1, BOX), F32)
        + both_ways((NX * NY, 1, BOX), F32)
        + [
            dma((3,)),
            dma((12,)),
            dma((7,)),
            dma((7,)),
            dma((hop_count,)),
            dma((hop_count,)),
            dma((3,)),
            dma((3,)),
            pltpu.SemaphoreType.REGULAR,
        ],
        compiler_params=pltpu.CompilerParams(
            collective_id=0, has_side_effects=True, vmem_limit_bytes=60 * 1024 * 1024
        ),
    )(*operands)


def body(
    particles,
    defocus_class,
    noise_precision,
    live_count,
    defocus,
    reference_lines,
    line_index,
    line_weight,
    row_shifts,
    column_shifts,
):
    index = jnp.transpose(line_index, (0, 2, 1))
    weight = jnp.transpose(line_weight, (0, 2, 1))
    particle_total = particles.shape[0] * lax.axis_size("slab") * lax.axis_size("grp")
    owned, loglik = expect(
        defocus_class,
        noise_precision,
        live_count,
        defocus,
        row_shifts,
        column_shifts,
        particles,
        index,
        weight,
        reference_lines,
    )
    return owned.reshape(1, 3, BOX) * (LINES / (POSES * particle_total)), loglik


def solution(mesh):
    return jax.shard_map(
        body,
        mesh=mesh,
        in_specs=(
            P(("slab", "grp"), None, None, None),
            P(("slab", "grp")),
            P(("slab", "grp")),
            P("grp"),
            P(),
            P("slab", None, None),
            P(),
            P(),
            P(),
            P(),
        ),
        out_specs=(P(("slab", "grp"), None, None), P(("slab", "grp"))),
        check_vma=False,
    )
```

```python
import math

import jax
import jax.numpy as jnp
from jax import lax
from jax.experimental import pallas as pl
from jax.experimental.pallas import tpu as pltpu
from jax.sharding import PartitionSpec as P

MESH = pl.DeviceIdType.MESH
EXACT = lax.Precision.HIGHEST
F32 = jnp.float32
BF16 = jnp.bfloat16
I32 = jnp.int32
I16 = jnp.int16
F8 = jnp.float8_e4m3fn
LOW_SCALE = 512.0

NX, NY, NZ, Y_LO = 4, 8, 8, 4
SLABS = NZ * Y_LO
LINES = 512
KEEP = LINES // 2
BOX = 256
POSES = 16
GROUP = 16
WIDE = GROUP * POSES
ROWS = POSES * BOX
SHIFTS = 8


def place():
    slab = lax.axis_index("slab")
    grp = lax.axis_index("grp")
    z, y_lo = slab // Y_LO, slab % Y_LO
    y_hi, x, core = grp // (2 * NX), (grp // 2) % NX, grp % 2
    return z, y_hi * Y_LO + y_lo, x, core


def device_at(z, y, x, core):
    return (z * Y_LO + y % Y_LO, (y // Y_LO) * (2 * NX) + x * 2 + core)


def phase_angle(turns):
    signed = ((turns + BOX // 2) & (BOX - 1)) - BOX // 2
    return signed.astype(F32) * (2.0 * math.pi / BOX)


def shift_column(shifts_ref, shape):
    row = lax.broadcasted_iota(I32, shape, 0)
    column = jnp.zeros(shape, I32)
    for t in range(SHIFTS):
        column = jnp.where(row == t, shifts_ref[t], column)
    return column


def slot_of(line, z, y, x, core):
    line_y = ((line >> 3) & 1) * Y_LO + ((line >> 4) & (Y_LO - 1))
    return (
        ((line ^ core) & 1) * KEEP
        + ((((line >> 1) - x) & (NX - 1)) * (NY * NZ))
        + (((line_y - y) & (NY - 1)) * NZ)
        + (((line >> 6) - z) & (NZ - 1))
    )


def held_row(slot, z, y, x, core):
    line_z = (slot + z) & (NZ - 1)
    line_y = ((slot >> 3) + y) & (NY - 1)
    line_x = ((slot >> 6) + x) & (NX - 1)
    line_core = ((slot >> 8) ^ core) & 1
    return (line_y & 3) * (NZ * 16) + line_z * 16 + (line_y >> 2) * 8 + line_x * 2 + line_core


def expect_kernel(
    class_hbm,
    precision_hbm,
    live_hbm,
    defocus_hbm,
    row_shift_hbm,
    column_shift_hbm,
    image_hbm,
    index_hbm,
    weight_hbm,
    lines_hbm,
    out_ref,
    loglik_ref,
    class_ref,
    precision_ref,
    live_ref,
    defocus_ref,
    row_shift_ref,
    column_shift_ref,
    image_ref,
    index_ref,
    weight_ref,
    lines_ref,
    load_sem,
    held,
    slots,
    weights,
    lines_t,
    lines_low,
    spread,
    spread_low,
    slices,
    shifted,
    phases,
    squares,
    products,
    turned,
    rows,
    pose_slots,
    pose_weights,
    spread_square,
    sums,
    strided,
    pair_out,
    pair_in,
    ax_out,
    ax_in,
    by_out,
    by_in,
    cz_out,
    cz_in,
    a_last_out,
    a_last_in,
    b_last_out,
    b_last_in,
    c_last_out,
    c_last_in,
    gather_send,
    gather_recv,
    pair_send,
    pair_recv,
    hop_send,
    hop_recv,
    last_send,
    last_recv,
    ready,
):
    z, y, x, core = place()
    y_lo = y % Y_LO
    sibling = device_at(z, y, x, 1 - core)

    def along_x(k):
        return device_at(z, y, (x + k) % NX, core)

    def along_y(k):
        return device_at(z, (y + NY + k) % NY, x, core)

    def along_z(k):
        return device_at((z + k) % NZ, y, x, core)

    def remote(src, dst, send, recv, device):
        return pltpu.make_async_remote_copy(
            src_ref=src,
            dst_ref=dst,
            send_sem=send,
            recv_sem=recv,
            device_id=device,
            device_id_type=MESH,
        )

    barrier = pltpu.get_barrier_semaphore()
    peers = [sibling]
    peers += [along_x(k) for k in range(1, NX)]
    peers += [along_y(k) for k in range(1, NY)]
    peers += [along_z(k) for k in range(1, NZ)]
    for peer in peers:
        pl.semaphore_signal(barrier, inc=1, device_id=peer, device_id_type=MESH)

    loads = [
        pltpu.make_async_copy(src, dst, load_sem.at[n])
        for n, (src, dst) in enumerate(
            [
                (lines_hbm, lines_ref),
                (class_hbm, class_ref),
                (live_hbm, live_ref),
                (defocus_hbm, defocus_ref),
                (column_shift_hbm, column_shift_ref),
                (row_shift_hbm, row_shift_ref),
                (image_hbm, image_ref),
                (index_hbm, index_ref),
                (weight_hbm, weight_ref),
                (precision_hbm, precision_ref),
            ]
        )
    ]
    for load in loads:
        load.start()

    loads[0].wait()
    both = lines_ref[...]
    held[core, y_lo, z] = jnp.where(core == 0, both[:, 0, :], both[:, 1, :])

    pl.semaphore_wait(barrier, len(peers))
    for k in range(1, NX):
        pl.semaphore_signal(ready, inc=1, device_id=along_x(k), device_id_type=MESH)

    def send_block(src, send, recv, device):
        copy = remote(src, src, gather_send.at[send], gather_recv.at[recv], device)
        copy.start()
        return copy

    def landed(blocks, number):
        pltpu.make_async_copy(blocks, blocks, gather_recv.at[number]).wait()

    def left(blocks, number):
        pltpu.make_async_copy(blocks, blocks, gather_send.at[number]).wait()

    groups = ((0, 1, 7), (2, 6), (3, 5, 4))
    near_z = {
        k: send_block(held.at[core, y_lo, z], 0, k, along_z(k)) for k in (4, 3, 5, 2, 6, 1, 7)
    }
    far = 2 - 4 * core
    steps = {1: 1, 2: far, 3: -1}

    def pass_along_y(k):
        block = held.at[core, y_lo, (z + NZ - k) % NZ]
        group = [k in members for members in groups].index(True)
        for d in (2, 1, 3):
            send_block(block, 1, NZ + group, along_y(steps[d]))
        send_block(block, 2, 11, sibling)

    def pass_on(*distances):
        for k in distances:
            near_z[k].wait_recv()
            pass_along_y(k)

    def swap(group):
        landed(held.at[core, pl.ds(0, 3), pl.ds(0, len(groups[group]))], NZ + group)
        for k in groups[group]:
            for residue in (y_lo + 3, y_lo + 1, y_lo + 2):
                send_block(held.at[core, residue % Y_LO, (z + NZ - k) % NZ], 2, 11, sibling)

    pass_along_y(0)
    for load in loads[1:]:
        load.wait()
    alive = jnp.where(0 < live_ref[0], 1.0, 0.0).astype(F32)
    chosen = defocus_ref[class_ref[0]]

    lane_y = lax.broadcasted_iota(I32, (SHIFTS, BOX), 1) - BOX // 2
    angle_y = phase_angle(lane_y * shift_column(column_shift_ref, (SHIFTS, BOX)))
    cos_y = jnp.cos(angle_y)
    sin_y = jnp.sin(angle_y)
    freq_y = (lax.broadcasted_iota(I32, (GROUP, BOX), 1) - BOX // 2).astype(F32) / BOX
    row_in_group = lax.broadcasted_iota(I32, (GROUP, BOX), 0)

    def shift_rows(g, carry):
        at = pl.ds(pl.multiple_of(g * WIDE, WIDE), WIDE)
        kx = pl.ds(pl.multiple_of(g * GROUP, GROUP), GROUP)
        freq_x = (row_in_group + (g * GROUP - BOX // 2)).astype(F32) / BOX
        ctf = -jnp.sin(chosen * (freq_x * freq_x + freq_y * freq_y) + 0.1) * alive
        squares[kx, :] = (ctf * ctf).astype(BF16)
        real = ctf * image_ref[0, 0, kx, :].astype(F32)
        imag = ctf * image_ref[0, 1, kx, :].astype(F32)
        blocks = []
        for k in range(GROUP):
            real_row = real[k : k + 1, :]
            imag_row = imag[k : k + 1, :]
            shift_re = real_row * cos_y + imag_row * sin_y
            shift_im = real_row * sin_y - imag_row * cos_y
            blocks.append(jnp.concatenate([shift_re, -shift_im], axis=1))
            blocks.append(jnp.concatenate([shift_im, shift_re], axis=1))
        shifted[at, :] = jnp.concatenate(blocks, axis=0).astype(BF16)
        return carry

    lane = lax.broadcasted_iota(I32, (SHIFTS, ROWS), 1)
    freq = (lane >> 4) - BOX // 2
    part = (lane >> 3) & 1
    turns = freq * shift_column(row_shift_ref, (SHIFTS, ROWS)) + part * (BOX // 4)
    row_phase = jnp.cos(phase_angle(turns))
    row_high = row_phase.astype(BF16).astype(F32)
    row_low = row_phase - row_high
    for t in range(0, SHIFTS, 2):
        for base, table in ((0, row_high), (SHIFTS * SHIFTS, row_low)):
            phases[pl.ds(base + t * SHIFTS, 2 * SHIFTS), :] = jnp.concatenate(
                [jnp.where((lane & 7) == t + u, table, 0.0) for u in range(2)], axis=0
            ).astype(BF16)

    first = slot_of(index_ref[:, 0, :], z, y, x, core)
    second = slot_of(index_ref[:, 1, :], z, y, x, core)
    first_weight = weight_ref[:, 0, :]
    second_weight = weight_ref[:, 1, :]
    same = first == second
    first_weight = jnp.where(same, first_weight + second_weight, first_weight)
    second_weight = jnp.where(same, 0.0, second_weight)
    first_high = first_weight.astype(BF16).astype(F32)
    second_high = second_weight.astype(BF16).astype(F32)
    tables = jnp.concatenate(
        [
            (first >> 4).astype(F32),
            (first & 15).astype(F32),
            (second >> 4).astype(F32),
            (second & 15).astype(F32),
            first_high,
            second_high,
            (first_weight - first_high) * LOW_SCALE,
            (second_weight - second_high) * LOW_SCALE,
        ],
        axis=0,
    ).astype(BF16)
    table_step = (
        lax.broadcasted_iota(I32, (BOX, WIDE), 0)
        - (lax.broadcasted_iota(I32, (BOX, WIDE), 1) >> 4)
    ).astype(I16)
    one = jnp.ones((BOX, WIDE), BF16)
    pose_row = lax.broadcasted_iota(I32, (POSES, WIDE), 0) == (
        lax.broadcasted_iota(I32, (POSES, WIDE), 1) & (POSES - 1)
    )

    def table_rows(g, carry):
        at = pl.ds(pl.multiple_of(g * WIDE, WIDE), WIDE)
        first_row = jnp.full((BOX, WIDE), g * GROUP, I32).astype(I16)
        chosen_row = jnp.where(table_step == first_row, one, jnp.zeros_like(one))
        wide = jnp.dot(tables, chosen_row, preferred_element_type=F32)
        found = [
            jnp.sum(
                jnp.where(pose_row, wide[n * POSES : (n + 1) * POSES, :], 0.0),
                axis=0,
                keepdims=True,
            )
            for n in range(8)
        ]
        for n in range(2):
            slot = (found[2 * n] * 16.0 + found[2 * n + 1]).astype(I32)
            slots[n, :, at] = jnp.broadcast_to(slot, (GROUP, WIDE)).astype(I16)
        for n in range(4):
            weights[n, :, at] = jnp.broadcast_to(found[4 + n], (GROUP, WIDE)).astype(BF16)
        return carry

    lax.fori_loop(0, BOX // GROUP, table_rows, 0, unroll=8)
    pass_on(1, 7)
    slot_row = lax.broadcasted_iota(I32, (GROUP, WIDE), 0).astype(I16)

    def spread_rows(g, carry):
        at = pl.ds(pl.multiple_of(g * WIDE, WIDE), WIDE)
        first_slot, second_slot = slots[0, :, at], slots[1, :, at]
        parts = [weights[n, :, at] for n in range(4)]
        lows = []
        for block in range(LINES // GROUP):
            row = slot_row + jnp.int16(block * GROUP)
            is_first = first_slot == row
            is_second = second_slot == row
            high, low = (
                jnp.where(
                    is_first,
                    parts[n],
                    jnp.where(is_second, parts[n + 1], jnp.zeros_like(parts[n])),
                )
                for n in (0, 2)
            )
            spread[block * GROUP : (block + 1) * GROUP, at] = high
            lows.append(low)
            if block % 2:
                spread_low[(block - 1) * GROUP : (block + 1) * GROUP, at] = jnp.concatenate(
                    lows[-2:], axis=0
                ).astype(F8)
        return carry

    lax.fori_loop(0, BOX // GROUP, spread_rows, 0)
    pass_on(2, 6)

    slot_rows = lax.broadcasted_iota(I32, (GROUP, BOX), 0).astype(I16)
    for n, table, target, kind in (
        (0, first, pose_slots, I16),
        (1, second, pose_slots, I16),
        (0, first_high, pose_weights, BF16),
        (1, second_high, pose_weights, BF16),
    ):
        for p in range(POSES):
            target[n, p * GROUP : (p + 1) * GROUP, :] = jnp.broadcast_to(
                table[p : p + 1, :], (GROUP, BOX)
            ).astype(kind)

    def spread_squares(p, carry):
        rows_p = pl.ds(pl.multiple_of(p * GROUP, GROUP), GROUP)
        first_slot, second_slot = pose_slots[0, rows_p, :], pose_slots[1, rows_p, :]
        first_part, second_part = pose_weights[0, rows_p, :], pose_weights[1, rows_p, :]
        blocks = []
        for block in range(LINES // GROUP):
            row = slot_rows + jnp.int16(block * GROUP)
            rest = jnp.where(second_slot == row, second_part, jnp.zeros_like(second_part))
            blocks.append(jnp.where(first_slot == row, first_part, rest))
        spread_square[p] = jnp.dot(
            jnp.concatenate(blocks, axis=0), squares[...], preferred_element_type=F32
        )
        return carry

    pass_on(3, 5, 4)
    lax.fori_loop(0, 8, shift_rows, 0)
    swap(0)
    lax.fori_loop(8, BOX // GROUP, shift_rows, 0)
    swap(1)
    lax.fori_loop(0, POSES, spread_squares, 0, unroll=8)
    swap(2)

    slot_lines = held_row(lax.broadcasted_iota(I32, (1, LINES), 1), z, y, x, core)
    order = jnp.where(
        lax.broadcasted_iota(I32, (LINES, LINES), 0) == slot_lines, 1.0, 0.0
    ).astype(BF16)

    def transpose_half(c):
        rows_c = pl.ds(pl.multiple_of(c * BOX, BOX), BOX)
        half = lax.dot_general(
            held[c].reshape(LINES, BOX),
            order,
            (((0,), (0,)), ((), ())),
            preferred_element_type=F32,
        )
        lines_t[rows_c, :] = half.astype(BF16)
        lines_low[rows_c, :] = half.astype(F8)

    def slice_half(c):
        half = pl.ds(pl.multiple_of(c * BOX, BOX), BOX)

        def step(n, carry):
            at = pl.ds(pl.multiple_of(n * 4 * WIDE, 4 * WIDE), 4 * WIDE)
            high = jnp.dot(lines_t[half, :], spread[:, at], preferred_element_type=F32)
            low = jnp.dot(lines_low[half, :], spread_low[:, at], preferred_element_type=F32)
            slices[half, at] = (high + low * (1.0 / LOW_SCALE)).astype(BF16)
            return carry

        lax.fori_loop(0, ROWS // (4 * WIDE), step, 0, unroll=True)

    transpose_half(core)
    slice_half(core)
    landed(held.at[1 - core], 11)
    transpose_half(1 - core)
    slice_half(1 - core)

    lane_row = lax.broadcasted_iota(I32, (GROUP, 128), 1) >> 4
    nothing = jnp.zeros((GROUP, 128), BF16)

    def diagonal(k, tile):
        return jnp.concatenate([tile, nothing] if k < GROUP // 2 else [nothing, tile], axis=1)

    lane_pose = lax.broadcasted_iota(I32, (GROUP, 128), 1) < POSES

    def correlate(g, carry):
        at = pl.ds(pl.multiple_of(g * WIDE, WIDE), WIDE)
        found = jnp.dot(shifted[at, :], slices[:, at], preferred_element_type=F32)
        parts = []
        for k in range(GROUP):
            lane_at = k // (GROUP // 2) * 128
            block = found[k * GROUP : (k + 1) * GROUP, lane_at : lane_at + 128]
            if k % (GROUP // 2):
                block = pltpu.roll(block, 128 - k % (GROUP // 2) * POSES, 1)
            block = jnp.where(lane_pose, block, 0.0)
            high = block.astype(BF16)
            low = (block - high.astype(F32)).astype(BF16)
            parts.append(jnp.concatenate([high, low], axis=1))
        products[at, :] = jnp.concatenate(parts, axis=0)
        return carry

    lax.fori_loop(0, BOX // GROUP, correlate, 0, unroll=True)
    corr = jnp.dot(phases[...], products[...], preferred_element_type=F32)
    half = SHIFTS * SHIFTS
    corr = corr[:half, :POSES] + (corr[half:, :POSES] + corr[:half, 128 : 128 + POSES])
    score = corr * (precision_ref[0] / BOX)
    top = jnp.max(score, axis=(0, 1), keepdims=True)
    terms = jnp.exp(score - top)
    total = jnp.sum(terms, axis=(0, 1), keepdims=True)
    posterior = terms / total
    loglik_ref[0] = ((top + jnp.log(total)) * alive)[0, 0]
    posterior_t = posterior.T
    mass = jnp.sum(posterior_t, axis=1, keepdims=True)

    ring8 = (4, 3, 5, 2, 6, 1, 7)
    ring4 = (2, 1, 3)
    pairs = []

    def spread_half(first_slot, c):
        return jnp.dot(
            spread[first_slot : first_slot + KEEP, :],
            rows[:, c * BOX : (c + 1) * BOX],
            preferred_element_type=F32,
        )

    def send_pair(c, total):
        pair_out[c] = total.astype(BF16)
        copy = remote(pair_out.at[c], pair_in.at[c], pair_send.at[c], pair_recv.at[c], sibling)
        copy.start()
        pairs.append(copy)

    part = NY * NZ
    a_pairs = {}

    def send_pair_blocks(c, total):
        pair_out[c] = total.astype(BF16)
        for n, k in enumerate(ring4 + (0,)):
            block = pl.ds(k * part, part)
            copy = remote(
                pair_out.at[c, block],
                pair_in.at[c, block],
                pair_send.at[3 + n],
                pair_recv.at[3 + n],
                sibling,
            )
            copy.start()
            pairs.append(copy)
            a_pairs[k] = copy

    def spread_own(c):
        sums[c] = spread_half(0, c)

    def spread_mass(first_slot):
        total = spread_square[0, first_slot : first_slot + KEEP, :] * mass[0:1, :]
        for p in range(1, POSES):
            total = total + spread_square[p, first_slot : first_slot + KEEP, :] * mass[p : p + 1, :]
        return total

    def turn_poses():
        high = posterior_t.astype(BF16)
        low = (posterior_t - high.astype(F32)).astype(BF16)
        parts = jnp.concatenate(
            [
                jnp.concatenate([high, high], axis=1),
                jnp.concatenate([low, jnp.zeros_like(low)], axis=1),
            ],
            axis=0,
        )
        both_parts = jnp.dot(parts, phases[...], preferred_element_type=F32)
        turned[...] = (both_parts[:POSES] + both_parts[POSES:]).astype(BF16)

    def insert(g, carry):
        at = pl.ds(pl.multiple_of(g * WIDE, WIDE), WIDE)
        turns_g = turned[:, at]
        weight = jnp.concatenate(
            [
                diagonal(
                    k,
                    jnp.where(
                        lane_row == k % (GROUP // 2),
                        turns_g[:, k // (GROUP // 2) * 128 : k // (GROUP // 2) * 128 + 128],
                        nothing,
                    ),
                )
                for k in range(GROUP)
            ],
            axis=0,
        )
        rows[at, :] = jnp.dot(
            weight, shifted[at, :], preferred_element_type=F32
        ).astype(BF16)
        return carry

    hops = []

    def hop(number, src, dst, device):
        copy = remote(src, dst, hop_send.at[number], hop_recv.at[number], device)
        copy.start()
        hops.append(copy)
        return copy


    send_pair(2, spread_mass(KEEP))
    sums[2] = spread_mass(0)
    turn_poses()
    lax.fori_loop(0, BOX // GROUP, insert, 0, unroll=True)
    pairs[0].wait_recv()
    c_sum = sums[2] + pair_in[2].astype(F32)
    for half in range(2):
        strided[half] = c_sum[:, half * 128 : (half + 1) * 128]

    def c_rows(k):
        rows_k = pl.ds(k, NX * NY, NZ)
        return jnp.concatenate([strided[0, rows_k, :], strided[1, rows_k, :]], axis=1)

    c_hops = []
    for k in ring8:
        cz_out[k] = c_rows(k).astype(BF16)
        c_hops.append(hop(k, cz_out.at[k], cz_in.at[k], along_z(k)))
    send_pair(0, spread_half(KEEP, 0))
    send_pair_blocks(1, spread_half(KEEP, 1))
    spread_own(0)
    spread_own(1)

    pairs[1].wait_recv()
    b_sum = (sums[0] + pair_in[0].astype(F32)).reshape(NX, NY, NZ, BOX)
    b_hops = []
    for k in ring8:
        by_out[k] = b_sum[:, k].reshape(NX * NZ, BOX).astype(BF16)
        b_hops.append(hop(NZ + k, by_out.at[k], by_in.at[k], along_y(k)))
    b_sum = b_sum[:, 0].reshape(NX * NZ, BOX)
    def a_block(k):
        a_pairs[k].wait_recv()
        block = pl.ds(k * part, part)
        return sums[1, block, :] + pair_in[1, block, :].astype(F32)

    a_hops = []
    for k in ring4:
        ax_out[k] = a_block(k).astype(BF16)
        a_hops.append(hop(2 * NZ + k, ax_out.at[k], ax_in.at[k], along_x(k)))
    a_sum = a_block(0)

    pl.semaphore_wait(ready, NX - 1)
    left(held.at[core, y_lo, pl.ds(0, NZ - 1)], 0)
    left(held.at[core, pl.ds(0, 3)], 1)
    left(held.at[core], 2)
    for copy in pairs + hops:
        copy.wait_send()

    def last(rows_out, rows_in, total, number, size, owner):
        count = total.shape[0]
        rows_out[...] = total.reshape(count, 1, BOX)

        def hops_to(n):
            far_step, near_step = divmod(n, 8)
            return min(far_step, size - far_step) + min(near_step, 8 - near_step)

        for n in sorted(range(1, count), key=hops_to, reverse=True):
            remote(
                rows_out.at[n], rows_in.at[n], last_send.at[number], last_recv.at[number], owner(n)
            ).start()

    def collect(rows_in, total, number):
        arrived = rows_in.at[pl.ds(1, total.shape[0] - 1)]
        pltpu.make_async_copy(arrived, arrived, last_recv.at[number]).wait()
        return total[0:1, :] + jnp.sum(rows_in[1:], axis=0)

    def drain(rows_out, number):
        gone = rows_out.at[pl.ds(1, rows_out.shape[0] - 1)]
        pltpu.make_async_copy(gone, gone, last_send.at[number]).wait()

    c_sum = c_rows(0)
    for k, copy in zip(ring8, c_hops):
        copy.wait_recv()
        c_sum = c_sum + cz_in[k].astype(F32)
    last(
        c_last_out,
        c_last_in,
        c_sum,
        2,
        NX,
        lambda n: device_at(z, (y + n % NY) % NY, (x + n // NY) % NX, core),
    )
    for k, copy in zip(ring4, a_hops):
        copy.wait_recv()
        a_sum = a_sum + ax_in[k].astype(F32)
    last(
        a_last_out,
        a_last_in,
        a_sum,
        1,
        NY,
        lambda n: device_at((z + n % NZ) % NZ, (y + n // NZ) % NY, x, core),
    )
    for k, copy in zip(ring8, b_hops):
        copy.wait_recv()
        b_sum = b_sum + by_in[k].astype(F32)
    last(
        b_last_out,
        b_last_in,
        b_sum,
        0,
        NX,
        lambda n: device_at((z + n % NZ) % NZ, y, (x + n // NZ) % NX, core),
    )
    out_ref[:, 2 * BOX :] = collect(c_last_in, c_sum, 2)
    out_ref[:, BOX : 2 * BOX] = collect(a_last_in, a_sum, 1)
    out_ref[:, :BOX] = collect(b_last_in, b_sum, 0)
    drain(c_last_out, 2)
    drain(a_last_out, 1)
    drain(b_last_out, 0)


def expect(*operands):
    smem = pl.BlockSpec(memory_space=pltpu.SMEM)
    vmem = pl.BlockSpec(memory_space=pltpu.VMEM)
    dma = pltpu.SemaphoreType.DMA
    hop_count = 2 * NZ + NX

    def both_ways(shape, kind):
        return [pltpu.VMEM(shape, kind), pltpu.VMEM(shape, kind)]

    return pl.pallas_call(
        expect_kernel,
        out_shape=(
            jax.ShapeDtypeStruct((1, 3 * BOX), F32),
            jax.ShapeDtypeStruct((1,), F32),
        ),
        in_specs=[pl.BlockSpec(memory_space=pltpu.HBM)] * 10,
        out_specs=(vmem, smem),
        scratch_shapes=[
            pltpu.SMEM(operand.shape, operand.dtype) for operand in operands[:6]
        ]
        + [pltpu.VMEM(operand.shape, operand.dtype) for operand in operands[6:]]
        + [dma((10,))]
        + [
            pltpu.VMEM((2, Y_LO, NZ, 16, BOX), BF16),
            pltpu.VMEM((2, GROUP, ROWS), I16),
            pltpu.VMEM((4, GROUP, ROWS), BF16),
            pltpu.VMEM((2 * BOX, LINES), BF16),
            pltpu.VMEM((2 * BOX, LINES), F8),
            pltpu.VMEM((LINES, ROWS), BF16),
            pltpu.VMEM((LINES, ROWS), F8),
            pltpu.VMEM((2 * BOX, ROWS), BF16),
            pltpu.VMEM((ROWS, 2 * BOX), BF16),
            pltpu.VMEM((2 * SHIFTS * SHIFTS, ROWS), BF16),
            pltpu.VMEM((BOX, BOX), BF16),
            pltpu.VMEM((ROWS, WIDE), BF16),
            pltpu.VMEM((POSES, ROWS), BF16),
            pltpu.VMEM((ROWS, 2 * BOX), BF16),
            pltpu.VMEM((2, POSES * GROUP, BOX), I16),
            pltpu.VMEM((2, POSES * GROUP, BOX), BF16),
            pltpu.VMEM((POSES, LINES, BOX), F32),
            pltpu.VMEM((3, KEEP, BOX), F32),
            pltpu.VMEM((2, KEEP, BOX // 2), F32),
        ]
        + both_ways((3, KEEP, BOX), BF16)
        + both_ways((NX, NY * NZ, BOX), BF16)
        + both_ways((NY, NX * NZ, BOX), BF16)
        + both_ways((NZ, NX * NY, BOX), BF16)
        + both_ways((NY * NZ, 1, BOX), F32)
        + both_ways((NX * NZ, 1, BOX), F32)
        + both_ways((NX * NY, 1, BOX), F32)
        + [
            dma((3,)),
            dma((12,)),
            dma((7,)),
            dma((7,)),
            dma((hop_count,)),
            dma((hop_count,)),
            dma((3,)),
            dma((3,)),
            pltpu.SemaphoreType.REGULAR,
        ],
        compiler_params=pltpu.CompilerParams(
            collective_id=0, has_side_effects=True, vmem_limit_bytes=60 * 1024 * 1024
        ),
    )(*operands)


def body(
    particles,
    defocus_class,
    noise_precision,
    live_count,
    defocus,
    reference_lines,
    line_index,
    line_weight,
    row_shifts,
    column_shifts,
):
    index = jnp.transpose(line_index, (0, 2, 1))
    weight = jnp.transpose(line_weight, (0, 2, 1))
    particle_total = particles.shape[0] * lax.axis_size("slab") * lax.axis_size("grp")
    owned, loglik = expect(
        defocus_class,
        noise_precision,
        live_count,
        defocus,
        row_shifts,
        column_shifts,
        particles,
        index,
        weight,
        reference_lines,
    )
    return owned.reshape(1, 3, BOX) * (LINES / (POSES * particle_total)), loglik


def solution(mesh):
    return jax.shard_map(
        body,
        mesh=mesh,
        in_specs=(
            P(("slab", "grp"), None, None, None),
            P(("slab", "grp")),
            P(("slab", "grp")),
            P("grp"),
            P(),
            P("slab", None, None),
            P(),
            P(),
            P(),
            P(),
        ),
        out_specs=(P(("slab", "grp"), None, None), P(("slab", "grp"))),
        check_vma=False,
    )
```

```python
import math

import jax
import jax.numpy as jnp
from jax import lax
from jax.experimental import pallas as pl
from jax.experimental.pallas import tpu as pltpu
from jax.sharding import PartitionSpec as P

MESH = pl.DeviceIdType.MESH
EXACT = lax.Precision.HIGHEST
F32 = jnp.float32
BF16 = jnp.bfloat16
I32 = jnp.int32
I16 = jnp.int16
F8 = jnp.float8_e4m3fn
LOW_SCALE = 512.0

NX, NY, NZ, Y_LO = 4, 8, 8, 4
SLABS = NZ * Y_LO
LINES = 512
KEEP = LINES // 2
BOX = 256
POSES = 16
GROUP = 16
WIDE = GROUP * POSES
ROWS = POSES * BOX
SHIFTS = 8


def place():
    slab = lax.axis_index("slab")
    grp = lax.axis_index("grp")
    z, y_lo = slab // Y_LO, slab % Y_LO
    y_hi, x, core = grp // (2 * NX), (grp // 2) % NX, grp % 2
    return z, y_hi * Y_LO + y_lo, x, core


def device_at(z, y, x, core):
    return (z * Y_LO + y % Y_LO, (y // Y_LO) * (2 * NX) + x * 2 + core)


def phase_angle(turns):
    signed = ((turns + BOX // 2) & (BOX - 1)) - BOX // 2
    return signed.astype(F32) * (2.0 * math.pi / BOX)


def shift_column(shifts_ref, shape):
    row = lax.broadcasted_iota(I32, shape, 0)
    column = jnp.zeros(shape, I32)
    for t in range(SHIFTS):
        column = jnp.where(row == t, shifts_ref[t], column)
    return column


def slot_of(line, z, y, x, core):
    line_y = ((line >> 3) & 1) * Y_LO + ((line >> 4) & (Y_LO - 1))
    return (
        ((line ^ core) & 1) * KEEP
        + ((((line >> 1) - x) & (NX - 1)) * (NY * NZ))
        + (((line_y - y) & (NY - 1)) * NZ)
        + (((line >> 6) - z) & (NZ - 1))
    )


def held_row(slot, z, y, x, core):
    line_z = (slot + z) & (NZ - 1)
    line_y = ((slot >> 3) + y) & (NY - 1)
    line_x = ((slot >> 6) + x) & (NX - 1)
    line_core = ((slot >> 8) ^ core) & 1
    return (line_y & 3) * (NZ * 16) + line_z * 16 + (line_y >> 2) * 8 + line_x * 2 + line_core


def expect_kernel(
    class_hbm,
    precision_hbm,
    live_hbm,
    defocus_hbm,
    row_shift_hbm,
    column_shift_hbm,
    image_hbm,
    index_hbm,
    weight_hbm,
    lines_hbm,
    out_ref,
    loglik_ref,
    class_ref,
    precision_ref,
    live_ref,
    defocus_ref,
    row_shift_ref,
    column_shift_ref,
    image_ref,
    index_ref,
    weight_ref,
    lines_ref,
    load_sem,
    held,
    slots,
    weights,
    lines_t,
    lines_low,
    spread,
    spread_low,
    slices,
    shifted,
    phases,
    squares,
    products,
    turned,
    rows,
    pose_slots,
    pose_weights,
    spread_square,
    sums,
    strided,
    pair_out,
    pair_in,
    ax_out,
    ax_in,
    by_out,
    by_in,
    cz_out,
    cz_in,
    a_last_out,
    a_last_in,
    b_last_out,
    b_last_in,
    c_last_out,
    c_last_in,
    gather_send,
    gather_recv,
    pair_send,
    pair_recv,
    hop_send,
    hop_recv,
    last_send,
    last_recv,
    ready,
):
    z, y, x, core = place()
    y_lo = y % Y_LO
    sibling = device_at(z, y, x, 1 - core)

    def along_x(k):
        return device_at(z, y, (x + k) % NX, core)

    def along_y(k):
        return device_at(z, (y + NY + k) % NY, x, core)

    def along_z(k):
        return device_at((z + k) % NZ, y, x, core)

    def remote(src, dst, send, recv, device):
        return pltpu.make_async_remote_copy(
            src_ref=src,
            dst_ref=dst,
            send_sem=send,
            recv_sem=recv,
            device_id=device,
            device_id_type=MESH,
        )

    barrier = pltpu.get_barrier_semaphore()
    peers = [sibling]
    peers += [along_x(k) for k in range(1, NX)]
    peers += [along_y(k) for k in range(1, NY)]
    peers += [along_z(k) for k in range(1, NZ)]
    for peer in peers:
        pl.semaphore_signal(barrier, inc=1, device_id=peer, device_id_type=MESH)

    loads = [
        pltpu.make_async_copy(src, dst, load_sem.at[n])
        for n, (src, dst) in enumerate(
            [
                (lines_hbm, lines_ref),
                (class_hbm, class_ref),
                (live_hbm, live_ref),
                (defocus_hbm, defocus_ref),
                (column_shift_hbm, column_shift_ref),
                (row_shift_hbm, row_shift_ref),
                (image_hbm, image_ref),
                (index_hbm, index_ref),
                (weight_hbm, weight_ref),
                (precision_hbm, precision_ref),
            ]
        )
    ]
    for load in loads:
        load.start()

    loads[0].wait()
    both = lines_ref[...]
    held[core, y_lo, z] = jnp.where(core == 0, both[:, 0, :], both[:, 1, :])

    pl.semaphore_wait(barrier, len(peers))
    for k in range(1, NX):
        pl.semaphore_signal(ready, inc=1, device_id=along_x(k), device_id_type=MESH)

    def send_block(src, send, recv, device):
        copy = remote(src, src, gather_send.at[send], gather_recv.at[recv], device)
        copy.start()
        return copy

    def landed(blocks, number):
        pltpu.make_async_copy(blocks, blocks, gather_recv.at[number]).wait()

    def left(blocks, number):
        pltpu.make_async_copy(blocks, blocks, gather_send.at[number]).wait()

    groups = ((0, 1, 7), (2, 6), (3, 5, 4))
    near_z = {
        k: send_block(held.at[core, y_lo, z], 0, k, along_z(k)) for k in (4, 3, 5, 2, 6, 1, 7)
    }
    far = 2 - 4 * core
    steps = {1: 1, 2: far, 3: -1}

    def pass_along_y(k):
        block = held.at[core, y_lo, (z + NZ - k) % NZ]
        group = [k in members for members in groups].index(True)
        for d in (2, 1, 3):
            send_block(block, 1, NZ + group, along_y(steps[d]))
        send_block(block, 2, 11, sibling)

    def pass_on(*distances):
        for k in distances:
            near_z[k].wait_recv()
            pass_along_y(k)

    def swap(group):
        landed(held.at[core, pl.ds(0, 3), pl.ds(0, len(groups[group]))], NZ + group)
        for k in groups[group]:
            for residue in (y_lo + 3, y_lo + 1, y_lo + 2):
                send_block(held.at[core, residue % Y_LO, (z + NZ - k) % NZ], 2, 11, sibling)

    pass_along_y(0)
    for load in loads[1:]:
        load.wait()
    alive = jnp.where(0 < live_ref[0], 1.0, 0.0).astype(F32)
    chosen = defocus_ref[class_ref[0]]

    lane_y = lax.broadcasted_iota(I32, (SHIFTS, BOX), 1) - BOX // 2
    angle_y = phase_angle(lane_y * shift_column(column_shift_ref, (SHIFTS, BOX)))
    cos_y = jnp.cos(angle_y)
    sin_y = jnp.sin(angle_y)
    freq_y = (lax.broadcasted_iota(I32, (GROUP, BOX), 1) - BOX // 2).astype(F32) / BOX
    row_in_group = lax.broadcasted_iota(I32, (GROUP, BOX), 0)

    def shift_rows(g, carry):
        at = pl.ds(pl.multiple_of(g * WIDE, WIDE), WIDE)
        kx = pl.ds(pl.multiple_of(g * GROUP, GROUP), GROUP)
        freq_x = (row_in_group + (g * GROUP - BOX // 2)).astype(F32) / BOX
        ctf = -jnp.sin(chosen * (freq_x * freq_x + freq_y * freq_y) + 0.1) * alive
        squares[kx, :] = (ctf * ctf).astype(BF16)
        real = ctf * image_ref[0, 0, kx, :].astype(F32)
        imag = ctf * image_ref[0, 1, kx, :].astype(F32)
        blocks = []
        for k in range(GROUP):
            real_row = real[k : k + 1, :]
            imag_row = imag[k : k + 1, :]
            shift_re = real_row * cos_y + imag_row * sin_y
            shift_im = real_row * sin_y - imag_row * cos_y
            blocks.append(jnp.concatenate([shift_re, -shift_im], axis=1))
            blocks.append(jnp.concatenate([shift_im, shift_re], axis=1))
        shifted[at, :] = jnp.concatenate(blocks, axis=0).astype(BF16)
        return carry

    lane = lax.broadcasted_iota(I32, (SHIFTS, ROWS), 1)
    freq = (lane >> 4) - BOX // 2
    part = (lane >> 3) & 1
    turns = freq * shift_column(row_shift_ref, (SHIFTS, ROWS)) + part * (BOX // 4)
    row_phase = jnp.cos(phase_angle(turns))
    row_high = row_phase.astype(BF16).astype(F32)
    row_low = row_phase - row_high
    for t in range(0, SHIFTS, 2):
        for base, table in ((0, row_high), (SHIFTS * SHIFTS, row_low)):
            phases[pl.ds(base + t * SHIFTS, 2 * SHIFTS), :] = jnp.concatenate(
                [jnp.where((lane & 7) == t + u, table, 0.0) for u in range(2)], axis=0
            ).astype(BF16)

    first = slot_of(index_ref[:, 0, :], z, y, x, core)
    second = slot_of(index_ref[:, 1, :], z, y, x, core)
    first_weight = weight_ref[:, 0, :]
    second_weight = weight_ref[:, 1, :]
    same = first == second
    first_weight = jnp.where(same, first_weight + second_weight, first_weight)
    second_weight = jnp.where(same, 0.0, second_weight)
    first_high = first_weight.astype(BF16).astype(F32)
    second_high = second_weight.astype(BF16).astype(F32)
    tables = jnp.concatenate(
        [
            (first >> 4).astype(F32),
            (first & 15).astype(F32),
            (second >> 4).astype(F32),
            (second & 15).astype(F32),
            first_high,
            second_high,
            (first_weight - first_high) * LOW_SCALE,
            (second_weight - second_high) * LOW_SCALE,
        ],
        axis=0,
    ).astype(BF16)
    table_step = (
        lax.broadcasted_iota(I32, (BOX, WIDE), 0)
        - (lax.broadcasted_iota(I32, (BOX, WIDE), 1) >> 4)
    ).astype(I16)
    one = jnp.ones((BOX, WIDE), BF16)
    pose_row = lax.broadcasted_iota(I32, (POSES, WIDE), 0) == (
        lax.broadcasted_iota(I32, (POSES, WIDE), 1) & (POSES - 1)
    )

    def table_rows(g, carry):
        at = pl.ds(pl.multiple_of(g * WIDE, WIDE), WIDE)
        first_row = jnp.full((BOX, WIDE), g * GROUP, I32).astype(I16)
        chosen_row = jnp.where(table_step == first_row, one, jnp.zeros_like(one))
        wide = jnp.dot(tables, chosen_row, preferred_element_type=F32)
        found = [
            jnp.sum(
                jnp.where(pose_row, wide[n * POSES : (n + 1) * POSES, :], 0.0),
                axis=0,
                keepdims=True,
            )
            for n in range(8)
        ]
        for n in range(2):
            slot = (found[2 * n] * 16.0 + found[2 * n + 1]).astype(I32)
            slots[n, :, at] = jnp.broadcast_to(slot, (GROUP, WIDE)).astype(I16)
        for n in range(4):
            weights[n, :, at] = jnp.broadcast_to(found[4 + n], (GROUP, WIDE)).astype(BF16)
        return carry

    lax.fori_loop(0, BOX // GROUP, table_rows, 0, unroll=8)
    pass_on(1, 7)
    slot_row = lax.broadcasted_iota(I32, (GROUP, WIDE), 0).astype(I16)

    def spread_rows(g, carry):
        at = pl.ds(pl.multiple_of(g * WIDE, WIDE), WIDE)
        first_slot, second_slot = slots[0, :, at], slots[1, :, at]
        parts = [weights[n, :, at] for n in range(4)]
        lows = []
        for block in range(LINES // GROUP):
            row = slot_row + jnp.int16(block * GROUP)
            is_first = first_slot == row
            is_second = second_slot == row
            high, low = (
                jnp.where(
                    is_first,
                    parts[n],
                    jnp.where(is_second, parts[n + 1], jnp.zeros_like(parts[n])),
                )
                for n in (0, 2)
            )
            spread[block * GROUP : (block + 1) * GROUP, at] = high
            lows.append(low)
            if block % 2:
                spread_low[(block - 1) * GROUP : (block + 1) * GROUP, at] = jnp.concatenate(
                    lows[-2:], axis=0
                ).astype(F8)
        return carry

    lax.fori_loop(0, BOX // GROUP, spread_rows, 0)
    pass_on(2, 6)

    slot_rows = lax.broadcasted_iota(I32, (GROUP, BOX), 0).astype(I16)
    for n, table, target, kind in (
        (0, first, pose_slots, I16),
        (1, second, pose_slots, I16),
        (0, first_high, pose_weights, BF16),
        (1, second_high, pose_weights, BF16),
    ):
        for p in range(POSES):
            target[n, p * GROUP : (p + 1) * GROUP, :] = jnp.broadcast_to(
                table[p : p + 1, :], (GROUP, BOX)
            ).astype(kind)

    def spread_squares(p, carry):
        rows_p = pl.ds(pl.multiple_of(p * GROUP, GROUP), GROUP)
        first_slot, second_slot = pose_slots[0, rows_p, :], pose_slots[1, rows_p, :]
        first_part, second_part = pose_weights[0, rows_p, :], pose_weights[1, rows_p, :]
        blocks = []
        for block in range(LINES // GROUP):
            row = slot_rows + jnp.int16(block * GROUP)
            rest = jnp.where(second_slot == row, second_part, jnp.zeros_like(second_part))
            blocks.append(jnp.where(first_slot == row, first_part, rest))
        spread_square[p] = jnp.dot(
            jnp.concatenate(blocks, axis=0), squares[...], preferred_element_type=F32
        )
        return carry

    pass_on(3, 5, 4)
    lax.fori_loop(0, 8, shift_rows, 0)
    swap(0)
    lax.fori_loop(8, BOX // GROUP, shift_rows, 0)
    swap(1)
    lax.fori_loop(0, POSES, spread_squares, 0, unroll=8)
    swap(2)

    slot_lines = held_row(lax.broadcasted_iota(I32, (1, LINES), 1), z, y, x, core)
    order = jnp.where(
        lax.broadcasted_iota(I32, (LINES, LINES), 0) == slot_lines, 1.0, 0.0
    ).astype(BF16)

    def transpose_half(c):
        rows_c = pl.ds(pl.multiple_of(c * BOX, BOX), BOX)
        half = lax.dot_general(
            held[c].reshape(LINES, BOX),
            order,
            (((0,), (0,)), ((), ())),
            preferred_element_type=F32,
        )
        lines_t[rows_c, :] = half.astype(BF16)
        lines_low[rows_c, :] = half.astype(F8)

    def slice_half(c):
        half = pl.ds(pl.multiple_of(c * BOX, BOX), BOX)

        def step(n, carry):
            at = pl.ds(pl.multiple_of(n * 4 * WIDE, 4 * WIDE), 4 * WIDE)
            high = jnp.dot(lines_t[half, :], spread[:, at], preferred_element_type=F32)
            low = jnp.dot(lines_low[half, :], spread_low[:, at], preferred_element_type=F32)
            slices[half, at] = (high + low * (1.0 / LOW_SCALE)).astype(BF16)
            return carry

        lax.fori_loop(0, ROWS // (4 * WIDE), step, 0, unroll=True)

    transpose_half(core)
    slice_half(core)
    landed(held.at[1 - core], 11)
    transpose_half(1 - core)
    slice_half(1 - core)

    lane_row = lax.broadcasted_iota(I32, (GROUP, 128), 1) >> 4
    nothing = jnp.zeros((GROUP, 128), BF16)

    def diagonal(k, tile):
        return jnp.concatenate([tile, nothing] if k < GROUP // 2 else [nothing, tile], axis=1)

    lane_pose = lax.broadcasted_iota(I32, (GROUP, 128), 1) < POSES

    def correlate(g, carry):
        at = pl.ds(pl.multiple_of(g * WIDE, WIDE), WIDE)
        found = jnp.dot(shifted[at, :], slices[:, at], preferred_element_type=F32)
        parts = []
        for k in range(GROUP):
            lane_at = k // (GROUP // 2) * 128
            block = found[k * GROUP : (k + 1) * GROUP, lane_at : lane_at + 128]
            if k % (GROUP // 2):
                block = pltpu.roll(block, 128 - k % (GROUP // 2) * POSES, 1)
            block = jnp.where(lane_pose, block, 0.0)
            high = block.astype(BF16)
            low = (block - high.astype(F32)).astype(BF16)
            parts.append(jnp.concatenate([high, low], axis=1))
        products[at, :] = jnp.concatenate(parts, axis=0)
        return carry

    lax.fori_loop(0, BOX // GROUP, correlate, 0, unroll=True)
    corr = jnp.dot(phases[...], products[...], preferred_element_type=F32)
    half = SHIFTS * SHIFTS
    corr = corr[:half, :POSES] + (corr[half:, :POSES] + corr[:half, 128 : 128 + POSES])
    score = corr * (precision_ref[0] / BOX)
    top = jnp.max(score, axis=(0, 1), keepdims=True)
    terms = jnp.exp(score - top)
    total = jnp.sum(terms, axis=(0, 1), keepdims=True)
    posterior = terms / total
    loglik_ref[0] = ((top + jnp.log(total)) * alive)[0, 0]
    posterior_t = posterior.T
    mass = jnp.sum(posterior_t, axis=1, keepdims=True)

    ring8 = (4, 3, 5, 2, 6, 1, 7)
    ring4 = (2, 1, 3)
    pairs = []

    def spread_half(first_slot, c):
        return jnp.dot(
            spread[first_slot : first_slot + KEEP, :],
            rows[:, c * BOX : (c + 1) * BOX],
            preferred_element_type=F32,
        )

    def send_pair(c, total):
        pair_out[c] = total.astype(BF16)
        copy = remote(pair_out.at[c], pair_in.at[c], pair_send.at[c], pair_recv.at[c], sibling)
        copy.start()
        pairs.append(copy)

    part = NY * NZ
    a_pairs = {}

    def send_pair_blocks(c, total):
        pair_out[c] = total.astype(BF16)
        for n, k in enumerate(ring4 + (0,)):
            block = pl.ds(k * part, part)
            copy = remote(
                pair_out.at[c, block],
                pair_in.at[c, block],
                pair_send.at[3 + n],
                pair_recv.at[3 + n],
                sibling,
            )
            copy.start()
            pairs.append(copy)
            a_pairs[k] = copy

    def spread_own(c):
        sums[c] = spread_half(0, c)

    def spread_mass(first_slot):
        total = spread_square[0, first_slot : first_slot + KEEP, :] * mass[0:1, :]
        for p in range(1, POSES):
            total = total + spread_square[p, first_slot : first_slot + KEEP, :] * mass[p : p + 1, :]
        return total

    def turn_poses():
        high = posterior_t.astype(BF16)
        low = (posterior_t - high.astype(F32)).astype(BF16)
        parts = jnp.concatenate(
            [
                jnp.concatenate([high, high], axis=1),
                jnp.concatenate([low, jnp.zeros_like(low)], axis=1),
            ],
            axis=0,
        )
        both_parts = jnp.dot(parts, phases[...], preferred_element_type=F32)
        turned[...] = (both_parts[:POSES] + both_parts[POSES:]).astype(BF16)

    def insert(g, carry):
        at = pl.ds(pl.multiple_of(g * WIDE, WIDE), WIDE)
        turns_g = turned[:, at]
        weight = jnp.concatenate(
            [
                diagonal(
                    k,
                    jnp.where(
                        lane_row == k % (GROUP // 2),
                        turns_g[:, k // (GROUP // 2) * 128 : k // (GROUP // 2) * 128 + 128],
                        nothing,
                    ),
                )
                for k in range(GROUP)
            ],
            axis=0,
        )
        rows[at, :] = jnp.dot(
            weight, shifted[at, :], preferred_element_type=F32
        ).astype(BF16)
        return carry

    hops = []

    def hop(number, src, dst, device):
        copy = remote(src, dst, hop_send.at[number], hop_recv.at[number], device)
        copy.start()
        hops.append(copy)
        return copy


    send_pair(2, spread_mass(KEEP))
    sums[2] = spread_mass(0)
    turn_poses()
    lax.fori_loop(0, BOX // GROUP, insert, 0, unroll=True)
    pairs[0].wait_recv()
    c_sum = sums[2] + pair_in[2].astype(F32)
    for half in range(2):
        strided[half] = c_sum[:, half * 128 : (half + 1) * 128]

    def c_rows(k):
        rows_k = pl.ds(k, NX * NY, NZ)
        return jnp.concatenate([strided[0, rows_k, :], strided[1, rows_k, :]], axis=1)

    c_hops = []
    for k in ring8:
        cz_out[k] = c_rows(k).astype(BF16)
        c_hops.append(hop(k, cz_out.at[k], cz_in.at[k], along_z(k)))
    send_pair(0, spread_half(KEEP, 0))
    send_pair_blocks(1, spread_half(KEEP, 1))
    spread_own(0)
    spread_own(1)

    pairs[1].wait_recv()
    b_sum = (sums[0] + pair_in[0].astype(F32)).reshape(NX, NY, NZ, BOX)
    b_hops = []
    for k in ring8:
        by_out[k] = b_sum[:, k].reshape(NX * NZ, BOX).astype(BF16)
        b_hops.append(hop(NZ + k, by_out.at[k], by_in.at[k], along_y(k)))
    b_sum = b_sum[:, 0].reshape(NX * NZ, BOX)
    def a_block(k):
        a_pairs[k].wait_recv()
        block = pl.ds(k * part, part)
        return sums[1, block, :] + pair_in[1, block, :].astype(F32)

    a_hops = []
    for k in ring4:
        ax_out[k] = a_block(k).astype(BF16)
        a_hops.append(hop(2 * NZ + k, ax_out.at[k], ax_in.at[k], along_x(k)))
    a_sum = a_block(0)

    pl.semaphore_wait(ready, NX - 1)
    left(held.at[core, y_lo, pl.ds(0, NZ - 1)], 0)
    left(held.at[core, pl.ds(0, 3)], 1)
    left(held.at[core], 2)
    for copy in pairs + hops:
        copy.wait_send()

    def last(rows_out, rows_in, total, number, size, owner):
        count = total.shape[0]
        rows_out[...] = total.reshape(count, 1, BOX)

        def hops_to(n):
            far_step, near_step = divmod(n, 8)
            return min(far_step, size - far_step) + min(near_step, 8 - near_step)

        for n in sorted(range(1, count), key=hops_to, reverse=True):
            remote(
                rows_out.at[n], rows_in.at[n], last_send.at[number], last_recv.at[number], owner(n)
            ).start()

    def collect(rows_in, total, number):
        arrived = rows_in.at[pl.ds(1, total.shape[0] - 1)]
        pltpu.make_async_copy(arrived, arrived, last_recv.at[number]).wait()
        return total[0:1, :] + jnp.sum(rows_in[1:], axis=0)

    def drain(rows_out, number):
        gone = rows_out.at[pl.ds(1, rows_out.shape[0] - 1)]
        pltpu.make_async_copy(gone, gone, last_send.at[number]).wait()

    c_sum = c_rows(0)
    for k, copy in zip(ring8, c_hops):
        copy.wait_recv()
        c_sum = c_sum + cz_in[k].astype(F32)
    last(
        c_last_out,
        c_last_in,
        c_sum,
        2,
        NX,
        lambda n: device_at(z, (y + n % NY) % NY, (x + n // NY) % NX, core),
    )
    for k, copy in zip(ring4, a_hops):
        copy.wait_recv()
        a_sum = a_sum + ax_in[k].astype(F32)
    last(
        a_last_out,
        a_last_in,
        a_sum,
        1,
        NY,
        lambda n: device_at((z + n % NZ) % NZ, (y + n // NZ) % NY, x, core),
    )
    for k, copy in zip(ring8, b_hops):
        copy.wait_recv()
        b_sum = b_sum + by_in[k].astype(F32)
    last(
        b_last_out,
        b_last_in,
        b_sum,
        0,
        NX,
        lambda n: device_at((z + n % NZ) % NZ, y, (x + n // NZ) % NX, core),
    )
    out_ref[:, 2 * BOX :] = collect(c_last_in, c_sum, 2)
    out_ref[:, BOX : 2 * BOX] = collect(a_last_in, a_sum, 1)
    out_ref[:, :BOX] = collect(b_last_in, b_sum, 0)
    drain(c_last_out, 2)
    drain(a_last_out, 1)
    drain(b_last_out, 0)


def expect(*operands):
    smem = pl.BlockSpec(memory_space=pltpu.SMEM)
    vmem = pl.BlockSpec(memory_space=pltpu.VMEM)
    dma = pltpu.SemaphoreType.DMA
    hop_count = 2 * NZ + NX

    def both_ways(shape, kind):
        return [pltpu.VMEM(shape, kind), pltpu.VMEM(shape, kind)]

    return pl.pallas_call(
        expect_kernel,
        out_shape=(
            jax.ShapeDtypeStruct((1, 3 * BOX), F32),
            jax.ShapeDtypeStruct((1,), F32),
        ),
        in_specs=[pl.BlockSpec(memory_space=pltpu.HBM)] * 10,
        out_specs=(vmem, smem),
        scratch_shapes=[
            pltpu.SMEM(operand.shape, operand.dtype) for operand in operands[:6]
        ]
        + [pltpu.VMEM(operand.shape, operand.dtype) for operand in operands[6:]]
        + [dma((10,))]
        + [
            pltpu.VMEM((2, Y_LO, NZ, 16, BOX), BF16),
            pltpu.VMEM((2, GROUP, ROWS), I16),
            pltpu.VMEM((4, GROUP, ROWS), BF16),
            pltpu.VMEM((2 * BOX, LINES), BF16),
            pltpu.VMEM((2 * BOX, LINES), F8),
            pltpu.VMEM((LINES, ROWS), BF16),
            pltpu.VMEM((LINES, ROWS), F8),
            pltpu.VMEM((2 * BOX, ROWS), BF16),
            pltpu.VMEM((ROWS, 2 * BOX), BF16),
            pltpu.VMEM((2 * SHIFTS * SHIFTS, ROWS), BF16),
            pltpu.VMEM((BOX, BOX), BF16),
            pltpu.VMEM((ROWS, WIDE), BF16),
            pltpu.VMEM((POSES, ROWS), BF16),
            pltpu.VMEM((ROWS, 2 * BOX), BF16),
            pltpu.VMEM((2, POSES * GROUP, BOX), I16),
            pltpu.VMEM((2, POSES * GROUP, BOX), BF16),
            pltpu.VMEM((POSES, LINES, BOX), F32),
            pltpu.VMEM((3, KEEP, BOX), F32),
            pltpu.VMEM((2, KEEP, BOX // 2), F32),
        ]
        + both_ways((3, KEEP, BOX), BF16)
        + both_ways((NX, NY * NZ, BOX), BF16)
        + both_ways((NY, NX * NZ, BOX), BF16)
        + both_ways((NZ, NX * NY, BOX), BF16)
        + both_ways((NY * NZ, 1, BOX), F32)
        + both_ways((NX * NZ, 1, BOX), F32)
        + both_ways((NX * NY, 1, BOX), F32)
        + [
            dma((3,)),
            dma((12,)),
            dma((7,)),
            dma((7,)),
            dma((hop_count,)),
            dma((hop_count,)),
            dma((3,)),
            dma((3,)),
            pltpu.SemaphoreType.REGULAR,
        ],
        compiler_params=pltpu.CompilerParams(
            collective_id=0, has_side_effects=True, vmem_limit_bytes=55208 * 1024
        ),
    )(*operands)


def body(
    particles,
    defocus_class,
    noise_precision,
    live_count,
    defocus,
    reference_lines,
    line_index,
    line_weight,
    row_shifts,
    column_shifts,
):
    index = jnp.transpose(line_index, (0, 2, 1))
    weight = jnp.transpose(line_weight, (0, 2, 1))
    particle_total = particles.shape[0] * lax.axis_size("slab") * lax.axis_size("grp")
    owned, loglik = expect(
        defocus_class,
        noise_precision,
        live_count,
        defocus,
        row_shifts,
        column_shifts,
        particles,
        index,
        weight,
        reference_lines,
    )
    return owned.reshape(1, 3, BOX) * (LINES / (POSES * particle_total)), loglik


def solution(mesh):
    return jax.shard_map(
        body,
        mesh=mesh,
        in_specs=(
            P(("slab", "grp"), None, None, None),
            P(("slab", "grp")),
            P(("slab", "grp")),
            P("grp"),
            P(),
            P("slab", None, None),
            P(),
            P(),
            P(),
            P(),
        ),
        out_specs=(P(("slab", "grp"), None, None), P(("slab", "grp"))),
        check_vma=False,
    )
```

```python
import math

import jax
import jax.numpy as jnp
from jax import lax
from jax.experimental import pallas as pl
from jax.experimental.pallas import tpu as pltpu
from jax.sharding import PartitionSpec as P

MESH = pl.DeviceIdType.MESH
EXACT = lax.Precision.HIGHEST
F32 = jnp.float32
BF16 = jnp.bfloat16
I32 = jnp.int32
I16 = jnp.int16
F8 = jnp.float8_e4m3fn
LOW_SCALE = 512.0

NX, NY, NZ, Y_LO = 4, 8, 8, 4
SLABS = NZ * Y_LO
LINES = 512
KEEP = LINES // 2
BOX = 256
POSES = 16
GROUP = 16
WIDE = GROUP * POSES
ROWS = POSES * BOX
SHIFTS = 8


def place():
    slab = lax.axis_index("slab")
    grp = lax.axis_index("grp")
    z, y_lo = slab // Y_LO, slab % Y_LO
    y_hi, x, core = grp // (2 * NX), (grp // 2) % NX, grp % 2
    return z, y_hi * Y_LO + y_lo, x, core


def device_at(z, y, x, core):
    return (z * Y_LO + y % Y_LO, (y // Y_LO) * (2 * NX) + x * 2 + core)


def phase_angle(turns):
    signed = ((turns + BOX // 2) & (BOX - 1)) - BOX // 2
    return signed.astype(F32) * (2.0 * math.pi / BOX)


def shift_column(shifts_ref, shape):
    row = lax.broadcasted_iota(I32, shape, 0)
    column = jnp.zeros(shape, I32)
    for t in range(SHIFTS):
        column = jnp.where(row == t, shifts_ref[t], column)
    return column


def slot_of(line, z, y, x, core):
    line_y = ((line >> 3) & 1) * Y_LO + ((line >> 4) & (Y_LO - 1))
    return (
        ((line ^ core) & 1) * KEEP
        + ((((line >> 1) - x) & (NX - 1)) * (NY * NZ))
        + (((line_y - y) & (NY - 1)) * NZ)
        + (((line >> 6) - z) & (NZ - 1))
    )


def held_row(slot, z, y, x, core):
    line_z = (slot + z) & (NZ - 1)
    line_y = ((slot >> 3) + y) & (NY - 1)
    line_x = ((slot >> 6) + x) & (NX - 1)
    line_core = ((slot >> 8) ^ core) & 1
    return (line_y & 3) * (NZ * 16) + line_z * 16 + (line_y >> 2) * 8 + line_x * 2 + line_core


def expect_kernel(
    class_hbm,
    precision_hbm,
    live_hbm,
    defocus_hbm,
    row_shift_hbm,
    column_shift_hbm,
    image_hbm,
    index_hbm,
    weight_hbm,
    lines_hbm,
    out_ref,
    loglik_ref,
    class_ref,
    precision_ref,
    live_ref,
    defocus_ref,
    row_shift_ref,
    column_shift_ref,
    image_ref,
    index_ref,
    weight_ref,
    lines_ref,
    load_sem,
    held,
    slots,
    weights,
    lines_t,
    lines_low,
    spread,
    spread_low,
    slices,
    shifted,
    phases,
    squares,
    products,
    turned,
    rows,
    pose_slots,
    pose_weights,
    spread_square,
    sums,
    strided,
    pair_out,
    pair_in,
    ax_out,
    ax_in,
    by_out,
    by_in,
    cz_out,
    cz_in,
    a_last_out,
    a_last_in,
    b_last_out,
    b_last_in,
    c_last_out,
    c_last_in,
    gather_send,
    gather_recv,
    pair_send,
    pair_recv,
    hop_send,
    hop_recv,
    last_send,
    last_recv,
    ready,
):
    z, y, x, core = place()
    y_lo = y % Y_LO
    sibling = device_at(z, y, x, 1 - core)

    def along_x(k):
        return device_at(z, y, (x + k) % NX, core)

    def along_y(k):
        return device_at(z, (y + NY + k) % NY, x, core)

    def along_z(k):
        return device_at((z + k) % NZ, y, x, core)

    def remote(src, dst, send, recv, device):
        return pltpu.make_async_remote_copy(
            src_ref=src,
            dst_ref=dst,
            send_sem=send,
            recv_sem=recv,
            device_id=device,
            device_id_type=MESH,
        )

    barrier = pltpu.get_barrier_semaphore()
    peers = [sibling]
    peers += [along_x(k) for k in range(1, NX)]
    peers += [along_y(k) for k in range(1, NY)]
    peers += [along_z(k) for k in range(1, NZ)]
    for peer in peers:
        pl.semaphore_signal(barrier, inc=1, device_id=peer, device_id_type=MESH)

    loads = [
        pltpu.make_async_copy(src, dst, load_sem.at[n])
        for n, (src, dst) in enumerate(
            [
                (lines_hbm, lines_ref),
                (class_hbm, class_ref),
                (live_hbm, live_ref),
                (defocus_hbm, defocus_ref),
                (column_shift_hbm, column_shift_ref),
                (row_shift_hbm, row_shift_ref),
                (image_hbm, image_ref),
                (index_hbm, index_ref),
                (weight_hbm, weight_ref),
                (precision_hbm, precision_ref),
            ]
        )
    ]
    for load in loads:
        load.start()

    loads[0].wait()
    both = lines_ref[...]
    held[core, y_lo, z] = jnp.where(core == 0, both[:, 0, :], both[:, 1, :])

    pl.semaphore_wait(barrier, len(peers))
    for k in range(1, NX):
        pl.semaphore_signal(ready, inc=1, device_id=along_x(k), device_id_type=MESH)

    def send_block(src, send, recv, device):
        copy = remote(src, src, gather_send.at[send], gather_recv.at[recv], device)
        copy.start()
        return copy

    def landed(blocks, number):
        pltpu.make_async_copy(blocks, blocks, gather_recv.at[number]).wait()

    def left(blocks, number):
        pltpu.make_async_copy(blocks, blocks, gather_send.at[number]).wait()

    groups = ((0, 1, 7), (2, 6), (3, 5, 4))
    near_z = {
        k: send_block(held.at[core, y_lo, z], 0, k, along_z(k)) for k in (4, 3, 5, 2, 6, 1, 7)
    }
    far = 2 - 4 * core
    steps = {1: 1, 2: far, 3: -1}

    def pass_along_y(k):
        block = held.at[core, y_lo, (z + NZ - k) % NZ]
        group = [k in members for members in groups].index(True)
        for d in (2, 1, 3):
            send_block(block, 1, NZ + group, along_y(steps[d]))
        send_block(block, 2, 11, sibling)

    def pass_on(*distances):
        for k in distances:
            near_z[k].wait_recv()
            pass_along_y(k)

    def swap(group):
        landed(held.at[core, pl.ds(0, 3), pl.ds(0, len(groups[group]))], NZ + group)
        for k in groups[group]:
            for residue in (y_lo + 3, y_lo + 1, y_lo + 2):
                send_block(held.at[core, residue % Y_LO, (z + NZ - k) % NZ], 2, 11, sibling)

    pass_along_y(0)
    for load in loads[1:]:
        load.wait()
    alive = jnp.where(0 < live_ref[0], 1.0, 0.0).astype(F32)
    chosen = defocus_ref[class_ref[0]]

    lane_y = lax.broadcasted_iota(I32, (SHIFTS, BOX), 1) - BOX // 2
    angle_y = phase_angle(lane_y * shift_column(column_shift_ref, (SHIFTS, BOX)))
    cos_y = jnp.cos(angle_y)
    sin_y = jnp.sin(angle_y)
    freq_y = (lax.broadcasted_iota(I32, (GROUP, BOX), 1) - BOX // 2).astype(F32) / BOX
    row_in_group = lax.broadcasted_iota(I32, (GROUP, BOX), 0)

    def shift_rows(g, carry):
        at = pl.ds(pl.multiple_of(g * WIDE, WIDE), WIDE)
        kx = pl.ds(pl.multiple_of(g * GROUP, GROUP), GROUP)
        freq_x = (row_in_group + (g * GROUP - BOX // 2)).astype(F32) / BOX
        ctf = -jnp.sin(chosen * (freq_x * freq_x + freq_y * freq_y) + 0.1) * alive
        squares[kx, :] = (ctf * ctf).astype(BF16)
        real = ctf * image_ref[0, 0, kx, :].astype(F32)
        imag = ctf * image_ref[0, 1, kx, :].astype(F32)
        blocks = []
        for k in range(GROUP):
            real_row = real[k : k + 1, :]
            imag_row = imag[k : k + 1, :]
            shift_re = real_row * cos_y + imag_row * sin_y
            shift_im = real_row * sin_y - imag_row * cos_y
            blocks.append(jnp.concatenate([shift_re, -shift_im], axis=1))
            blocks.append(jnp.concatenate([shift_im, shift_re], axis=1))
        shifted[at, :] = jnp.concatenate(blocks, axis=0).astype(BF16)
        return carry

    lane = lax.broadcasted_iota(I32, (SHIFTS, ROWS), 1)
    freq = (lane >> 4) - BOX // 2
    part = (lane >> 3) & 1
    turns = freq * shift_column(row_shift_ref, (SHIFTS, ROWS)) + part * (BOX // 4)
    row_phase = jnp.cos(phase_angle(turns))
    row_high = row_phase.astype(BF16).astype(F32)
    row_low = row_phase - row_high
    for t in range(0, SHIFTS, 2):
        for base, table in ((0, row_high), (SHIFTS * SHIFTS, row_low)):
            phases[pl.ds(base + t * SHIFTS, 2 * SHIFTS), :] = jnp.concatenate(
                [jnp.where((lane & 7) == t + u, table, 0.0) for u in range(2)], axis=0
            ).astype(BF16)

    first = slot_of(index_ref[:, 0, :], z, y, x, core)
    second = slot_of(index_ref[:, 1, :], z, y, x, core)
    first_weight = weight_ref[:, 0, :]
    second_weight = weight_ref[:, 1, :]
    same = first == second
    first_weight = jnp.where(same, first_weight + second_weight, first_weight)
    second_weight = jnp.where(same, 0.0, second_weight)
    first_high = first_weight.astype(BF16).astype(F32)
    second_high = second_weight.astype(BF16).astype(F32)
    tables = jnp.concatenate(
        [
            (first >> 4).astype(F32),
            (first & 15).astype(F32),
            (second >> 4).astype(F32),
            (second & 15).astype(F32),
            first_high,
            second_high,
            (first_weight - first_high) * LOW_SCALE,
            (second_weight - second_high) * LOW_SCALE,
        ],
        axis=0,
    ).astype(BF16)
    table_step = (
        lax.broadcasted_iota(I32, (BOX, WIDE), 0)
        - (lax.broadcasted_iota(I32, (BOX, WIDE), 1) >> 4)
    ).astype(I16)
    one = jnp.ones((BOX, WIDE), BF16)
    pose_row = lax.broadcasted_iota(I32, (POSES, WIDE), 0) == (
        lax.broadcasted_iota(I32, (POSES, WIDE), 1) & (POSES - 1)
    )

    def table_rows(g, carry):
        at = pl.ds(pl.multiple_of(g * WIDE, WIDE), WIDE)
        first_row = jnp.full((BOX, WIDE), g * GROUP, I32).astype(I16)
        chosen_row = jnp.where(table_step == first_row, one, jnp.zeros_like(one))
        wide = jnp.dot(tables, chosen_row, preferred_element_type=F32)
        found = [
            jnp.sum(
                jnp.where(pose_row, wide[n * POSES : (n + 1) * POSES, :], 0.0),
                axis=0,
                keepdims=True,
            )
            for n in range(8)
        ]
        for n in range(2):
            slot = (found[2 * n] * 16.0 + found[2 * n + 1]).astype(I32)
            slots[n, :, at] = jnp.broadcast_to(slot, (GROUP, WIDE)).astype(I16)
        for n in range(4):
            weights[n, :, at] = jnp.broadcast_to(found[4 + n], (GROUP, WIDE)).astype(BF16)
        return carry

    lax.fori_loop(0, BOX // GROUP, table_rows, 0, unroll=8)
    pass_on(1, 7)
    slot_row = lax.broadcasted_iota(I32, (GROUP, WIDE), 0).astype(I16)

    def spread_rows(g, carry):
        at = pl.ds(pl.multiple_of(g * WIDE, WIDE), WIDE)
        first_slot, second_slot = slots[0, :, at], slots[1, :, at]
        parts = [weights[n, :, at] for n in range(4)]
        lows = []
        for block in range(LINES // GROUP):
            row = slot_row + jnp.int16(block * GROUP)
            is_first = first_slot == row
            is_second = second_slot == row
            high, low = (
                jnp.where(
                    is_first,
                    parts[n],
                    jnp.where(is_second, parts[n + 1], jnp.zeros_like(parts[n])),
                )
                for n in (0, 2)
            )
            spread[block * GROUP : (block + 1) * GROUP, at] = high
            lows.append(low)
            if block % 2:
                spread_low[(block - 1) * GROUP : (block + 1) * GROUP, at] = jnp.concatenate(
                    lows[-2:], axis=0
                ).astype(F8)
        return carry

    lax.fori_loop(0, BOX // GROUP, spread_rows, 0)
    pass_on(2, 6)

    slot_rows = lax.broadcasted_iota(I32, (GROUP, BOX), 0).astype(I16)
    for n, table, target, kind in (
        (0, first, pose_slots, I16),
        (1, second, pose_slots, I16),
        (0, first_high, pose_weights, BF16),
        (1, second_high, pose_weights, BF16),
    ):
        for p in range(POSES):
            target[n, p * GROUP : (p + 1) * GROUP, :] = jnp.broadcast_to(
                table[p : p + 1, :], (GROUP, BOX)
            ).astype(kind)

    def spread_squares(p, carry):
        rows_p = pl.ds(pl.multiple_of(p * GROUP, GROUP), GROUP)
        first_slot, second_slot = pose_slots[0, rows_p, :], pose_slots[1, rows_p, :]
        first_part, second_part = pose_weights[0, rows_p, :], pose_weights[1, rows_p, :]
        blocks = []
        for block in range(LINES // GROUP):
            row = slot_rows + jnp.int16(block * GROUP)
            rest = jnp.where(second_slot == row, second_part, jnp.zeros_like(second_part))
            blocks.append(jnp.where(first_slot == row, first_part, rest))
        spread_square[p] = jnp.dot(
            jnp.concatenate(blocks, axis=0), squares[...], preferred_element_type=F32
        )
        return carry

    pass_on(3, 5, 4)
    lax.fori_loop(0, 8, shift_rows, 0)
    swap(0)
    lax.fori_loop(8, BOX // GROUP, shift_rows, 0)
    swap(1)
    lax.fori_loop(0, POSES, spread_squares, 0, unroll=8)
    swap(2)

    slot_lines = held_row(lax.broadcasted_iota(I32, (1, LINES), 1), z, y, x, core)
    order = jnp.where(
        lax.broadcasted_iota(I32, (LINES, LINES), 0) == slot_lines, 1.0, 0.0
    ).astype(BF16)

    def transpose_half(c):
        rows_c = pl.ds(pl.multiple_of(c * BOX, BOX), BOX)
        half = lax.dot_general(
            held[c].reshape(LINES, BOX),
            order,
            (((0,), (0,)), ((), ())),
            preferred_element_type=F32,
        )
        lines_t[rows_c, :] = half.astype(BF16)
        lines_low[rows_c, :] = half.astype(F8)

    def slice_half(c):
        half = pl.ds(pl.multiple_of(c * BOX, BOX), BOX)

        def step(n, carry):
            at = pl.ds(pl.multiple_of(n * 4 * WIDE, 4 * WIDE), 4 * WIDE)
            high = jnp.dot(lines_t[half, :], spread[:, at], preferred_element_type=F32)
            low = jnp.dot(lines_low[half, :], spread_low[:, at], preferred_element_type=F32)
            slices[half, at] = (high + low * (1.0 / LOW_SCALE)).astype(BF16)
            return carry

        lax.fori_loop(0, ROWS // (4 * WIDE), step, 0, unroll=True)

    transpose_half(core)
    slice_half(core)
    landed(held.at[1 - core], 11)
    transpose_half(1 - core)
    slice_half(1 - core)

    lane_row = lax.broadcasted_iota(I32, (GROUP, 128), 1) >> 4
    nothing = jnp.zeros((GROUP, 128), BF16)

    def diagonal(k, tile):
        return jnp.concatenate([tile, nothing] if k < GROUP // 2 else [nothing, tile], axis=1)

    lane_pose = lax.broadcasted_iota(I32, (GROUP, 128), 1) < POSES

    def correlate(g, carry):
        at = pl.ds(pl.multiple_of(g * WIDE, WIDE), WIDE)
        found = jnp.dot(shifted[at, :], slices[:, at], preferred_element_type=F32)
        parts = []
        for k in range(GROUP):
            lane_at = k // (GROUP // 2) * 128
            block = found[k * GROUP : (k + 1) * GROUP, lane_at : lane_at + 128]
            if k % (GROUP // 2):
                block = pltpu.roll(block, 128 - k % (GROUP // 2) * POSES, 1)
            block = jnp.where(lane_pose, block, 0.0)
            high = block.astype(BF16)
            low = (block - high.astype(F32)).astype(BF16)
            parts.append(jnp.concatenate([high, low], axis=1))
        products[at, :] = jnp.concatenate(parts, axis=0)
        return carry

    lax.fori_loop(0, BOX // GROUP, correlate, 0, unroll=True)
    corr = jnp.dot(phases[...], products[...], preferred_element_type=F32)
    half = SHIFTS * SHIFTS
    corr = corr[:half, :POSES] + (corr[half:, :POSES] + corr[:half, 128 : 128 + POSES])
    score = corr * (precision_ref[0] / BOX)
    top = jnp.max(score, axis=(0, 1), keepdims=True)
    terms = jnp.exp(score - top)
    total = jnp.sum(terms, axis=(0, 1), keepdims=True)
    posterior = terms / total
    loglik_ref[0] = ((top + jnp.log(total)) * alive)[0, 0]
    posterior_t = posterior.T
    mass = jnp.sum(posterior_t, axis=1, keepdims=True)

    ring8 = (4, 3, 5, 2, 6, 1, 7)
    ring4 = (2, 1, 3)
    pairs = []

    def spread_half(first_slot, c):
        return jnp.dot(
            spread[first_slot : first_slot + KEEP, :],
            rows[:, c * BOX : (c + 1) * BOX],
            preferred_element_type=F32,
        )

    def send_pair(c, total):
        pair_out[c] = total.astype(BF16)
        copy = remote(pair_out.at[c], pair_in.at[c], pair_send.at[c], pair_recv.at[c], sibling)
        copy.start()
        pairs.append(copy)

    part = NY * NZ
    a_pairs = {}

    def send_pair_blocks(c, total):
        pair_out[c] = total.astype(BF16)
        for n, k in enumerate(ring4 + (0,)):
            block = pl.ds(k * part, part)
            copy = remote(
                pair_out.at[c, block],
                pair_in.at[c, block],
                pair_send.at[3 + n],
                pair_recv.at[3 + n],
                sibling,
            )
            copy.start()
            pairs.append(copy)
            a_pairs[k] = copy

    def spread_own(c):
        sums[c] = spread_half(0, c)

    def spread_mass(first_slot):
        total = spread_square[0, first_slot : first_slot + KEEP, :] * mass[0:1, :]
        for p in range(1, POSES):
            total = total + spread_square[p, first_slot : first_slot + KEEP, :] * mass[p : p + 1, :]
        return total

    def turn_poses():
        high = posterior_t.astype(BF16)
        low = (posterior_t - high.astype(F32)).astype(BF16)
        parts = jnp.concatenate(
            [
                jnp.concatenate([high, high], axis=1),
                jnp.concatenate([low, jnp.zeros_like(low)], axis=1),
            ],
            axis=0,
        )
        both_parts = jnp.dot(parts, phases[...], preferred_element_type=F32)
        turned[...] = (both_parts[:POSES] + both_parts[POSES:]).astype(BF16)

    def insert(g, carry):
        at = pl.ds(pl.multiple_of(g * WIDE, WIDE), WIDE)
        turns_g = turned[:, at]
        weight = jnp.concatenate(
            [
                diagonal(
                    k,
                    jnp.where(
                        lane_row == k % (GROUP // 2),
                        turns_g[:, k // (GROUP // 2) * 128 : k // (GROUP // 2) * 128 + 128],
                        nothing,
                    ),
                )
                for k in range(GROUP)
            ],
            axis=0,
        )
        rows[at, :] = jnp.dot(
            weight, shifted[at, :], preferred_element_type=F32
        ).astype(BF16)
        return carry

    hops = []

    def hop(number, src, dst, device):
        copy = remote(src, dst, hop_send.at[number], hop_recv.at[number], device)
        copy.start()
        hops.append(copy)
        return copy


    turn_poses()
    send_pair(2, spread_mass(KEEP))
    sums[2] = spread_mass(0)
    lax.fori_loop(0, BOX // GROUP, insert, 0, unroll=True)
    pairs[0].wait_recv()
    c_sum = sums[2] + pair_in[2].astype(F32)
    for half in range(2):
        strided[half] = c_sum[:, half * 128 : (half + 1) * 128]

    def c_rows(k):
        rows_k = pl.ds(k, NX * NY, NZ)
        return jnp.concatenate([strided[0, rows_k, :], strided[1, rows_k, :]], axis=1)

    c_hops = []
    for k in ring8:
        cz_out[k] = c_rows(k).astype(BF16)
        c_hops.append(hop(k, cz_out.at[k], cz_in.at[k], along_z(k)))
    send_pair(0, spread_half(KEEP, 0))
    send_pair_blocks(1, spread_half(KEEP, 1))
    spread_own(0)
    spread_own(1)

    pairs[1].wait_recv()
    b_sum = (sums[0] + pair_in[0].astype(F32)).reshape(NX, NY, NZ, BOX)
    b_hops = []
    for k in ring8:
        by_out[k] = b_sum[:, k].reshape(NX * NZ, BOX).astype(BF16)
        b_hops.append(hop(NZ + k, by_out.at[k], by_in.at[k], along_y(k)))
    b_sum = b_sum[:, 0].reshape(NX * NZ, BOX)
    def a_block(k):
        a_pairs[k].wait_recv()
        block = pl.ds(k * part, part)
        return sums[1, block, :] + pair_in[1, block, :].astype(F32)

    a_hops = []
    for k in ring4:
        ax_out[k] = a_block(k).astype(BF16)
        a_hops.append(hop(2 * NZ + k, ax_out.at[k], ax_in.at[k], along_x(k)))
    a_sum = a_block(0)

    pl.semaphore_wait(ready, NX - 1)
    left(held.at[core, y_lo, pl.ds(0, NZ - 1)], 0)
    left(held.at[core, pl.ds(0, 3)], 1)
    left(held.at[core], 2)
    for copy in pairs + hops:
        copy.wait_send()

    def last(rows_out, rows_in, total, number, size, owner):
        count = total.shape[0]
        rows_out[...] = total.reshape(count, 1, BOX)

        def hops_to(n):
            far_step, near_step = divmod(n, 8)
            return min(far_step, size - far_step) + min(near_step, 8 - near_step)

        for n in sorted(range(1, count), key=hops_to, reverse=True):
            remote(
                rows_out.at[n], rows_in.at[n], last_send.at[number], last_recv.at[number], owner(n)
            ).start()

    def collect(rows_in, total, number):
        arrived = rows_in.at[pl.ds(1, total.shape[0] - 1)]
        pltpu.make_async_copy(arrived, arrived, last_recv.at[number]).wait()
        return total[0:1, :] + jnp.sum(rows_in[1:], axis=0)

    def drain(rows_out, number):
        gone = rows_out.at[pl.ds(1, rows_out.shape[0] - 1)]
        pltpu.make_async_copy(gone, gone, last_send.at[number]).wait()

    c_sum = c_rows(0)
    for k, copy in zip(ring8, c_hops):
        copy.wait_recv()
        c_sum = c_sum + cz_in[k].astype(F32)
    last(
        c_last_out,
        c_last_in,
        c_sum,
        2,
        NX,
        lambda n: device_at(z, (y + n % NY) % NY, (x + n // NY) % NX, core),
    )
    for k, copy in zip(ring4, a_hops):
        copy.wait_recv()
        a_sum = a_sum + ax_in[k].astype(F32)
    last(
        a_last_out,
        a_last_in,
        a_sum,
        1,
        NY,
        lambda n: device_at((z + n % NZ) % NZ, (y + n // NZ) % NY, x, core),
    )
    for k, copy in zip(ring8, b_hops):
        copy.wait_recv()
        b_sum = b_sum + by_in[k].astype(F32)
    last(
        b_last_out,
        b_last_in,
        b_sum,
        0,
        NX,
        lambda n: device_at((z + n % NZ) % NZ, y, (x + n // NZ) % NX, core),
    )
    out_ref[:, 2 * BOX :] = collect(c_last_in, c_sum, 2)
    out_ref[:, BOX : 2 * BOX] = collect(a_last_in, a_sum, 1)
    out_ref[:, :BOX] = collect(b_last_in, b_sum, 0)
    drain(c_last_out, 2)
    drain(a_last_out, 1)
    drain(b_last_out, 0)


def expect(*operands):
    smem = pl.BlockSpec(memory_space=pltpu.SMEM)
    vmem = pl.BlockSpec(memory_space=pltpu.VMEM)
    dma = pltpu.SemaphoreType.DMA
    hop_count = 2 * NZ + NX

    def both_ways(shape, kind):
        return [pltpu.VMEM(shape, kind), pltpu.VMEM(shape, kind)]

    return pl.pallas_call(
        expect_kernel,
        out_shape=(
            jax.ShapeDtypeStruct((1, 3 * BOX), F32),
            jax.ShapeDtypeStruct((1,), F32),
        ),
        in_specs=[pl.BlockSpec(memory_space=pltpu.HBM)] * 10,
        out_specs=(vmem, smem),
        scratch_shapes=[
            pltpu.SMEM(operand.shape, operand.dtype) for operand in operands[:6]
        ]
        + [pltpu.VMEM(operand.shape, operand.dtype) for operand in operands[6:]]
        + [dma((10,))]
        + [
            pltpu.VMEM((2, Y_LO, NZ, 16, BOX), BF16),
            pltpu.VMEM((2, GROUP, ROWS), I16),
            pltpu.VMEM((4, GROUP, ROWS), BF16),
            pltpu.VMEM((2 * BOX, LINES), BF16),
            pltpu.VMEM((2 * BOX, LINES), F8),
            pltpu.VMEM((LINES, ROWS), BF16),
            pltpu.VMEM((LINES, ROWS), F8),
            pltpu.VMEM((2 * BOX, ROWS), BF16),
            pltpu.VMEM((ROWS, 2 * BOX), BF16),
            pltpu.VMEM((2 * SHIFTS * SHIFTS, ROWS), BF16),
            pltpu.VMEM((BOX, BOX), BF16),
            pltpu.VMEM((ROWS, WIDE), BF16),
            pltpu.VMEM((POSES, ROWS), BF16),
            pltpu.VMEM((ROWS, 2 * BOX), BF16),
            pltpu.VMEM((2, POSES * GROUP, BOX), I16),
            pltpu.VMEM((2, POSES * GROUP, BOX), BF16),
            pltpu.VMEM((POSES, LINES, BOX), F32),
            pltpu.VMEM((3, KEEP, BOX), F32),
            pltpu.VMEM((2, KEEP, BOX // 2), F32),
        ]
        + both_ways((3, KEEP, BOX), BF16)
        + both_ways((NX, NY * NZ, BOX), BF16)
        + both_ways((NY, NX * NZ, BOX), BF16)
        + both_ways((NZ, NX * NY, BOX), BF16)
        + both_ways((NY * NZ, 1, BOX), F32)
        + both_ways((NX * NZ, 1, BOX), F32)
        + both_ways((NX * NY, 1, BOX), F32)
        + [
            dma((3,)),
            dma((12,)),
            dma((7,)),
            dma((7,)),
            dma((hop_count,)),
            dma((hop_count,)),
            dma((3,)),
            dma((3,)),
            pltpu.SemaphoreType.REGULAR,
        ],
        compiler_params=pltpu.CompilerParams(
            collective_id=0, has_side_effects=True, vmem_limit_bytes=60 * 1024 * 1024
        ),
    )(*operands)


def body(
    particles,
    defocus_class,
    noise_precision,
    live_count,
    defocus,
    reference_lines,
    line_index,
    line_weight,
    row_shifts,
    column_shifts,
):
    index = jnp.transpose(line_index, (0, 2, 1))
    weight = jnp.transpose(line_weight, (0, 2, 1))
    particle_total = particles.shape[0] * lax.axis_size("slab") * lax.axis_size("grp")
    owned, loglik = expect(
        defocus_class,
        noise_precision,
        live_count,
        defocus,
        row_shifts,
        column_shifts,
        particles,
        index,
        weight,
        reference_lines,
    )
    return owned.reshape(1, 3, BOX) * (LINES / (POSES * particle_total)), loglik


def solution(mesh):
    return jax.shard_map(
        body,
        mesh=mesh,
        in_specs=(
            P(("slab", "grp"), None, None, None),
            P(("slab", "grp")),
            P(("slab", "grp")),
            P("grp"),
            P(),
            P("slab", None, None),
            P(),
            P(),
            P(),
            P(),
        ),
        out_specs=(P(("slab", "grp"), None, None), P(("slab", "grp"))),
        check_vma=False,
    )
```
